32 devices in a mesh: row: 4 (over z), col: 8 (over y, x, core).
Axes of the slice: x: 2, y: 2, z: 4, core: 2. Of those that a mesh axis runs over, the one named last changes fastest.
Arguments:
- pair: bfloat16 [256, 256, 128], P(('row', 'col')), may hold values from -6 to 6
- residue_mask: int32 [256], replicated, may hold values from 0 to 1, as said below
- ln_gain: float32 [2, 128], replicated, may hold values from 0.5 to 1.5
- ln_shift: float32 [2, 128], replicated, may hold values from -3 to 3
- w_proj: bfloat16 [2, 128, 512], replicated, may hold values from -0.5 to 0.5
- w_bias: bfloat16 [2, 128, 4], replicated, may hold values from -10.606602 to 10.606602
- gate_bias: float32 [2, 128], replicated, may hold values from -4 to 4
- w_out: bfloat16 [2, 128, 128], replicated, may hold values from -0.5 to 0.5
- out_bias: float32 [2, 128], replicated, may hold values from -3 to 3
Outputs:
- starting_update: bfloat16 [64, 256, 128], P(('row', 'col'))
- ending_update: bfloat16 [64, 256, 128], P(('row', 'col'))
The draws below stay inside these ranges and needn't reach their ends.
Inputs may be any that keep to these rules, and one draw needn't show every extreme that they name: `residue_mask`: residue 0 is always a real residue.
All inputs are finite; a program needn't handle non-finite values.
Results may differ from the reference program's by a relative error of at most 0.0065.
The reference program's roundings to bfloat16 on the way count: a program that leaves them out, or rounds other values in their place, can miss the bound.
Values may be sent and summed in bfloat16 or wider, within the bound.
No kernel may reach another device: no remote copies, remote signals or barrier semaphores. Data moves between devices by JAX's collectives and lax.ppermute only.
A program may use at most 128 MiB of HBM per device.

```python
import jax
import jax.numpy as jnp
from jax import lax

C = 128
HEADS = 4
DH = 32
RD = 8
WD = 2
N = 256
N_ROW = 4
N_COL = 8


def draw_residue_mask(key, part):
    key = jax.random.fold_in(key, 11)
    levels = jax.random.randint(key, (N,), 0, 20)
    live = (levels < 17).astype(jnp.int32)
    return live.at[0].set(1)


def draw_w_bias(key, part):
    key = jax.random.fold_in(key, 23)
    base = jnp.clip(jax.random.normal(key, (2, C, HEADS), jnp.float32), -4.0, 4.0)
    factor = 1.5
    return (base * (factor / C ** 0.5)).astype(jnp.bfloat16)


def level_of(stream_key, shape, split, least, top_value):
    def one(dim, parts):
        heights = jax.random.uniform(jax.random.fold_in(jax.random.fold_in(stream_key, 6), dim), (parts,), jnp.float32, least / len(split), top_value / len(split))
        return jnp.repeat(jnp.exp(heights), shape[dim] // parts).reshape((-1,) + (1,) * (len(shape) - dim - 1))

    level = one(*split[0])
    for cut in split[1:]:
        level = level * one(*cut)
    return level


def normal_values(stream_key, extent, deviation, bound, pieces=(), held_as=jnp.bfloat16):
    loudness = level_of(stream_key, extent, pieces, -0.22, 0.18) if pieces else 1.0
    entries = jax.random.normal(stream_key, extent, jnp.float32) * deviation * loudness
    return jnp.minimum(jnp.maximum(entries, -bound), bound).astype(held_as)


def setup_inputs(seed: int = 0) -> dict:
    keys = jax.random.split(jax.random.key(seed), 10)
    return {
        "pair": normal_values(keys[0], (N, N, C), 1.0, 6.0, ((0, 32),)),
        "residue_mask": draw_residue_mask(jax.random.fold_in(keys[9], 71), 0),
        "ln_gain": jnp.clip(1.0 + 0.1 * jax.random.normal(keys[2], (2, C), jnp.float32), 0.5, 1.5),
        "ln_shift": normal_values(keys[3], (2, C), 0.5, 3.0, (), jnp.float32),
        "w_proj": normal_values(keys[4], (2, C, 4 * HEADS * DH), C ** -0.5, 0.5),
        "w_bias": draw_w_bias(jax.random.fold_in(keys[9], 71), 0),
        "gate_bias": normal_values(keys[6], (2, HEADS * DH), 1.0, 4.0, (), jnp.float32),
        "w_out": normal_values(keys[7], (2, HEADS * DH, C), (HEADS * DH) ** -0.5, 0.5),
        "out_bias": normal_values(keys[8], (2, C), 0.5, 3.0, (), jnp.float32),
    }


EPS = 1e-05

def layer_norm(values, gain, shift):
    wide = values.astype(jnp.float32)
    center = lax.optimization_barrier(jnp.mean(wide, -1, keepdims=True))
    spread = lax.optimization_barrier(jnp.mean(jnp.square(wide - center), -1, keepdims=True))
    return ((wide - center) * lax.rsqrt(spread + EPS) * gain + shift).astype(jnp.bfloat16)

def project(normed, weight, offset, head_count):
    lead = normed.shape[:-1]
    inner = weight.shape[1] // 4
    size = inner // head_count
    full = jnp.dot(normed.reshape(-1, normed.shape[-1]), weight, preferred_element_type=jnp.float32)
    queries = (full[:, :inner] * size ** (-0.5)).astype(jnp.bfloat16).reshape(lead + (head_count, size))
    key_rows = full[:, inner:2 * inner].astype(jnp.bfloat16).reshape(lead + (head_count, size))
    value_rows = full[:, 2 * inner:3 * inner].astype(jnp.bfloat16).reshape(lead + (head_count, size))
    gating = jax.nn.sigmoid(full[:, 3 * inner:] + offset).reshape(lead + (inner,))
    return (queries, key_rows, value_rows, gating)

def attend(queries, key_rows, value_rows, gating, bias, live, weight_out, offset_out):
    scores = jnp.einsum('qhd,khd->hqk', queries.astype(jnp.float32), key_rows.astype(jnp.float32)) + bias.astype(jnp.float32)
    scores = jnp.where(live[None, None, :] > 0, scores, jnp.float32(-1000000000.0))
    top = lax.optimization_barrier(jnp.max(scores, -1, keepdims=True))
    expo = jnp.exp(scores - top)
    weights = (expo / lax.optimization_barrier(jnp.sum(expo, -1, keepdims=True))).astype(jnp.bfloat16)
    mixed = jnp.einsum('hqk,khd->qhd', weights.astype(jnp.float32), value_rows.astype(jnp.float32))
    gated = (mixed.reshape(mixed.shape[0], -1) * gating).astype(jnp.bfloat16)
    return (jnp.dot(gated, weight_out, preferred_element_type=jnp.float32) + offset_out).astype(jnp.bfloat16)

def bias_rows(pair, gain, shift, weight):

    def one_line(line):
        normed = layer_norm(line, gain, shift)
        return jnp.dot(normed, weight, preferred_element_type=jnp.float32).astype(jnp.bfloat16)
    return jnp.transpose(lax.map(one_line, pair), (2, 0, 1))

def reference(pair, residue_mask, ln_gain, ln_shift, w_proj, w_bias, gate_bias, w_out, out_bias):
    devices = N_ROW * N_COL
    window_index = (jnp.arange(devices, dtype=jnp.int32)[:, None] * RD + jnp.arange(WD, dtype=jnp.int32)[None, :]).reshape(-1).astype(jnp.int32)
    start_bias = bias_rows(pair, ln_gain[0], ln_shift[0], w_bias[0])
    end_bias = jnp.transpose(bias_rows(pair, ln_gain[1], ln_shift[1], w_bias[1]), (0, 2, 1))

    def run(line, which, bias):
        normed = layer_norm(line, ln_gain[which], ln_shift[which])
        queries, key_rows, value_rows, gating = project(normed, w_proj[which], gate_bias[which], HEADS)
        return attend(queries, key_rows, value_rows, gating, bias, residue_mask, w_out[which], out_bias[which])
    starting_update = lax.map(lambda index: run(pair[index], 0, start_bias), window_index)
    ending_update = lax.map(lambda index: run(pair[:, index, :], 1, end_bias), window_index)
    return (starting_update, ending_update)
```

```python
import functools

import jax
import jax.numpy as jnp
from jax import lax
from jax.experimental import pallas as pl
from jax.experimental.pallas import tpu as pltpu
from jax.sharding import PartitionSpec as P

WD = 2
EPS = 1e-05
MASKED = -1000000000.0
CHUNK = 256
LANES = 128
VMEM = pl.BlockSpec(memory_space=pltpu.VMEM)
SMEM = pl.BlockSpec(memory_space=pltpu.SMEM)


def params(megabytes):
    return pltpu.CompilerParams(vmem_limit_bytes=megabytes * 1024 * 1024)


def for_each(count, step, unrolled):
    if unrolled:
        for index in range(count):
            step(index)
    else:
        lax.fori_loop(0, count, lambda index, carry: (step(index), carry)[1], 0)


def standardize(wide):
    center = jnp.mean(wide, -1, keepdims=True)
    away = wide - center
    spread = jnp.mean(jnp.square(away), -1, keepdims=True)
    return away * lax.rsqrt(spread + EPS)


def contract(left, right, left_dim, right_dim):
    return lax.dot_general(
        left, right, (((left_dim,), (right_dim,)), ((), ())), preferred_element_type=jnp.float32
    )


def bias_kernel(pair_ref, own_ref, live_ref, gain_ref, shift_ref, weight_ref, bias_ref, pick_ref, wide, rows_out, picked):
    rows, length, channels = pair_ref.shape
    heads = weight_ref.shape[1]
    devices = length // rows
    live = live_ref[...] > 0
    for a in range(rows):
        x = pair_ref[a].astype(jnp.float32)
        wide[a] = x
        z = standardize(x)
        for p in range(2):
            normed = (z * gain_ref[p : p + 1, :] + shift_ref[p : p + 1, :]).astype(jnp.bfloat16)
            bias = contract(weight_ref[p], normed, 1, 1)
            if p == 0:
                bias = jnp.where(live, bias, MASKED)
            else:
                bias = jnp.where(own_ref[a] > 0, bias, MASKED)
            for lane in range(length // LANES):
                part = bias[:, lane * LANES : (lane + 1) * LANES]
                rows_out[lane, pl.ds(p * heads * rows + a, heads, stride=rows), :] = part
        for w in range(WD):
            column = wide[a, pl.ds(w, devices, stride=rows), :]
            picked[pl.ds(w * rows + a, devices, stride=WD * rows), :] = column
    for lane in range(length // LANES):
        bias_ref[:, lane * LANES : (lane + 1) * LANES] = rows_out[lane].astype(jnp.bfloat16)
    pick_ref[...] = picked[...].astype(jnp.bfloat16).reshape(pick_ref.shape)


def local_bias(pair, own, live, gain, shift, weight):
    rows, length, channels = pair.shape
    heads = weight.shape[1]
    devices = length // rows
    return pl.pallas_call(
        bias_kernel,
        out_shape=(
            jax.ShapeDtypeStruct((2 * heads * rows, length), jnp.bfloat16),
            jax.ShapeDtypeStruct((devices, WD * rows, channels), jnp.bfloat16),
        ),
        in_specs=[VMEM, SMEM, VMEM, VMEM, VMEM, VMEM],
        out_specs=(VMEM, VMEM),
        scratch_shapes=[
            pltpu.VMEM((rows, length, channels), jnp.float32),
            pltpu.VMEM((length // LANES, 2 * heads * rows, LANES), jnp.float32),
            pltpu.VMEM((devices * WD * rows, channels), jnp.float32),
        ],
        compiler_params=params(40),
        name="bias",
    )(pair, own, live, gain, shift, weight)


def project_kernel(which, scale, lines_ref, gain_ref, shift_ref, weight_ref, offset_ref, q_ref, k_ref, v_ref, g_ref):
    inner = k_ref.shape[-1]
    length = k_ref.shape[1]
    for w in range(WD):
        if which == 0:
            x = lines_ref[w].astype(jnp.float32)
        else:
            blocks, packed, channels = lines_ref.shape
            x = lines_ref[...].astype(jnp.float32).reshape(blocks, WD, packed // WD, channels)
            x = x[:, w].reshape(length, channels)
        gain, shift = gain_ref[which : which + 1, :], shift_ref[which : which + 1, :]
        normed = (standardize(x) * gain + shift).astype(jnp.bfloat16)
        weight = weight_ref[0]
        q_ref[w] = (contract(weight[:, :inner], normed, 0, 1) * scale).astype(jnp.bfloat16)
        k_ref[w] = contract(normed, weight[:, inner : 2 * inner], 1, 0).astype(jnp.bfloat16)
        v_ref[w] = contract(weight[:, 2 * inner : 3 * inner], normed, 0, 1).astype(jnp.bfloat16)
        g_ref[w] = jax.nn.sigmoid(contract(weight[:, 3 * inner :], normed, 0, 1) + offset_ref[0])


def project(which, lines, length, gain, shift, weight, offset, head_count):
    channels, wide = weight.shape[1:]
    inner = wide // 4
    if which == 0:
        lines_spec = pl.BlockSpec((WD, length, channels), lambda i: (0, 0, 0))
    else:
        lines_spec = pl.BlockSpec(lines.shape, lambda i: (0, 0, 0))
    flat = pl.BlockSpec(gain.shape, lambda i: (0, 0))
    turned = jax.ShapeDtypeStruct((WD, inner, length), jnp.bfloat16)
    out = lambda shape: pl.BlockSpec(shape, lambda i: (0, 0, 0))
    return pl.pallas_call(
        functools.partial(project_kernel, which, (inner // head_count) ** (-0.5)),
        grid=(1,),
        out_shape=(
            turned,
            jax.ShapeDtypeStruct((WD, length, inner), jnp.bfloat16),
            turned,
            jax.ShapeDtypeStruct((WD, inner, length), jnp.float32),
        ),
        in_specs=[
            lines_spec,
            flat,
            flat,
            pl.BlockSpec((1, channels, wide), lambda i: (which, 0, 0)),
            pl.BlockSpec((1, inner, 1), lambda i: (which, 0, 0)),
        ],
        out_specs=(
            out((WD, inner, length)),
            out((WD, length, inner)),
            out((WD, inner, length)),
            out((WD, inner, length)),
        ),
        compiler_params=params(40),
        cost_estimate=pl.CostEstimate(
            flops=2 * WD * length * channels * wide, bytes_accessed=4 * WD * length * wide, transcendentals=0
        ),
        name="project",
    )(lines, gain, shift, weight, offset[:, :, None])


def attend_kernel(
    mine_ref, other_ref, q0, k0, v0, g0, q1, k1, v1, g1, weight_ref, offset_ref, out0, out1, bias, mixed
):
    chips, along, packed, length = mine_ref.shape
    inner = k0.shape[-1]
    rows = length // (2 * chips * along)
    heads = packed // (2 * rows)
    size = inner // heads
    unrolled = length <= CHUNK
    core = lax.rem(lax.axis_index("col"), 2)
    sides = ((q0, k0, v0, g0, out0), (q1, k1, v1, g1, out1))
    owner = lax.broadcasted_iota(jnp.int32, (inner, CHUNK), 0) // size
    for p, (q, k, v, g, out) in enumerate(sides):
        for pack in range(heads // 2):
            first = (p * heads + 2 * pack) * rows

            def unpack(block):
                chip, row = block // along, block % along
                for source, parity in ((mine_ref, core), (other_ref, 1 - core)):
                    at = pl.multiple_of(((row * chips + chip) * 2 + parity) * rows, rows)
                    both = source[chip, row, first : first + 2 * rows, :].astype(jnp.float32)
                    for i in range(2):
                        bias[i, pl.ds(at, rows), :] = both[i * rows : (i + 1) * rows]

            for_each(chips * along, unpack, unrolled)
            for i in range(2):
                h = 2 * pack + i

                def columns(chunk):
                    at = chunk * CHUNK if unrolled else pl.multiple_of(chunk * CHUNK, CHUNK)
                    if p == 0:
                        added = bias[i, pl.ds(at, CHUNK), :].T
                    else:
                        added = bias[i, :, pl.ds(at, CHUNK)]
                    for w in range(WD):
                        queries = jnp.where(owner == h, q[w, :, pl.ds(at, CHUNK)], jnp.bfloat16(0))
                        scores = contract(k[w], queries, 1, 0) + added
                        expo = jnp.exp(scores - jnp.max(scores, 0, keepdims=True))
                        weights = expo * (1.0 / jnp.sum(expo, 0, keepdims=True))
                        part = contract(
                            v[w, h * size : (h + 1) * size, :], weights.astype(jnp.bfloat16), 1, 0
                        )
                        mixed[w, h * size : (h + 1) * size, pl.ds(at, CHUNK)] = part

                for_each(length // CHUNK, columns, unrolled)
        for w in range(WD):
            gated = (mixed[w] * g[w]).astype(jnp.bfloat16)
            full = contract(gated, weight_ref[p], 0, 0) + offset_ref[p : p + 1, :]
            out[w] = full.astype(jnp.bfloat16)


def attend(mine, other, start, end, weight, offset):
    length = mine.shape[-1]
    inner, channels = weight.shape[1:]
    result = jax.ShapeDtypeStruct((WD, length, channels), jnp.bfloat16)
    return pl.pallas_call(
        attend_kernel,
        out_shape=(result, result),
        in_specs=[VMEM] * 12,
        out_specs=(VMEM, VMEM),
        scratch_shapes=[
            pltpu.VMEM((2, length, length), jnp.float32),
            pltpu.VMEM((WD, inner, length), jnp.float32),
        ],
        compiler_params=params(56),
        name="attend",
    )(mine, other, *start, *end, weight, offset)


def place(pieces, positions):
    out = jnp.zeros((len(pieces),) + pieces[0].shape, pieces[0].dtype)
    for piece, position in zip(pieces, positions):
        out = lax.dynamic_update_index_in_dim(out, piece, position, 0)
    return out


def staged_gather(block):
    rows, cols = lax.axis_size("row"), lax.axis_size("col")
    row, col = lax.axis_index("row"), lax.axis_index("col")
    pieces, positions = [block], [row]
    for shift in range(1, rows):
        pieces.append(lax.ppermute(block, "row", [(i, (i + shift) % rows) for i in range(rows)]))
        positions.append((row - shift) % rows)
    along = place(pieces, positions)
    pieces, positions = [along], [col // 2]
    for flip in range(2, cols, 2):
        pieces.append(lax.ppermute(along, "col", [(i, i ^ flip) for i in range(cols)]))
        positions.append((col ^ flip) // 2)
    chips = place(pieces, positions)
    other = lax.ppermute(chips, "col", [(i, i ^ 1) for i in range(cols)])
    return chips, other


def body(pair, residue_mask, ln_gain, ln_shift, w_proj, w_bias, gate_bias, w_out, out_bias):
    rows, length, channels = pair.shape
    heads = w_bias.shape[2]
    cols = lax.axis_size("col")
    device = lax.axis_index("row") * cols + lax.axis_index("col")
    own = lax.dynamic_slice(residue_mask, (device * rows,), (rows,))
    block, picked = local_bias(
        pair, own, residue_mask[None, :], ln_gain, ln_shift, jnp.transpose(w_bias, (0, 2, 1))
    )
    moved = lax.all_to_all(picked, ("row", "col"), split_axis=0, concat_axis=0, tiled=True)
    mine, other = staged_gather(block)
    start = project(0, pair, length, ln_gain, ln_shift, w_proj, gate_bias, heads)
    end = project(1, moved, length, ln_gain, ln_shift, w_proj, gate_bias, heads)
    return attend(mine, other, start, end, w_out, out_bias)


def solution(mesh):
    return jax.shard_map(
        body,
        mesh=mesh,
        in_specs=(P(("row", "col"), None, None), P(), P(), P(), P(), P(), P(), P(), P()),
        out_specs=(P(("row", "col"), None, None), P(("row", "col"), None, None)),
        check_vma=False,
    )
```

```python
import functools

import jax
import jax.numpy as jnp
from jax import lax
from jax.experimental import pallas as pl
from jax.experimental.pallas import tpu as pltpu
from jax.sharding import PartitionSpec as P

WD = 2
EPS = 1e-05
MASKED = -1000000000.0
CHUNK = 256
VMEM = pl.BlockSpec(memory_space=pltpu.VMEM)
HBM = pl.BlockSpec(memory_space=pltpu.HBM)


def params(megabytes):
    return pltpu.CompilerParams(vmem_limit_bytes=megabytes * 1024 * 1024)


def for_each(count, step, unrolled):
    if unrolled:
        for index in range(count):
            step(index)
    else:
        lax.fori_loop(0, count, lambda index, carry: (step(index), carry)[1], 0)


def standardize(wide):
    center = jnp.mean(wide, -1, keepdims=True)
    away = wide - center
    spread = jnp.mean(jnp.square(away), -1, keepdims=True)
    return away * lax.rsqrt(spread + EPS)


def contract(left, right, left_dim, right_dim):
    return lax.dot_general(
        left, right, (((left_dim,), (right_dim,)), ((), ())), preferred_element_type=jnp.float32
    )


def flipped(index, flip):
    bit = 1
    while bit <= flip:
        if flip & bit:
            index = index + bit - 2 * bit * lax.rem(lax.div(index, bit), 2)
        bit *= 2
    return index


def bias_kernel(along, chips, pair_hbm, live_hbm, gain_hbm, shift_hbm, weight_hbm, out_ref, *rest):
    picks = rest[:chips]
    pair, live_row, live_each, gain, shift, weight, blocks, rows_out, wide, picked, sems, pair_sems = rest[chips:]
    rows, length, channels = pair.shape
    heads = weight.shape[1]
    lanes = out_ref.shape[1]
    small = [
        pltpu.make_async_copy(source, target, sems.at[i])
        for i, (source, target) in enumerate(
            ((live_hbm, live_row), (live_hbm, live_each), (gain_hbm, gain), (shift_hbm, shift), (weight_hbm, weight))
        )
    ]
    large = [pltpu.make_async_copy(pair_hbm.at[a], pair.at[a], pair_sems.at[a]) for a in range(rows)]
    large[0].start()
    for copy in small:
        copy.start()
    for copy in large[1:]:
        copy.start()
    device = lax.axis_index("row") * lax.axis_size("col") + lax.axis_index("col")
    for copy in small + large:
        copy.wait()
    blocks[...] = jnp.zeros_like(blocks)
    for p in range(2):
        at = slice(p * heads, (p + 1) * heads)
        blocks[at, p * channels : (p + 1) * channels] = weight[p].astype(jnp.float32)
    paired = blocks[: 2 * heads].astype(jnp.bfloat16)
    live = jnp.broadcast_to(live_row[...], (2 * heads, length))
    first = lax.broadcasted_iota(jnp.int32, live.shape, 0) < heads
    for a in range(rows):
        x = pair[a].astype(jnp.float32)
        wide[a] = x
        z = standardize(x)
        normed = jnp.concatenate(
            [(z * gain[p : p + 1, :] + shift[p : p + 1, :]).astype(jnp.bfloat16) for p in range(2)], 1
        )
        bias = contract(paired, normed, 1, 1)
        kept = jnp.where(first, live, live_each[0, device * rows + a])
        bias = jnp.where(kept > 0, bias, MASKED)
        for lane in range(length // lanes):
            part = bias[:, lane * lanes : (lane + 1) * lanes]
            rows_out[pl.ds(2 * lane * heads * rows + a, 2 * heads, stride=rows), :] = part
    out_ref[...] = rows_out[...].astype(jnp.bfloat16)
    devices = length // rows
    for a in range(rows):
        for w in range(WD):
            column = wide[a, pl.ds(w, devices, stride=rows), :]
            picked[pl.ds(w * rows + a, devices, stride=WD * rows), :] = column
    chip = lax.div(lax.axis_index("col"), 2)
    both = 2 * WD * rows
    for flip, pick in enumerate(picks):
        for shift in range(along):
            row = lax.rem(lax.axis_index("row") + shift, along)
            at = pl.multiple_of((row * chips + flipped(chip, flip)) * both, both)
            pick[shift] = picked[pl.ds(at, both), :].astype(jnp.bfloat16)


def local_bias(pair, live, gain, shift, weight, along, chips):
    rows, length, channels = pair.shape
    heads = weight.shape[1]
    pick = jax.ShapeDtypeStruct((along, 2 * WD * rows, channels), jnp.bfloat16)
    packed = 2 * heads * rows * (length // channels)
    out = pl.pallas_call(
        functools.partial(bias_kernel, along, chips),
        out_shape=(jax.ShapeDtypeStruct((packed, channels), jnp.bfloat16),) + (pick,) * chips,
        in_specs=[HBM] * 5,
        out_specs=(VMEM,) * (1 + chips),
        scratch_shapes=[
            pltpu.VMEM(pair.shape, pair.dtype),
            pltpu.VMEM(live.shape, live.dtype),
            pltpu.SMEM(live.shape, live.dtype),
            pltpu.VMEM(gain.shape, gain.dtype),
            pltpu.VMEM(shift.shape, shift.dtype),
            pltpu.VMEM(weight.shape, weight.dtype),
            pltpu.VMEM((4 * heads, 2 * channels), jnp.float32),
            pltpu.VMEM((packed, channels), jnp.float32),
            pltpu.VMEM(pair.shape, jnp.float32),
            pltpu.VMEM((length * WD, channels), jnp.float32),
            pltpu.SemaphoreType.DMA((5,)),
            pltpu.SemaphoreType.DMA((rows,)),
        ],
        compiler_params=params(60),
        name="bias",
    )(pair, live, gain, shift, weight)
    return out[0], out[1:]


def turned(row):
    return jnp.broadcast_to(row, (row.shape[1], row.shape[1])).T[:, :1]


def turned_over(index, bit):
    return lax.rem(lax.div(index, bit), 2) == 1


def to_relative(x, along, chips, rows):
    row, col = lax.axis_index("row"), lax.axis_index("col")
    cols = 2 * chips
    grid = [[x[(r * cols + c) * rows : (r * cols + c + 1) * rows] for c in range(cols)] for r in range(along)]
    bit = 1
    while bit < cols:
        swap = turned_over(col, bit)
        grid = [[jnp.where(swap, line[c ^ bit], line[c]) for c in range(cols)] for line in grid]
        bit *= 2
    grid = [grid[-t % along] for t in range(along)]
    bit = 1
    while bit < along:
        move = turned_over(row, bit)
        grid = [
            [jnp.where(move, grid[(t - bit) % along][c], grid[t][c]) for c in range(cols)] for t in range(along)
        ]
        bit *= 2
    return jnp.concatenate(
        [grid[s][2 * flip + other] for other in range(2) for flip in range(chips) for s in range(along)], 0
    )


def to_devices(x, along, chips, rows):
    row, col = lax.axis_index("row"), lax.axis_index("col")
    cols = 2 * chips
    at = lambda c, s: (((c % 2) * chips + c // 2) * along + s) * rows
    grid = [[x[at(c, s) : at(c, s) + rows] for c in range(cols)] for s in range(along)]
    bit = 1
    while bit < along:
        move = turned_over(row, bit)
        grid = [
            [jnp.where(move, grid[(s + bit) % along][c], grid[s][c]) for c in range(cols)] for s in range(along)
        ]
        bit *= 2
    grid = [grid[-r % along] for r in range(along)]
    bit = 1
    while bit < cols:
        swap = turned_over(col, bit)
        grid = [[jnp.where(swap, line[c ^ bit], line[c]) for c in range(cols)] for line in grid]
        bit *= 2
    return jnp.concatenate([block for line in grid for block in line], 0)


def queries_and_gates(normed, scale, weight, offset, q_ref, g_ref, w):
    inner = weight.shape[1] // 4
    q_ref[w] = (contract(weight[:, :inner], normed, 0, 1) * scale).astype(jnp.bfloat16)
    g_ref[w] = jax.nn.sigmoid(contract(weight[:, 3 * inner :], normed, 0, 1) + offset)


def keys_and_values(normed, weight, k_ref, v_ref, w):
    _, heads, _, size = k_ref.shape
    inner = heads * size
    for h in range(heads):
        at = inner + h * size
        k_ref[w, h] = contract(normed, weight[:, at : at + size], 1, 0).astype(jnp.bfloat16)
    v_ref[w] = contract(weight[:, 2 * inner : 3 * inner], normed, 0, 1).astype(jnp.bfloat16)


def lines_kernel(along, chips, lines_ref, gain_ref, shift_ref, weight_ref, offset_ref, q_ref, k_ref, v_ref, g_ref):
    size = k_ref.shape[-1]
    rows = lines_ref.shape[1] // (2 * chips * along)
    offset = turned(offset_ref[0:1, :])
    weight = weight_ref[0]
    for w in range(WD):
        normed = standardize(lines_ref[w].astype(jnp.float32)) * gain_ref[0:1, :] + shift_ref[0:1, :]
        keys_and_values(normed.astype(jnp.bfloat16), weight, k_ref, v_ref, w)
        near = to_relative(normed, along, chips, rows).astype(jnp.bfloat16)
        queries_and_gates(near, size ** (-0.5), weight, offset, q_ref, g_ref, w)


def projected(length, inner, heads):
    wide = (WD, inner, length)
    return (
        (wide, jnp.bfloat16),
        ((WD, heads, length, inner // heads), jnp.bfloat16),
        (wide, jnp.bfloat16),
        (wide, jnp.float32),
    )


def local_lines(pair, gain, shift, weight, offset, heads, along, chips):
    _, length, channels = pair.shape
    wide = weight.shape[2]
    shapes = projected(length, wide // 4, heads)
    whole = lambda shape: pl.BlockSpec(shape, lambda i: (0,) * len(shape))
    return pl.pallas_call(
        functools.partial(lines_kernel, along, chips),
        grid=(1,),
        out_shape=tuple(jax.ShapeDtypeStruct(shape, dtype) for shape, dtype in shapes),
        in_specs=[
            whole((WD, length, channels)), whole(gain.shape), whole(gain.shape),
            whole((1, channels, wide)), whole(gain.shape),
        ],
        out_specs=tuple(whole(shape) for shape, _ in shapes),
        compiler_params=params(8 + length // 32),
        cost_estimate=pl.CostEstimate(
            flops=2 * WD * length * channels * wide, bytes_accessed=4 * WD * length * wide, transcendentals=0
        ),
        name="lines",
    )(pair, gain, shift, weight, offset)


def unpack(source, p, pack, rows, heads, turn, into, at):
    chips, along, _, lanes = source.shape
    packed = 2 * heads * rows
    half = chips * along * rows
    slots = into.shape[0]
    for lane in range(into.shape[2 - turn] // lanes):
        first = lane * packed + (p * heads + 2 * pack) * rows
        both = [
            source[flip, shift, first : first + 2 * rows, :].astype(jnp.float32)
            for flip in range(chips)
            for shift in range(along)
        ]
        there = slice(lane * lanes, (lane + 1) * lanes)
        for i in range(2):
            slot = (2 * pack + i) % slots
            block = jnp.concatenate([part[i * rows : (i + 1) * rows] for part in both], 0)
            if turn:
                into[slot, there, at : at + half] = block.T
            else:
                into[slot, at : at + half, there] = block


def softmax_mix(keys, queries, values, added):
    scores = [contract(k, q, 1, 0) + added for k, q in zip(keys, queries)]
    tops = [jnp.max(score, 0, keepdims=True) for score in scores]
    expos = [jnp.exp(score - top) for score, top in zip(scores, tops)]
    shares = [1.0 / jnp.sum(expo, 0, keepdims=True) for expo in expos]
    weights = [(expo * share).astype(jnp.bfloat16) for expo, share in zip(expos, shares)]
    return [contract(v, weight, 1, 0) for v, weight in zip(values, weights)]


def start_half(source, other, q, k, v, mixed, bias):
    _, heads, length, size = k.shape
    half = length // 2
    rows = half // (source.shape[0] * source.shape[1])
    width = min(half, CHUNK)
    for pack in range(heads // 2):
        unpack(source, 0, pack, rows, heads, 1, bias, 0)
        for i in range(2):
            part = slice((2 * pack + i) * size, (2 * pack + i + 1) * size)

            def step(chunk):
                near = pl.ds(chunk * width if half == width else pl.multiple_of(chunk * width, width), width)
                there = pl.ds(other * half + chunk * width, width)
                if half != width:
                    there = pl.ds(pl.multiple_of(other * half + chunk * width, width), width)
                outs = softmax_mix(
                    [k[w, 2 * pack + i] for w in range(WD)],
                    [q[w, part, there] for w in range(WD)],
                    [v[w, part, :] for w in range(WD)],
                    bias[(2 * pack + i) % bias.shape[0], :, near],
                )
                for w in range(WD):
                    mixed[w, part, near] = outs[w]

            for_each(half // width, step, half == width)


def early_kernel(mine_ref, q, k, v, mixed, bias):
    start_half(mine_ref, 0, q, k, v, mixed, bias)


def attend_early(mine, q, k, v):
    _, heads, length, size = k.shape
    return pl.pallas_call(
        early_kernel,
        out_shape=jax.ShapeDtypeStruct((WD, heads * size, length // 2), jnp.float32),
        in_specs=[VMEM] * 4,
        out_specs=VMEM,
        scratch_shapes=[pltpu.VMEM((heads if length <= CHUNK else 2, length, length // 2), jnp.float32)],
        compiler_params=params(8 if length <= CHUNK else 40),
        cost_estimate=pl.CostEstimate(
            flops=4 * WD * heads * size * length * length,
            bytes_accessed=4 * WD * heads * length * length,
            transcendentals=WD * heads * length * length // 2,
        ),
        name="early",
    )(mine, q, k, v)


def attend_kernel(
    mine_ref, other_ref, early_ref, q0, k0, v0, g0,
    gain_ref, shift_ref, proj_ref, gate_ref, weight_ref, offset_ref,
    out0, out1, turned_bias, bias, late, mixed, q1, k1, v1, g1,
):
    chips, along, _, _ = mine_ref.shape
    _, heads, length, size = k0.shape
    half = length // 2
    rows = half // (chips * along)
    packed = 2 * heads * rows * (length // mine_ref.shape[3])
    first = pl.multiple_of(packed + lax.rem(lax.axis_index("col"), 2) * WD * rows, WD * rows)
    offset = turned(gate_ref[1:2, :])
    blocks = []
    for source in (mine_ref, other_ref):
        for flip in range(chips):
            for shift in range(along):
                both = source[flip, shift, pl.ds(first, WD * rows), :].astype(jnp.float32)
                blocks.append(both.reshape(WD, rows, -1))
    for w in range(WD):
        x = jnp.concatenate([block[w] for block in blocks], 0)
        normed = standardize(x) * gain_ref[1:2, :] + shift_ref[1:2, :]
        keys_and_values(normed.astype(jnp.bfloat16), proj_ref[1], k1, v1, w)
        ordered = to_devices(normed, along, chips, rows).astype(jnp.bfloat16)
        queries_and_gates(ordered, size ** (-0.5), proj_ref[1], offset, q1, g1, w)
    start_half(other_ref, 1, q0, k0, v0, late, turned_bias)
    for w in range(WD):
        gated = (jnp.concatenate([early_ref[w], late[w]], 1) * g0[w]).astype(jnp.bfloat16)
        full = contract(gated, weight_ref[0], 0, 0) + offset_ref[0:1, :]
        out0[w] = to_devices(full, along, chips, rows).astype(jnp.bfloat16)
    for pack in range(heads // 2):
        unpack(mine_ref, 1, pack, rows, heads, 0, bias, 0)
        unpack(other_ref, 1, pack, rows, heads, 0, bias, half)
        for i in range(2):
            part = slice((2 * pack + i) * size, (2 * pack + i + 1) * size)

            def step(chunk):
                there = pl.ds(chunk * CHUNK if length == CHUNK else pl.multiple_of(chunk * CHUNK, CHUNK), CHUNK)
                outs = softmax_mix(
                    [k1[w, 2 * pack + i] for w in range(WD)],
                    [q1[w, part, there] for w in range(WD)],
                    [v1[w, part, :] for w in range(WD)],
                    bias[(2 * pack + i) % bias.shape[0], :, there],
                )
                for w in range(WD):
                    mixed[w, part, there] = outs[w]

            for_each(length // CHUNK, step, length == CHUNK)
    for w in range(WD):
        gated = (mixed[w] * g1[w]).astype(jnp.bfloat16)
        full = contract(gated, weight_ref[1], 0, 0) + offset_ref[1:2, :]
        out1[w] = full.astype(jnp.bfloat16)


def attend(mine, other, early, start, gain, shift, proj, gate, weight, offset):
    _, heads, length, size = start[1].shape
    inner, channels = weight.shape[1:]
    result = jax.ShapeDtypeStruct((WD, length, channels), jnp.bfloat16)
    slots = heads if length <= CHUNK else 2
    return pl.pallas_call(
        attend_kernel,
        out_shape=(result, result),
        in_specs=[VMEM] * 13,
        out_specs=(VMEM, VMEM),
        scratch_shapes=[
            pltpu.VMEM((slots, length, length // 2), jnp.float32),
            pltpu.VMEM((slots, length, length), jnp.float32),
            pltpu.VMEM((WD, inner, length // 2), jnp.float32),
            pltpu.VMEM((WD, inner, length), jnp.float32),
        ]
        + [pltpu.VMEM(shape, dtype) for shape, dtype in projected(length, inner, heads)],
        compiler_params=params(16 if length <= CHUNK else 60),
        name="attend",
    )(mine, other, early, *start, gain, shift, proj, gate, weight, offset)


def body(pair, residue_mask, ln_gain, ln_shift, w_proj, w_bias, gate_bias, w_out, out_bias):
    rows, length, channels = pair.shape
    heads = w_bias.shape[2]
    along, cols = lax.axis_size("row"), lax.axis_size("col")
    chips = cols // 2

    def by_row(block, shift):
        return lax.ppermute(block, "row", [(i, (i + shift) % along) for i in range(along)])

    def by_col(block, flip):
        return lax.ppermute(block, "col", [(i, i ^ flip) for i in range(cols)])

    block, picks = local_bias(
        pair, residue_mask[None, :], ln_gain, ln_shift, jnp.transpose(w_bias, (0, 2, 1)), along, chips
    )
    line = jnp.stack([block] + [by_row(block, shift) for shift in range(1, along)])
    picked = jnp.stack([picks[0]] + [by_col(picks[flip], 2 * flip) for flip in range(1, chips)], 1)
    start = local_lines(pair, ln_gain, ln_shift, w_proj, gate_bias, heads, along, chips)
    shared = jnp.stack([line] + [by_col(line, 2 * flip) for flip in range(1, chips)])
    owned = jnp.stack([picked[0]] + [by_row(picked[shift], shift) for shift in range(1, along)], 1)
    mine = jnp.concatenate([shared, owned], 2)
    mine, _ = lax.optimization_barrier((mine, start))
    other = by_col(mine, 1)
    early = attend_early(mine, *start[:3])
    return attend(mine, other, early, start, ln_gain, ln_shift, w_proj, gate_bias, w_out, out_bias)


def solution(mesh):
    return jax.shard_map(
        body,
        mesh=mesh,
        in_specs=(P(("row", "col"), None, None), P(), P(), P(), P(), P(), P(), P(), P()),
        out_specs=(P(("row", "col"), None, None), P(("row", "col"), None, None)),
        check_vma=False,
    )
```

```python
import functools

import jax
import jax.numpy as jnp
from jax import lax
from jax.experimental import pallas as pl
from jax.experimental.pallas import tpu as pltpu
from jax.sharding import PartitionSpec as P

WD = 2
EPS = 1e-05
MASKED = -1000000000.0
CHUNK = 256
VMEM = pl.BlockSpec(memory_space=pltpu.VMEM)
HBM = pl.BlockSpec(memory_space=pltpu.HBM)


def params(megabytes):
    return pltpu.CompilerParams(vmem_limit_bytes=megabytes * 1024 * 1024)


def for_each(count, step, unrolled):
    if unrolled:
        for index in range(count):
            step(index)
    else:
        lax.fori_loop(0, count, lambda index, carry: (step(index), carry)[1], 0)


def standardize(wide):
    center = jnp.mean(wide, -1, keepdims=True)
    away = wide - center
    spread = jnp.mean(jnp.square(away), -1, keepdims=True)
    return away * lax.rsqrt(spread + EPS)


def contract(left, right, left_dim, right_dim):
    return lax.dot_general(
        left, right, (((left_dim,), (right_dim,)), ((), ())), preferred_element_type=jnp.float32
    )


def flipped(index, flip):
    bit = 1
    while bit <= flip:
        if flip & bit:
            index = index + bit - 2 * bit * lax.rem(lax.div(index, bit), 2)
        bit *= 2
    return index


def bias_kernel(along, chips, pair_hbm, live_hbm, gain_hbm, shift_hbm, weight_hbm, *rest):
    outs = rest[:along]
    pair, live_row, live_each, gain, shift, weight, blocks, rows_out, wide, picked, sems, pair_sems = rest[along:]
    rows, length, channels = pair.shape
    heads = weight.shape[1]
    lanes = outs[0].shape[1]
    small = [
        pltpu.make_async_copy(source, target, sems.at[i])
        for i, (source, target) in enumerate(
            ((live_hbm, live_row), (live_hbm, live_each), (gain_hbm, gain), (shift_hbm, shift), (weight_hbm, weight))
        )
    ]
    large = [pltpu.make_async_copy(pair_hbm.at[a], pair.at[a], pair_sems.at[a]) for a in range(rows)]
    large[0].start()
    for copy in small:
        copy.start()
    for copy in large[1:]:
        copy.start()
    device = lax.axis_index("row") * lax.axis_size("col") + lax.axis_index("col")
    for copy in small + large:
        copy.wait()
    blocks[...] = jnp.zeros_like(blocks)
    for p in range(2):
        at = slice(p * heads, (p + 1) * heads)
        blocks[at, p * channels : (p + 1) * channels] = weight[p].astype(jnp.float32)
    paired = blocks[: 2 * heads].astype(jnp.bfloat16)
    live = jnp.broadcast_to(live_row[...], (2 * heads, length))
    first = lax.broadcasted_iota(jnp.int32, live.shape, 0) < heads
    for a in range(rows):
        x = pair[a].astype(jnp.float32)
        wide[a] = x
        z = standardize(x)
        normed = jnp.concatenate(
            [(z * gain[p : p + 1, :] + shift[p : p + 1, :]).astype(jnp.bfloat16) for p in range(2)], 1
        )
        bias = contract(paired, normed, 1, 1)
        kept = jnp.where(first, live, live_each[0, device * rows + a])
        bias = jnp.where(kept > 0, bias, MASKED)
        for lane in range(length // lanes):
            part = bias[:, lane * lanes : (lane + 1) * lanes]
            rows_out[pl.ds(2 * lane * heads * rows + a, 2 * heads, stride=rows), :] = part
    devices = length // rows
    for a in range(rows):
        for w in range(WD):
            column = wide[a, pl.ds(w, devices, stride=rows), :]
            picked[pl.ds(w * rows + a, devices, stride=WD * rows), :] = column
    chip = lax.div(lax.axis_index("col"), 2)
    both = 2 * WD * rows
    packed = rows_out.shape[0]
    sent = rows_out[...].astype(jnp.bfloat16)
    for shift_by, out in enumerate(outs):
        out[:packed] = sent
        row = lax.rem(lax.axis_index("row") + shift_by, along)
        for flip in range(chips):
            at = pl.multiple_of((row * chips + flipped(chip, flip)) * both, both)
            out[packed + flip * both : packed + (flip + 1) * both] = picked[pl.ds(at, both), :].astype(jnp.bfloat16)


def local_bias(pair, live, gain, shift, weight, along, chips):
    rows, length, channels = pair.shape
    heads = weight.shape[1]
    packed = 2 * heads * rows * (length // channels)
    sent = jax.ShapeDtypeStruct((packed + chips * 2 * WD * rows, channels), jnp.bfloat16)
    return pl.pallas_call(
        functools.partial(bias_kernel, along, chips),
        out_shape=(sent,) * along,
        in_specs=[HBM] * 5,
        out_specs=(VMEM,) * along,
        scratch_shapes=[
            pltpu.VMEM(pair.shape, pair.dtype),
            pltpu.VMEM(live.shape, live.dtype),
            pltpu.SMEM(live.shape, live.dtype),
            pltpu.VMEM(gain.shape, gain.dtype),
            pltpu.VMEM(shift.shape, shift.dtype),
            pltpu.VMEM(weight.shape, weight.dtype),
            pltpu.VMEM((4 * heads, 2 * channels), jnp.float32),
            pltpu.VMEM((packed, channels), jnp.float32),
            pltpu.VMEM(pair.shape, jnp.float32),
            pltpu.VMEM((length * WD, channels), jnp.float32),
            pltpu.SemaphoreType.DMA((5,)),
            pltpu.SemaphoreType.DMA((rows,)),
        ],
        compiler_params=params(60),
        name="bias",
    )(pair, live, gain, shift, weight)


def turned(row):
    return jnp.broadcast_to(row, (row.shape[1], row.shape[1])).T[:, :1]


def turned_over(index, bit):
    return lax.rem(lax.div(index, bit), 2) == 1


def to_relative(x, along, chips, rows):
    row, col = lax.axis_index("row"), lax.axis_index("col")
    cols = 2 * chips
    grid = [[x[(r * cols + c) * rows : (r * cols + c + 1) * rows] for c in range(cols)] for r in range(along)]
    bit = 1
    while bit < cols:
        swap = turned_over(col, bit)
        grid = [[jnp.where(swap, line[c ^ bit], line[c]) for c in range(cols)] for line in grid]
        bit *= 2
    grid = [grid[-t % along] for t in range(along)]
    bit = 1
    while bit < along:
        move = turned_over(row, bit)
        grid = [
            [jnp.where(move, grid[(t - bit) % along][c], grid[t][c]) for c in range(cols)] for t in range(along)
        ]
        bit *= 2
    return jnp.concatenate(
        [grid[s][2 * flip + other] for other in range(2) for flip in range(chips) for s in range(along)], 0
    )


def to_devices(x, along, chips, rows):
    row, col = lax.axis_index("row"), lax.axis_index("col")
    cols = 2 * chips
    at = lambda c, s: (((c % 2) * chips + c // 2) * along + s) * rows
    grid = [[x[at(c, s) : at(c, s) + rows] for c in range(cols)] for s in range(along)]
    bit = 1
    while bit < along:
        move = turned_over(row, bit)
        grid = [
            [jnp.where(move, grid[(s + bit) % along][c], grid[s][c]) for c in range(cols)] for s in range(along)
        ]
        bit *= 2
    grid = [grid[-r % along] for r in range(along)]
    bit = 1
    while bit < cols:
        swap = turned_over(col, bit)
        grid = [[jnp.where(swap, line[c ^ bit], line[c]) for c in range(cols)] for line in grid]
        bit *= 2
    return jnp.concatenate([block for line in grid for block in line], 0)


def queries_and_gates(normed, scale, weight, offset, q_ref, g_ref, w):
    inner = weight.shape[1] // 4
    q_ref[w] = (contract(weight[:, :inner], normed, 0, 1) * scale).astype(jnp.bfloat16)
    g_ref[w] = jax.nn.sigmoid(contract(weight[:, 3 * inner :], normed, 0, 1) + offset)


def keys_and_values(normed, weight, k_ref, v_ref, w):
    _, heads, _, size = k_ref.shape
    inner = heads * size
    for h in range(heads):
        at = inner + h * size
        k_ref[w, h] = contract(normed, weight[:, at : at + size], 1, 0).astype(jnp.bfloat16)
    v_ref[w] = contract(weight[:, 2 * inner : 3 * inner], normed, 0, 1).astype(jnp.bfloat16)


def lines_kernel(along, chips, lines_ref, gain_ref, shift_ref, weight_ref, offset_ref, q_ref, k_ref, v_ref, g_ref):
    size = k_ref.shape[-1]
    rows = lines_ref.shape[1] // (2 * chips * along)
    offset = turned(offset_ref[0:1, :])
    weight = weight_ref[0]
    for w in range(WD):
        normed = standardize(lines_ref[w].astype(jnp.float32)) * gain_ref[0:1, :] + shift_ref[0:1, :]
        keys_and_values(normed.astype(jnp.bfloat16), weight, k_ref, v_ref, w)
        near = to_relative(normed, along, chips, rows).astype(jnp.bfloat16)
        queries_and_gates(near, size ** (-0.5), weight, offset, q_ref, g_ref, w)


def projected(length, inner, heads):
    wide = (WD, inner, length)
    return (
        (wide, jnp.bfloat16),
        ((WD, heads, length, inner // heads), jnp.bfloat16),
        (wide, jnp.bfloat16),
        (wide, jnp.float32),
    )


def local_lines(pair, gain, shift, weight, offset, heads, along, chips):
    _, length, channels = pair.shape
    wide = weight.shape[2]
    shapes = projected(length, wide // 4, heads)
    whole = lambda shape: pl.BlockSpec(shape, lambda i: (0,) * len(shape))
    return pl.pallas_call(
        functools.partial(lines_kernel, along, chips),
        grid=(1,),
        out_shape=tuple(jax.ShapeDtypeStruct(shape, dtype) for shape, dtype in shapes),
        in_specs=[
            whole((WD, length, channels)), whole(gain.shape), whole(gain.shape),
            whole((1, channels, wide)), whole(gain.shape),
        ],
        out_specs=tuple(whole(shape) for shape, _ in shapes),
        compiler_params=params(8 + length // 32),
        cost_estimate=pl.CostEstimate(
            flops=2 * WD * length * channels * wide, bytes_accessed=4 * WD * length * wide, transcendentals=0
        ),
        name="lines",
    )(pair, gain, shift, weight, offset)


def unpack(source, p, pack, rows, heads, turn, into, at):
    chips, along, _, lanes = source.shape
    packed = 2 * heads * rows
    half = chips * along * rows
    slots = into.shape[0]
    for lane in range(into.shape[2 - turn] // lanes):
        first = lane * packed + (p * heads + 2 * pack) * rows
        both = [
            source[flip, shift, first : first + 2 * rows, :].astype(jnp.float32)
            for flip in range(chips)
            for shift in range(along)
        ]
        there = slice(lane * lanes, (lane + 1) * lanes)
        for i in range(2):
            slot = (2 * pack + i) % slots
            block = jnp.concatenate([part[i * rows : (i + 1) * rows] for part in both], 0)
            if turn:
                into[slot, there, at : at + half] = block.T
            else:
                into[slot, at : at + half, there] = block


def softmax_mix(keys, queries, values, added):
    scores = [contract(k, q, 1, 0) + added for k, q in zip(keys, queries)]
    tops = [jnp.max(score, 0, keepdims=True) for score in scores]
    expos = [jnp.exp(score - top) for score, top in zip(scores, tops)]
    shares = [1.0 / jnp.sum(expo, 0, keepdims=True) for expo in expos]
    weights = [(expo * share).astype(jnp.bfloat16) for expo, share in zip(expos, shares)]
    return [contract(v, weight, 1, 0) for v, weight in zip(values, weights)]


def start_half(source, other, q, k, v, mixed, bias):
    _, heads, length, size = k.shape
    half = length // 2
    rows = half // (source.shape[0] * source.shape[1])
    width = min(half, CHUNK)
    for pack in range(heads // 2):
        unpack(source, 0, pack, rows, heads, 1, bias, 0)
        for i in range(2):
            part = slice((2 * pack + i) * size, (2 * pack + i + 1) * size)

            def step(chunk):
                near = pl.ds(chunk * width if half == width else pl.multiple_of(chunk * width, width), width)
                there = pl.ds(other * half + chunk * width, width)
                if half != width:
                    there = pl.ds(pl.multiple_of(other * half + chunk * width, width), width)
                outs = softmax_mix(
                    [k[w, 2 * pack + i] for w in range(WD)],
                    [q[w, part, there] for w in range(WD)],
                    [v[w, part, :] for w in range(WD)],
                    bias[(2 * pack + i) % bias.shape[0], :, near],
                )
                for w in range(WD):
                    mixed[w, part, near] = outs[w]

            for_each(half // width, step, half == width)


def early_kernel(mine_ref, q, k, v, mixed, bias):
    start_half(mine_ref, 0, q, k, v, mixed, bias)


def attend_early(mine, q, k, v):
    _, heads, length, size = k.shape
    return pl.pallas_call(
        early_kernel,
        out_shape=jax.ShapeDtypeStruct((WD, heads * size, length // 2), jnp.float32),
        in_specs=[VMEM] * 4,
        out_specs=VMEM,
        scratch_shapes=[pltpu.VMEM((heads if length <= CHUNK else 2, length, length // 2), jnp.float32)],
        compiler_params=params(8 if length <= CHUNK else 40),
        cost_estimate=pl.CostEstimate(
            flops=4 * WD * heads * size * length * length,
            bytes_accessed=4 * WD * heads * length * length,
            transcendentals=WD * heads * length * length // 2,
        ),
        name="early",
    )(mine, q, k, v)


def attend_kernel(
    mine_ref, other_ref, early_ref, q0, k0, v0, g0,
    gain_ref, shift_ref, proj_ref, gate_ref, weight_ref, offset_ref,
    out0, out1, turned_bias, bias, late, mixed, q1, k1, v1, g1,
):
    chips, along, _, _ = mine_ref.shape
    _, heads, length, size = k0.shape
    half = length // 2
    rows = half // (chips * along)
    packed = 2 * heads * rows * (length // mine_ref.shape[3])
    first = pl.multiple_of(packed + lax.rem(lax.axis_index("col"), 2) * WD * rows, WD * rows)
    offset = turned(gate_ref[1:2, :])
    blocks = []
    for source in (mine_ref, other_ref):
        for flip in range(chips):
            for shift in range(along):
                both = source[flip, shift, pl.ds(first, WD * rows), :].astype(jnp.float32)
                blocks.append(both.reshape(WD, rows, -1))
    for w in range(WD):
        x = jnp.concatenate([block[w] for block in blocks], 0)
        normed = standardize(x) * gain_ref[1:2, :] + shift_ref[1:2, :]
        keys_and_values(normed.astype(jnp.bfloat16), proj_ref[1], k1, v1, w)
        ordered = to_devices(normed, along, chips, rows).astype(jnp.bfloat16)
        queries_and_gates(ordered, size ** (-0.5), proj_ref[1], offset, q1, g1, w)
    start_half(other_ref, 1, q0, k0, v0, late, turned_bias)
    for w in range(WD):
        gated = (jnp.concatenate([early_ref[w], late[w]], 1) * g0[w]).astype(jnp.bfloat16)
        full = contract(gated, weight_ref[0], 0, 0) + offset_ref[0:1, :]
        out0[w] = to_devices(full, along, chips, rows).astype(jnp.bfloat16)
    for pack in range(heads // 2):
        unpack(mine_ref, 1, pack, rows, heads, 0, bias, 0)
        unpack(other_ref, 1, pack, rows, heads, 0, bias, half)
        for i in range(2):
            part = slice((2 * pack + i) * size, (2 * pack + i + 1) * size)

            def step(chunk):
                there = pl.ds(chunk * CHUNK if length == CHUNK else pl.multiple_of(chunk * CHUNK, CHUNK), CHUNK)
                outs = softmax_mix(
                    [k1[w, 2 * pack + i] for w in range(WD)],
                    [q1[w, part, there] for w in range(WD)],
                    [v1[w, part, :] for w in range(WD)],
                    bias[(2 * pack + i) % bias.shape[0], :, there],
                )
                for w in range(WD):
                    mixed[w, part, there] = outs[w]

            for_each(length // CHUNK, step, length == CHUNK)
    for w in range(WD):
        gated = (mixed[w] * g1[w]).astype(jnp.bfloat16)
        full = contract(gated, weight_ref[1], 0, 0) + offset_ref[1:2, :]
        out1[w] = full.astype(jnp.bfloat16)


def attend(mine, other, early, start, gain, shift, proj, gate, weight, offset):
    _, heads, length, size = start[1].shape
    inner, channels = weight.shape[1:]
    result = jax.ShapeDtypeStruct((WD, length, channels), jnp.bfloat16)
    slots = heads if length <= CHUNK else 2
    return pl.pallas_call(
        attend_kernel,
        out_shape=(result, result),
        in_specs=[VMEM] * 13,
        out_specs=(VMEM, VMEM),
        scratch_shapes=[
            pltpu.VMEM((slots, length, length // 2), jnp.float32),
            pltpu.VMEM((slots, length, length), jnp.float32),
            pltpu.VMEM((WD, inner, length // 2), jnp.float32),
            pltpu.VMEM((WD, inner, length), jnp.float32),
        ]
        + [pltpu.VMEM(shape, dtype) for shape, dtype in projected(length, inner, heads)],
        compiler_params=params(16 if length <= CHUNK else 60),
        name="attend",
    )(mine, other, early, *start, gain, shift, proj, gate, weight, offset)


def body(pair, residue_mask, ln_gain, ln_shift, w_proj, w_bias, gate_bias, w_out, out_bias):
    rows, length, channels = pair.shape
    heads = w_bias.shape[2]
    along, cols = lax.axis_size("row"), lax.axis_size("col")
    chips = cols // 2

    def by_row(block, shift):
        return lax.ppermute(block, "row", [(i, (i + shift) % along) for i in range(along)])

    def by_col(block, flip):
        return lax.ppermute(block, "col", [(i, i ^ flip) for i in range(cols)])

    sent = local_bias(
        pair, residue_mask[None, :], ln_gain, ln_shift, jnp.transpose(w_bias, (0, 2, 1)), along, chips
    )
    line = jnp.stack([sent[0]] + [by_row(sent[shift], shift) for shift in range(1, along)])
    start = local_lines(pair, ln_gain, ln_shift, w_proj, gate_bias, heads, along, chips)
    packed = 2 * heads * rows * (length // channels)
    both = 2 * WD * rows

    def owned_by(flip):
        at = packed + flip * both
        return jnp.concatenate([line[:, :packed], line[:, at : at + both]], 1)

    mine = jnp.stack([owned_by(0)] + [by_col(owned_by(flip), 2 * flip) for flip in range(1, chips)])
    mine, _ = lax.optimization_barrier((mine, start))
    other = by_col(mine, 1)
    early = attend_early(mine, *start[:3])
    return attend(mine, other, early, start, ln_gain, ln_shift, w_proj, gate_bias, w_out, out_bias)


def solution(mesh):
    return jax.shard_map(
        body,
        mesh=mesh,
        in_specs=(P(("row", "col"), None, None), P(), P(), P(), P(), P(), P(), P(), P()),
        out_specs=(P(("row", "col"), None, None), P(("row", "col"), None, None)),
        check_vma=False,
    )
```

```python
import functools

import jax
import jax.numpy as jnp
from jax import lax
from jax.experimental import pallas as pl
from jax.experimental.pallas import tpu as pltpu
from jax.sharding import PartitionSpec as P

WD = 2
EPS = 1e-05
MASKED = -1000000000.0
CHUNK = 128
WHOLE = 256
VMEM = pl.BlockSpec(memory_space=pltpu.VMEM)
HBM = pl.BlockSpec(memory_space=pltpu.HBM)


def params(megabytes):
    return pltpu.CompilerParams(vmem_limit_bytes=megabytes * 1024 * 1024)


def for_each(count, step, unrolled):
    if unrolled:
        for index in range(count):
            step(index)
    else:
        lax.fori_loop(0, count, lambda index, carry: (step(index), carry)[1], 0)


def standardize(wide):
    center = jnp.mean(wide, -1, keepdims=True)
    away = wide - center
    spread = jnp.mean(jnp.square(away), -1, keepdims=True)
    return away * lax.rsqrt(spread + EPS)


def contract(left, right, left_dim, right_dim):
    return lax.dot_general(
        left, right, (((left_dim,), (right_dim,)), ((), ())), preferred_element_type=jnp.float32
    )


def flipped(index, flip):
    bit = 1
    while bit <= flip:
        if flip & bit:
            index = index + bit - 2 * bit * lax.rem(lax.div(index, bit), 2)
        bit *= 2
    return index


def bias_kernel(along, chips, pair_hbm, live_hbm, gain_hbm, shift_hbm, weight_hbm, *rest):
    outs = rest[:along]
    pair, live_row, live_each, gain, shift, weight, blocks, rows_out, wide, picked, sems, pair_sems = rest[along:]
    rows, length, channels = pair.shape
    heads = weight.shape[1]
    lanes = outs[0].shape[1]
    small = [
        pltpu.make_async_copy(source, target, sems.at[i])
        for i, (source, target) in enumerate(
            ((live_hbm, live_row), (live_hbm, live_each), (gain_hbm, gain), (shift_hbm, shift), (weight_hbm, weight))
        )
    ]
    large = [pltpu.make_async_copy(pair_hbm.at[a], pair.at[a], pair_sems.at[a]) for a in range(rows)]
    large[0].start()
    for copy in small:
        copy.start()
    for copy in large[1:]:
        copy.start()
    device = lax.axis_index("row") * lax.axis_size("col") + lax.axis_index("col")
    for copy in small + large:
        copy.wait()
    blocks[...] = jnp.zeros_like(blocks)
    for p in range(2):
        at = slice(p * heads, (p + 1) * heads)
        blocks[at, p * channels : (p + 1) * channels] = weight[p].astype(jnp.float32)
    paired = blocks[: 2 * heads].astype(jnp.bfloat16)
    live = jnp.broadcast_to(live_row[...], (2 * heads, length))
    first = lax.broadcasted_iota(jnp.int32, live.shape, 0) < heads
    for a in range(rows):
        x = pair[a].astype(jnp.float32)
        wide[a] = x
        z = standardize(x)
        normed = jnp.concatenate(
            [(z * gain[p : p + 1, :] + shift[p : p + 1, :]).astype(jnp.bfloat16) for p in range(2)], 1
        )
        bias = contract(paired, normed, 1, 1)
        kept = jnp.where(first, live, live_each[0, device * rows + a])
        bias = jnp.where(kept > 0, bias, MASKED)
        for lane in range(length // lanes):
            part = bias[:, lane * lanes : (lane + 1) * lanes]
            rows_out[pl.ds(2 * lane * heads * rows + a, 2 * heads, stride=rows), :] = part
    devices = length // rows
    for a in range(rows):
        for w in range(WD):
            column = wide[a, pl.ds(w, devices, stride=rows), :]
            picked[pl.ds(w * rows + a, devices, stride=WD * rows), :] = column
    chip = lax.div(lax.axis_index("col"), 2)
    both = 2 * WD * rows
    packed = rows_out.shape[0]
    sent = rows_out[...].astype(jnp.bfloat16)
    for shift_by, out in enumerate(outs):
        out[:packed] = sent
        row = lax.rem(lax.axis_index("row") + shift_by, along)
        for flip in range(chips):
            at = pl.multiple_of((row * chips + flipped(chip, flip)) * both, both)
            out[packed + flip * both : packed + (flip + 1) * both] = picked[pl.ds(at, both), :].astype(jnp.bfloat16)


def local_bias(pair, live, gain, shift, weight, along, chips):
    rows, length, channels = pair.shape
    heads = weight.shape[1]
    packed = 2 * heads * rows * (length // channels)
    sent = jax.ShapeDtypeStruct((packed + chips * 2 * WD * rows, channels), jnp.bfloat16)
    return pl.pallas_call(
        functools.partial(bias_kernel, along, chips),
        out_shape=(sent,) * along,
        in_specs=[HBM] * 5,
        out_specs=(VMEM,) * along,
        scratch_shapes=[
            pltpu.VMEM(pair.shape, pair.dtype),
            pltpu.VMEM(live.shape, live.dtype),
            pltpu.SMEM(live.shape, live.dtype),
            pltpu.VMEM(gain.shape, gain.dtype),
            pltpu.VMEM(shift.shape, shift.dtype),
            pltpu.VMEM(weight.shape, weight.dtype),
            pltpu.VMEM((4 * heads, 2 * channels), jnp.float32),
            pltpu.VMEM((packed, channels), jnp.float32),
            pltpu.VMEM(pair.shape, jnp.float32),
            pltpu.VMEM((length * WD, channels), jnp.float32),
            pltpu.SemaphoreType.DMA((5,)),
            pltpu.SemaphoreType.DMA((rows,)),
        ],
        compiler_params=params(60),
        name="bias",
    )(pair, live, gain, shift, weight)


def turned(row):
    return jnp.broadcast_to(row, (row.shape[1], row.shape[1])).T[:, :1]


def turned_over(index, bit):
    return lax.rem(lax.div(index, bit), 2) == 1


def to_relative(x, along, chips, rows):
    row, col = lax.axis_index("row"), lax.axis_index("col")
    cols = 2 * chips
    grid = [[x[(r * cols + c) * rows : (r * cols + c + 1) * rows] for c in range(cols)] for r in range(along)]
    bit = 1
    while bit < cols:
        swap = turned_over(col, bit)
        grid = [[jnp.where(swap, line[c ^ bit], line[c]) for c in range(cols)] for line in grid]
        bit *= 2
    grid = [grid[-t % along] for t in range(along)]
    bit = 1
    while bit < along:
        move = turned_over(row, bit)
        grid = [
            [jnp.where(move, grid[(t - bit) % along][c], grid[t][c]) for c in range(cols)] for t in range(along)
        ]
        bit *= 2
    return jnp.concatenate(
        [grid[s][2 * flip + other] for other in range(2) for flip in range(chips) for s in range(along)], 0
    )


def to_devices(x, along, chips, rows):
    row, col = lax.axis_index("row"), lax.axis_index("col")
    cols = 2 * chips
    at = lambda c, s: (((c % 2) * chips + c // 2) * along + s) * rows
    grid = [[x[at(c, s) : at(c, s) + rows] for c in range(cols)] for s in range(along)]
    bit = 1
    while bit < along:
        move = turned_over(row, bit)
        grid = [
            [jnp.where(move, grid[(s + bit) % along][c], grid[s][c]) for c in range(cols)] for s in range(along)
        ]
        bit *= 2
    grid = [grid[-r % along] for r in range(along)]
    bit = 1
    while bit < cols:
        swap = turned_over(col, bit)
        grid = [[jnp.where(swap, line[c ^ bit], line[c]) for c in range(cols)] for line in grid]
        bit *= 2
    return jnp.concatenate([block for line in grid for block in line], 0)


def queries_and_gates(normed, scale, weight, offset, q_ref, g_ref, w):
    inner = weight.shape[1] // 4
    q_ref[w] = (contract(weight[:, :inner], normed, 0, 1) * scale).astype(jnp.bfloat16)
    g_ref[w] = jax.nn.sigmoid(contract(weight[:, 3 * inner :], normed, 0, 1) + offset)


def keys_and_values(normed, weight, k_ref, v_ref, w):
    _, heads, _, size = k_ref.shape
    inner = heads * size
    for h in range(heads):
        at = inner + h * size
        k_ref[w, h] = contract(normed, weight[:, at : at + size], 1, 0).astype(jnp.bfloat16)
    v_ref[w] = contract(weight[:, 2 * inner : 3 * inner], normed, 0, 1).astype(jnp.bfloat16)


def lines_kernel(along, chips, lines_ref, gain_ref, shift_ref, weight_ref, offset_ref, q_ref, k_ref, v_ref, g_ref):
    size = k_ref.shape[-1]
    rows = lines_ref.shape[1] // (2 * chips * along)
    offset = turned(offset_ref[0:1, :])
    weight = weight_ref[0]
    for w in range(WD):
        normed = standardize(lines_ref[w].astype(jnp.float32)) * gain_ref[0:1, :] + shift_ref[0:1, :]
        keys_and_values(normed.astype(jnp.bfloat16), weight, k_ref, v_ref, w)
        near = to_relative(normed, along, chips, rows).astype(jnp.bfloat16)
        queries_and_gates(near, size ** (-0.5), weight, offset, q_ref, g_ref, w)


def projected(length, inner, heads):
    wide = (WD, inner, length)
    return (
        (wide, jnp.bfloat16),
        ((WD, heads, length, inner // heads), jnp.bfloat16),
        (wide, jnp.bfloat16),
        (wide, jnp.float32),
    )


def local_lines(pair, gain, shift, weight, offset, heads, along, chips):
    _, length, channels = pair.shape
    wide = weight.shape[2]
    shapes = projected(length, wide // 4, heads)
    whole = lambda shape: pl.BlockSpec(shape, lambda i: (0,) * len(shape))
    return pl.pallas_call(
        functools.partial(lines_kernel, along, chips),
        grid=(1,),
        out_shape=tuple(jax.ShapeDtypeStruct(shape, dtype) for shape, dtype in shapes),
        in_specs=[
            whole((WD, length, channels)), whole(gain.shape), whole(gain.shape),
            whole((1, channels, wide)), whole(gain.shape),
        ],
        out_specs=tuple(whole(shape) for shape, _ in shapes),
        compiler_params=params(8 + length // 32),
        cost_estimate=pl.CostEstimate(
            flops=2 * WD * length * channels * wide, bytes_accessed=4 * WD * length * wide, transcendentals=0
        ),
        name="lines",
    )(pair, gain, shift, weight, offset)


def unpack(source, p, pack, rows, heads, turn, into, at):
    chips, along, _, lanes = source.shape
    packed = 2 * heads * rows
    half = chips * along * rows
    slots = into.shape[0]
    for lane in range(into.shape[2 - turn] // lanes):
        first = lane * packed + (p * heads + 2 * pack) * rows
        both = [
            source[flip, shift, first : first + 2 * rows, :].astype(jnp.float32)
            for flip in range(chips)
            for shift in range(along)
        ]
        there = slice(lane * lanes, (lane + 1) * lanes)
        for i in range(2):
            slot = (2 * pack + i) % slots
            block = jnp.concatenate([part[i * rows : (i + 1) * rows] for part in both], 0)
            if turn:
                into[slot, there, at : at + half] = block.T
            else:
                into[slot, at : at + half, there] = block


def softmax_mix(key, query, value, added):
    scores = contract(key, query, 1, 0) + added
    expo = jnp.exp(scores - jnp.max(scores, 0, keepdims=True))
    weights = expo * (1.0 / jnp.sum(expo, 0, keepdims=True))
    return contract(value, weights.astype(jnp.bfloat16), 1, 0)


def start_half(source, other, q, k, v, mixed, bias):
    _, heads, length, size = k.shape
    half = length // 2
    rows = half // (source.shape[0] * source.shape[1])
    width = min(half, CHUNK)
    unrolled = length <= WHOLE
    for pack in range(heads // 2):
        unpack(source, 0, pack, rows, heads, 1, bias, 0)
        for i in range(2):
            part = slice((2 * pack + i) * size, (2 * pack + i + 1) * size)

            def step(chunk):
                near = pl.ds(chunk * width if unrolled else pl.multiple_of(chunk * width, width), width)
                there = pl.ds(other * half + chunk * width, width)
                if not unrolled:
                    there = pl.ds(pl.multiple_of(other * half + chunk * width, width), width)
                for w in range(WD):
                    mixed[w, part, near] = softmax_mix(
                        k[w, 2 * pack + i], q[w, part, there], v[w, part, :],
                        bias[(2 * pack + i) % bias.shape[0], :, near],
                    )

            for_each(half // width, step, unrolled)


def early_kernel(mine_ref, q, k, v, mixed, bias):
    start_half(mine_ref, 0, q, k, v, mixed, bias)


def attend_early(mine, q, k, v):
    _, heads, length, size = k.shape
    return pl.pallas_call(
        early_kernel,
        out_shape=jax.ShapeDtypeStruct((WD, heads * size, length // 2), jnp.float32),
        in_specs=[VMEM] * 4,
        out_specs=VMEM,
        scratch_shapes=[pltpu.VMEM((heads if length <= WHOLE else 2, length, length // 2), jnp.float32)],
        compiler_params=params(8 if length <= WHOLE else 40),
        cost_estimate=pl.CostEstimate(
            flops=4 * WD * heads * size * length * length,
            bytes_accessed=4 * WD * heads * length * length,
            transcendentals=WD * heads * length * length // 2,
        ),
        name="early",
    )(mine, q, k, v)


def attend_kernel(
    mine_ref, other_ref, early_ref, q0, k0, v0, g0,
    gain_ref, shift_ref, proj_ref, gate_ref, weight_ref, offset_ref,
    out0, out1, turned_bias, bias, late, mixed, q1, k1, v1, g1,
):
    chips, along, _, _ = mine_ref.shape
    _, heads, length, size = k0.shape
    half = length // 2
    rows = half // (chips * along)
    packed = 2 * heads * rows * (length // mine_ref.shape[3])
    unrolled = length <= WHOLE
    first = pl.multiple_of(packed + lax.rem(lax.axis_index("col"), 2) * WD * rows, WD * rows)
    offset = turned(gate_ref[1:2, :])
    blocks = []
    for source in (mine_ref, other_ref):
        for flip in range(chips):
            for shift in range(along):
                both = source[flip, shift, pl.ds(first, WD * rows), :].astype(jnp.float32)
                blocks.append(both.reshape(WD, rows, -1))
    for w in range(WD):
        x = jnp.concatenate([block[w] for block in blocks], 0)
        normed = standardize(x) * gain_ref[1:2, :] + shift_ref[1:2, :]
        keys_and_values(normed.astype(jnp.bfloat16), proj_ref[1], k1, v1, w)
        ordered = to_devices(normed, along, chips, rows).astype(jnp.bfloat16)
        queries_and_gates(ordered, size ** (-0.5), proj_ref[1], offset, q1, g1, w)
    start_half(other_ref, 1, q0, k0, v0, late, turned_bias)
    for w in range(WD):
        gated = (jnp.concatenate([early_ref[w], late[w]], 1) * g0[w]).astype(jnp.bfloat16)
        full = contract(gated, weight_ref[0], 0, 0) + offset_ref[0:1, :]
        out0[w] = to_devices(full, along, chips, rows).astype(jnp.bfloat16)
    for pack in range(heads // 2):
        unpack(mine_ref, 1, pack, rows, heads, 0, bias, 0)
        unpack(other_ref, 1, pack, rows, heads, 0, bias, half)
        for i in range(2):
            part = slice((2 * pack + i) * size, (2 * pack + i + 1) * size)

            def step(chunk):
                there = pl.ds(chunk * CHUNK if unrolled else pl.multiple_of(chunk * CHUNK, CHUNK), CHUNK)
                for w in range(WD):
                    mixed[w, part, there] = softmax_mix(
                        k1[w, 2 * pack + i], q1[w, part, there], v1[w, part, :],
                        bias[(2 * pack + i) % bias.shape[0], :, there],
                    )

            for_each(length // CHUNK, step, unrolled)
    for w in range(WD):
        gated = (mixed[w] * g1[w]).astype(jnp.bfloat16)
        full = contract(gated, weight_ref[1], 0, 0) + offset_ref[1:2, :]
        out1[w] = full.astype(jnp.bfloat16)


def attend(mine, other, early, start, gain, shift, proj, gate, weight, offset):
    _, heads, length, size = start[1].shape
    inner, channels = weight.shape[1:]
    result = jax.ShapeDtypeStruct((WD, length, channels), jnp.bfloat16)
    slots = heads if length <= WHOLE else 2
    return pl.pallas_call(
        attend_kernel,
        out_shape=(result, result),
        in_specs=[VMEM] * 13,
        out_specs=(VMEM, VMEM),
        scratch_shapes=[
            pltpu.VMEM((slots, length, length // 2), jnp.float32),
            pltpu.VMEM((slots, length, length), jnp.float32),
            pltpu.VMEM((WD, inner, length // 2), jnp.float32),
            pltpu.VMEM((WD, inner, length), jnp.float32),
        ]
        + [pltpu.VMEM(shape, dtype) for shape, dtype in projected(length, inner, heads)],
        compiler_params=params(16 if length <= WHOLE else 60),
        name="attend",
    )(mine, other, early, *start, gain, shift, proj, gate, weight, offset)


def body(pair, residue_mask, ln_gain, ln_shift, w_proj, w_bias, gate_bias, w_out, out_bias):
    rows, length, channels = pair.shape
    heads = w_bias.shape[2]
    along, cols = lax.axis_size("row"), lax.axis_size("col")
    chips = cols // 2

    def by_row(block, shift):
        return lax.ppermute(block, "row", [(i, (i + shift) % along) for i in range(along)])

    def by_col(block, flip):
        return lax.ppermute(block, "col", [(i, i ^ flip) for i in range(cols)])

    sent = local_bias(
        pair, residue_mask[None, :], ln_gain, ln_shift, jnp.transpose(w_bias, (0, 2, 1)), along, chips
    )
    line = jnp.stack([sent[0]] + [by_row(sent[shift], shift) for shift in range(1, along)])
    start = local_lines(pair, ln_gain, ln_shift, w_proj, gate_bias, heads, along, chips)
    packed = 2 * heads * rows * (length // channels)
    both = 2 * WD * rows

    def owned_by(flip):
        at = packed + flip * both
        return jnp.concatenate([line[:, :packed], line[:, at : at + both]], 1)

    mine = jnp.stack([owned_by(0)] + [by_col(owned_by(flip), 2 * flip) for flip in range(1, chips)])
    mine, _ = lax.optimization_barrier((mine, start))
    other = by_col(mine, 1)
    early = attend_early(mine, *start[:3])
    return attend(mine, other, early, start, ln_gain, ln_shift, w_proj, gate_bias, w_out, out_bias)


def solution(mesh):
    return jax.shard_map(
        body,
        mesh=mesh,
        in_specs=(P(("row", "col"), None, None), P(), P(), P(), P(), P(), P(), P(), P()),
        out_specs=(P(("row", "col"), None, None), P(("row", "col"), None, None)),
        check_vma=False,
    )
```

```python
import functools

import jax
import jax.numpy as jnp
from jax import lax
from jax.experimental import pallas as pl
from jax.experimental.pallas import tpu as pltpu
from jax.sharding import PartitionSpec as P

WD = 2
EPS = 1e-05
MASKED = -1000000000.0
CHUNK = 256
VMEM = pl.BlockSpec(memory_space=pltpu.VMEM)
HBM = pl.BlockSpec(memory_space=pltpu.HBM)


def params(megabytes):
    return pltpu.CompilerParams(vmem_limit_bytes=megabytes * 1024 * 1024)


def for_each(count, step, unrolled):
    if unrolled:
        for index in range(count):
            step(index)
    else:
        lax.fori_loop(0, count, lambda index, carry: (step(index), carry)[1], 0)


def standardize(wide):
    center = jnp.mean(wide, -1, keepdims=True)
    away = wide - center
    spread = jnp.mean(jnp.square(away), -1, keepdims=True)
    return away * lax.rsqrt(spread + EPS)


def contract(left, right, left_dim, right_dim):
    return lax.dot_general(
        left, right, (((left_dim,), (right_dim,)), ((), ())), preferred_element_type=jnp.float32
    )


def flipped(index, flip):
    bit = 1
    while bit <= flip:
        if flip & bit:
            index = index + bit - 2 * bit * lax.rem(lax.div(index, bit), 2)
        bit *= 2
    return index


def bias_kernel(along, chips, pair_hbm, live_hbm, gain_hbm, shift_hbm, weight_hbm, *rest):
    outs = rest[:along]
    pair, live_row, live_each, gain, shift, weight, blocks, rows_out, wide, picked, sems, pair_sems = rest[along:]
    rows, length, channels = pair.shape
    heads = weight.shape[1]
    lanes = outs[0].shape[1]
    small = [
        pltpu.make_async_copy(source, target, sems.at[i])
        for i, (source, target) in enumerate(
            ((live_hbm, live_row), (live_hbm, live_each), (gain_hbm, gain), (shift_hbm, shift), (weight_hbm, weight))
        )
    ]
    large = [pltpu.make_async_copy(pair_hbm.at[a], pair.at[a], pair_sems.at[a]) for a in range(rows)]
    large[0].start()
    for copy in small:
        copy.start()
    for copy in large[1:]:
        copy.start()
    device = lax.axis_index("row") * lax.axis_size("col") + lax.axis_index("col")
    for copy in small + large:
        copy.wait()
    blocks[...] = jnp.zeros_like(blocks)
    for p in range(2):
        at = slice(p * heads, (p + 1) * heads)
        blocks[at, p * channels : (p + 1) * channels] = weight[p].astype(jnp.float32)
    paired = blocks[: 2 * heads].astype(jnp.bfloat16)
    live = jnp.broadcast_to(live_row[...], (2 * heads, length))
    first = lax.broadcasted_iota(jnp.int32, live.shape, 0) < heads
    for a in range(rows):
        x = pair[a].astype(jnp.float32)
        wide[a] = x
        z = standardize(x)
        normed = jnp.concatenate(
            [(z * gain[p : p + 1, :] + shift[p : p + 1, :]).astype(jnp.bfloat16) for p in range(2)], 1
        )
        bias = contract(paired, normed, 1, 1)
        kept = jnp.where(first, live, live_each[0, device * rows + a])
        bias = jnp.where(kept > 0, bias, MASKED)
        for lane in range(length // lanes):
            part = bias[:, lane * lanes : (lane + 1) * lanes]
            rows_out[pl.ds(2 * lane * heads * rows + a, 2 * heads, stride=rows), :] = part
    devices = length // rows
    for a in range(rows):
        for w in range(WD):
            column = wide[a, pl.ds(w, devices, stride=rows), :]
            picked[pl.ds(w * rows + a, devices, stride=WD * rows), :] = column
    chip = lax.div(lax.axis_index("col"), 2)
    both = 2 * WD * rows
    packed = rows_out.shape[0]
    sent = rows_out[...].astype(jnp.bfloat16)
    for shift_by, out in enumerate(outs):
        out[:packed] = sent
        row = lax.rem(lax.axis_index("row") + shift_by, along)
        for flip in range(chips):
            at = pl.multiple_of((row * chips + flipped(chip, flip)) * both, both)
            out[packed + flip * both : packed + (flip + 1) * both] = picked[pl.ds(at, both), :].astype(jnp.bfloat16)


def local_bias(pair, live, gain, shift, weight, along, chips):
    rows, length, channels = pair.shape
    heads = weight.shape[1]
    packed = 2 * heads * rows * (length // channels)
    sent = jax.ShapeDtypeStruct((packed + chips * 2 * WD * rows, channels), jnp.bfloat16)
    return pl.pallas_call(
        functools.partial(bias_kernel, along, chips),
        out_shape=(sent,) * along,
        in_specs=[HBM] * 5,
        out_specs=(VMEM,) * along,
        scratch_shapes=[
            pltpu.VMEM(pair.shape, pair.dtype),
            pltpu.VMEM(live.shape, live.dtype),
            pltpu.SMEM(live.shape, live.dtype),
            pltpu.VMEM(gain.shape, gain.dtype),
            pltpu.VMEM(shift.shape, shift.dtype),
            pltpu.VMEM(weight.shape, weight.dtype),
            pltpu.VMEM((4 * heads, 2 * channels), jnp.float32),
            pltpu.VMEM((packed, channels), jnp.float32),
            pltpu.VMEM(pair.shape, jnp.float32),
            pltpu.VMEM((length * WD, channels), jnp.float32),
            pltpu.SemaphoreType.DMA((5,)),
            pltpu.SemaphoreType.DMA((rows,)),
        ],
        compiler_params=params(60),
        name="bias",
    )(pair, live, gain, shift, weight)


def turned(row):
    return jnp.broadcast_to(row, (row.shape[1], row.shape[1])).T[:, :1]


def turned_over(index, bit):
    return lax.rem(lax.div(index, bit), 2) == 1


def to_relative(x, along, chips, rows):
    row, col = lax.axis_index("row"), lax.axis_index("col")
    cols = 2 * chips
    grid = [[x[(r * cols + c) * rows : (r * cols + c + 1) * rows] for c in range(cols)] for r in range(along)]
    bit = 1
    while bit < cols:
        swap = turned_over(col, bit)
        grid = [[jnp.where(swap, line[c ^ bit], line[c]) for c in range(cols)] for line in grid]
        bit *= 2
    grid = [grid[-t % along] for t in range(along)]
    bit = 1
    while bit < along:
        move = turned_over(row, bit)
        grid = [
            [jnp.where(move, grid[(t - bit) % along][c], grid[t][c]) for c in range(cols)] for t in range(along)
        ]
        bit *= 2
    return jnp.concatenate(
        [grid[s][2 * flip + other] for other in range(2) for flip in range(chips) for s in range(along)], 0
    )


def to_devices(x, along, chips, rows):
    row, col = lax.axis_index("row"), lax.axis_index("col")
    cols = 2 * chips
    at = lambda c, s: (((c % 2) * chips + c // 2) * along + s) * rows
    grid = [[x[at(c, s) : at(c, s) + rows] for c in range(cols)] for s in range(along)]
    bit = 1
    while bit < along:
        move = turned_over(row, bit)
        grid = [
            [jnp.where(move, grid[(s + bit) % along][c], grid[s][c]) for c in range(cols)] for s in range(along)
        ]
        bit *= 2
    grid = [grid[-r % along] for r in range(along)]
    bit = 1
    while bit < cols:
        swap = turned_over(col, bit)
        grid = [[jnp.where(swap, line[c ^ bit], line[c]) for c in range(cols)] for line in grid]
        bit *= 2
    return jnp.concatenate([block for line in grid for block in line], 0)


def queries_and_gates(normed, scale, weight, offset, q_ref, g_ref, w):
    inner = weight.shape[1] // 4
    q_ref[w] = (contract(weight[:, :inner], normed, 0, 1) * scale).astype(jnp.bfloat16)
    g_ref[w] = jax.nn.sigmoid(contract(weight[:, 3 * inner :], normed, 0, 1) + offset)


def keys_and_values(normed, weight, k_ref, v_ref, w):
    _, heads, _, size = k_ref.shape
    inner = heads * size
    for h in range(heads):
        at = inner + h * size
        k_ref[w, h] = contract(normed, weight[:, at : at + size], 1, 0).astype(jnp.bfloat16)
    v_ref[w] = contract(weight[:, 2 * inner : 3 * inner], normed, 0, 1).astype(jnp.bfloat16)


def lines_kernel(along, chips, lines_ref, gain_ref, shift_ref, weight_ref, offset_ref, q_ref, k_ref, v_ref, g_ref):
    size = k_ref.shape[-1]
    rows = lines_ref.shape[1] // (2 * chips * along)
    offset = turned(offset_ref[0:1, :])
    weight = weight_ref[0]
    for w in range(WD):
        normed = standardize(lines_ref[w].astype(jnp.float32)) * gain_ref[0:1, :] + shift_ref[0:1, :]
        keys_and_values(normed.astype(jnp.bfloat16), weight, k_ref, v_ref, w)
        near = to_relative(normed, along, chips, rows).astype(jnp.bfloat16)
        queries_and_gates(near, size ** (-0.5), weight, offset, q_ref, g_ref, w)


def projected(length, inner, heads):
    wide = (WD, inner, length)
    return (
        (wide, jnp.bfloat16),
        ((WD, heads, length, inner // heads), jnp.bfloat16),
        (wide, jnp.bfloat16),
        (wide, jnp.float32),
    )


def local_lines(pair, gain, shift, weight, offset, heads, along, chips):
    _, length, channels = pair.shape
    wide = weight.shape[2]
    shapes = projected(length, wide // 4, heads)
    whole = lambda shape: pl.BlockSpec(shape, lambda i: (0,) * len(shape))
    return pl.pallas_call(
        functools.partial(lines_kernel, along, chips),
        grid=(1,),
        out_shape=tuple(jax.ShapeDtypeStruct(shape, dtype) for shape, dtype in shapes),
        in_specs=[
            whole((WD, length, channels)), whole(gain.shape), whole(gain.shape),
            whole((1, channels, wide)), whole(gain.shape),
        ],
        out_specs=tuple(whole(shape) for shape, _ in shapes),
        compiler_params=params(8 + length // 32),
        cost_estimate=pl.CostEstimate(
            flops=2 * WD * length * channels * wide, bytes_accessed=4 * WD * length * wide, transcendentals=0
        ),
        name="lines",
    )(pair, gain, shift, weight, offset)


def unpack(source, p, pack, rows, heads, turn, into, at):
    chips, along, _, lanes = source.shape
    packed = 2 * heads * rows
    half = chips * along * rows
    slots = into.shape[0]
    for lane in range(into.shape[2 - turn] // lanes):
        first = lane * packed + (p * heads + 2 * pack) * rows
        both = [
            source[flip, shift, first : first + 2 * rows, :].astype(jnp.float32)
            for flip in range(chips)
            for shift in range(along)
        ]
        there = slice(lane * lanes, (lane + 1) * lanes)
        for i in range(2):
            slot = (2 * pack + i) % slots
            block = jnp.concatenate([part[i * rows : (i + 1) * rows] for part in both], 0)
            if turn:
                into[slot, there, at : at + half] = block.T
            else:
                into[slot, at : at + half, there] = block


def score(units):
    return [contract(key, query, 1, 0) + added for key, query, added, _ in units]


def mix(units, scores):
    tops = [jnp.max(part, 0, keepdims=True) for part in scores]
    expos = [jnp.exp(part - top) for part, top in zip(scores, tops)]
    shares = [1.0 / jnp.sum(expo, 0, keepdims=True) for expo in expos]
    weights = [(expo * share).astype(jnp.bfloat16) for expo, share in zip(expos, shares)]
    return [contract(unit[3], weight, 1, 0) for unit, weight in zip(units, weights)]


def attend_groups(groups):
    ready = score(groups[0][0]())
    for i, (units, put) in enumerate(groups):
        ahead = score(groups[i + 1][0]()) if i + 1 < len(groups) else None
        put(mix(units(), ready))
        ready = ahead


def head_group(heads, size, q, k, v, bias, mixed, there, near):
    def units():
        return [
            (k[w, h], q[w, h * size : (h + 1) * size, there], bias[h % bias.shape[0], :, near],
             v[w, h * size : (h + 1) * size, :])
            for h in heads
            for w in range(WD)
        ]

    def put(outs):
        for i, h in enumerate(heads):
            for w in range(WD):
                mixed[w, h * size : (h + 1) * size, near] = outs[i * WD + w]

    return units, put


def start_half(source, other, q, k, v, mixed, bias):
    _, heads, length, size = k.shape
    half = length // 2
    rows = half // (source.shape[0] * source.shape[1])
    width = min(half, CHUNK)
    if half == width:
        groups = []
        for pack in range(heads // 2):
            unpack(source, 0, pack, rows, heads, 1, bias, 0)
            groups.append(
                head_group(
                    (2 * pack, 2 * pack + 1), size, q, k, v, bias, mixed,
                    pl.ds(other * half, half), pl.ds(0, half),
                )
            )
        attend_groups(groups)
        return
    for pack in range(heads // 2):
        unpack(source, 0, pack, rows, heads, 1, bias, 0)

        def step(chunk):
            near = pl.ds(pl.multiple_of(chunk * width, width), width)
            there = pl.ds(pl.multiple_of(other * half + chunk * width, width), width)
            for h in (2 * pack, 2 * pack + 1):
                attend_groups([head_group((h,), size, q, k, v, bias, mixed, there, near)])

        for_each(half // width, step, False)


def early_kernel(mine_ref, q, k, v, mixed, bias):
    start_half(mine_ref, 0, q, k, v, mixed, bias)


def attend_early(mine, q, k, v):
    _, heads, length, size = k.shape
    return pl.pallas_call(
        early_kernel,
        out_shape=jax.ShapeDtypeStruct((WD, heads * size, length // 2), jnp.float32),
        in_specs=[VMEM] * 4,
        out_specs=VMEM,
        scratch_shapes=[pltpu.VMEM((heads if length <= CHUNK else 2, length, length // 2), jnp.float32)],
        compiler_params=params(8 if length <= CHUNK else 40),
        cost_estimate=pl.CostEstimate(
            flops=4 * WD * heads * size * length * length,
            bytes_accessed=4 * WD * heads * length * length,
            transcendentals=WD * heads * length * length // 2,
        ),
        name="early",
    )(mine, q, k, v)


def attend_kernel(
    mine_ref, other_ref, early_ref, q0, k0, v0, g0,
    gain_ref, shift_ref, proj_ref, gate_ref, weight_ref, offset_ref,
    out0, out1, turned_bias, bias, late, mixed, q1, k1, v1, g1,
):
    chips, along, _, _ = mine_ref.shape
    _, heads, length, size = k0.shape
    half = length // 2
    rows = half // (chips * along)
    packed = 2 * heads * rows * (length // mine_ref.shape[3])
    first = pl.multiple_of(packed + lax.rem(lax.axis_index("col"), 2) * WD * rows, WD * rows)
    offset = turned(gate_ref[1:2, :])
    blocks = []
    for source in (mine_ref, other_ref):
        for flip in range(chips):
            for shift in range(along):
                both = source[flip, shift, pl.ds(first, WD * rows), :].astype(jnp.float32)
                blocks.append(both.reshape(WD, rows, -1))
    for w in range(WD):
        x = jnp.concatenate([block[w] for block in blocks], 0)
        normed = standardize(x) * gain_ref[1:2, :] + shift_ref[1:2, :]
        keys_and_values(normed.astype(jnp.bfloat16), proj_ref[1], k1, v1, w)
        ordered = to_devices(normed, along, chips, rows).astype(jnp.bfloat16)
        queries_and_gates(ordered, size ** (-0.5), proj_ref[1], offset, q1, g1, w)
    start_half(other_ref, 1, q0, k0, v0, late, turned_bias)
    for w in range(WD):
        gated = (jnp.concatenate([early_ref[w], late[w]], 1) * g0[w]).astype(jnp.bfloat16)
        full = contract(gated, weight_ref[0], 0, 0) + offset_ref[0:1, :]
        out0[w] = to_devices(full, along, chips, rows).astype(jnp.bfloat16)
    groups = []
    for pack in range(heads // 2):
        unpack(mine_ref, 1, pack, rows, heads, 0, bias, 0)
        unpack(other_ref, 1, pack, rows, heads, 0, bias, half)
        pair = (2 * pack, 2 * pack + 1)
        if length == CHUNK:
            groups.append(
                head_group(pair, size, q1, k1, v1, bias, mixed, pl.ds(0, length), pl.ds(0, length))
            )
            continue

        def step(chunk):
            there = pl.ds(pl.multiple_of(chunk * CHUNK, CHUNK), CHUNK)
            for h in pair:
                attend_groups([head_group((h,), size, q1, k1, v1, bias, mixed, there, there)])

        for_each(length // CHUNK, step, False)
    if groups:
        attend_groups(groups)
    for w in range(WD):
        gated = (mixed[w] * g1[w]).astype(jnp.bfloat16)
        full = contract(gated, weight_ref[1], 0, 0) + offset_ref[1:2, :]
        out1[w] = full.astype(jnp.bfloat16)


def attend(mine, other, early, start, gain, shift, proj, gate, weight, offset):
    _, heads, length, size = start[1].shape
    inner, channels = weight.shape[1:]
    result = jax.ShapeDtypeStruct((WD, length, channels), jnp.bfloat16)
    slots = heads if length <= CHUNK else 2
    return pl.pallas_call(
        attend_kernel,
        out_shape=(result, result),
        in_specs=[VMEM] * 13,
        out_specs=(VMEM, VMEM),
        scratch_shapes=[
            pltpu.VMEM((slots, length, length // 2), jnp.float32),
            pltpu.VMEM((slots, length, length), jnp.float32),
            pltpu.VMEM((WD, inner, length // 2), jnp.float32),
            pltpu.VMEM((WD, inner, length), jnp.float32),
        ]
        + [pltpu.VMEM(shape, dtype) for shape, dtype in projected(length, inner, heads)],
        compiler_params=params(16 if length <= CHUNK else 60),
        name="attend",
    )(mine, other, early, *start, gain, shift, proj, gate, weight, offset)


def body(pair, residue_mask, ln_gain, ln_shift, w_proj, w_bias, gate_bias, w_out, out_bias):
    rows, length, channels = pair.shape
    heads = w_bias.shape[2]
    along, cols = lax.axis_size("row"), lax.axis_size("col")
    chips = cols // 2

    def by_row(block, shift):
        return lax.ppermute(block, "row", [(i, (i + shift) % along) for i in range(along)])

    def by_col(block, flip):
        return lax.ppermute(block, "col", [(i, i ^ flip) for i in range(cols)])

    sent = local_bias(
        pair, residue_mask[None, :], ln_gain, ln_shift, jnp.transpose(w_bias, (0, 2, 1)), along, chips
    )
    line = jnp.stack([sent[0]] + [by_row(sent[shift], shift) for shift in range(1, along)])
    start = local_lines(pair, ln_gain, ln_shift, w_proj, gate_bias, heads, along, chips)
    packed = 2 * heads * rows * (length // channels)
    both = 2 * WD * rows

    def owned_by(flip):
        at = packed + flip * both
        return jnp.concatenate([line[:, :packed], line[:, at : at + both]], 1)

    mine = jnp.stack([owned_by(0)] + [by_col(owned_by(flip), 2 * flip) for flip in range(1, chips)])
    mine, _ = lax.optimization_barrier((mine, start))
    other = by_col(mine, 1)
    early = attend_early(mine, *start[:3])
    return attend(mine, other, early, start, ln_gain, ln_shift, w_proj, gate_bias, w_out, out_bias)


def solution(mesh):
    return jax.shard_map(
        body,
        mesh=mesh,
        in_specs=(P(("row", "col"), None, None), P(), P(), P(), P(), P(), P(), P(), P()),
        out_specs=(P(("row", "col"), None, None), P(("row", "col"), None, None)),
        check_vma=False,
    )
```

```python
import functools

import jax
import jax.numpy as jnp
from jax import lax
from jax.experimental import pallas as pl
from jax.experimental.pallas import tpu as pltpu
from jax.sharding import PartitionSpec as P

WD = 2
EPS = 1e-05
MASKED = -1000000000.0
CHUNK = 256
VMEM = pl.BlockSpec(memory_space=pltpu.VMEM)
HBM = pl.BlockSpec(memory_space=pltpu.HBM)


def params(megabytes):
    return pltpu.CompilerParams(vmem_limit_bytes=megabytes * 1024 * 1024)


def for_each(count, step, unrolled):
    if unrolled:
        for index in range(count):
            step(index)
    else:
        lax.fori_loop(0, count, lambda index, carry: (step(index), carry)[1], 0)


def standardize_all(lines):
    centers = [jnp.mean(wide, -1, keepdims=True) for wide in lines]
    aways = [wide - center for wide, center in zip(lines, centers)]
    spreads = [jnp.mean(jnp.square(away), -1, keepdims=True) for away in aways]
    return [away * lax.rsqrt(spread + EPS) for away, spread in zip(aways, spreads)]


def contract(left, right, left_dim, right_dim):
    return lax.dot_general(
        left, right, (((left_dim,), (right_dim,)), ((), ())), preferred_element_type=jnp.float32
    )


def flipped(index, flip):
    bit = 1
    while bit <= flip:
        if flip & bit:
            index = index + bit - 2 * bit * lax.rem(lax.div(index, bit), 2)
        bit *= 2
    return index


def bias_kernel(along, chips, pair_hbm, live_hbm, gain_hbm, shift_hbm, weight_hbm, *rest):
    outs = rest[:along]
    pair, live_row, live_each, gain, shift, weight, blocks, rows_out, wide, picked, sems, pair_sems = rest[along:]
    rows, length, channels = pair.shape
    heads = weight.shape[1]
    lanes = outs[0].shape[1]
    small = [
        pltpu.make_async_copy(source, target, sems.at[i])
        for i, (source, target) in enumerate(
            ((live_hbm, live_row), (live_hbm, live_each), (gain_hbm, gain), (shift_hbm, shift), (weight_hbm, weight))
        )
    ]
    large = [pltpu.make_async_copy(pair_hbm.at[a], pair.at[a], pair_sems.at[a]) for a in range(rows)]
    large[0].start()
    for copy in small:
        copy.start()
    for copy in large[1:]:
        copy.start()
    device = lax.axis_index("row") * lax.axis_size("col") + lax.axis_index("col")
    for copy in small + large:
        copy.wait()
    blocks[...] = jnp.zeros_like(blocks)
    for p in range(2):
        at = slice(p * heads, (p + 1) * heads)
        blocks[at, p * channels : (p + 1) * channels] = weight[p].astype(jnp.float32)
    paired = blocks[: 2 * heads].astype(jnp.bfloat16)
    live = jnp.broadcast_to(live_row[...], (2 * heads, length))
    first = lax.broadcasted_iota(jnp.int32, live.shape, 0) < heads
    lines = [pair[a].astype(jnp.float32) for a in range(rows)]
    for a, x in enumerate(lines):
        wide[a] = x
    lines = standardize_all(lines)
    normed = [
        jnp.concatenate(
            [(z * gain[p : p + 1, :] + shift[p : p + 1, :]).astype(jnp.bfloat16) for p in range(2)], 1
        )
        for z in lines
    ]
    biases = [contract(paired, line, 1, 1) for line in normed]
    for a, bias in enumerate(biases):
        kept = jnp.where(first, live, live_each[0, device * rows + a])
        bias = jnp.where(kept > 0, bias, MASKED)
        for lane in range(length // lanes):
            part = bias[:, lane * lanes : (lane + 1) * lanes]
            rows_out[pl.ds(2 * lane * heads * rows + a, 2 * heads, stride=rows), :] = part
    devices = length // rows
    for a in range(rows):
        for w in range(WD):
            column = wide[a, pl.ds(w, devices, stride=rows), :]
            picked[pl.ds(w * rows + a, devices, stride=WD * rows), :] = column
    chip = lax.div(lax.axis_index("col"), 2)
    both = 2 * WD * rows
    packed = rows_out.shape[0]
    sent = rows_out[...].astype(jnp.bfloat16)
    for shift_by, out in enumerate(outs):
        out[:packed] = sent
        row = lax.rem(lax.axis_index("row") + shift_by, along)
        for flip in range(chips):
            at = pl.multiple_of((row * chips + flipped(chip, flip)) * both, both)
            out[packed + flip * both : packed + (flip + 1) * both] = picked[pl.ds(at, both), :].astype(jnp.bfloat16)


def local_bias(pair, live, gain, shift, weight, along, chips):
    rows, length, channels = pair.shape
    heads = weight.shape[1]
    packed = 2 * heads * rows * (length // channels)
    sent = jax.ShapeDtypeStruct((packed + chips * 2 * WD * rows, channels), jnp.bfloat16)
    return pl.pallas_call(
        functools.partial(bias_kernel, along, chips),
        out_shape=(sent,) * along,
        in_specs=[HBM] * 5,
        out_specs=(VMEM,) * along,
        scratch_shapes=[
            pltpu.VMEM(pair.shape, pair.dtype),
            pltpu.VMEM(live.shape, live.dtype),
            pltpu.SMEM(live.shape, live.dtype),
            pltpu.VMEM(gain.shape, gain.dtype),
            pltpu.VMEM(shift.shape, shift.dtype),
            pltpu.VMEM(weight.shape, weight.dtype),
            pltpu.VMEM((4 * heads, 2 * channels), jnp.float32),
            pltpu.VMEM((packed, channels), jnp.float32),
            pltpu.VMEM(pair.shape, jnp.float32),
            pltpu.VMEM((length * WD, channels), jnp.float32),
            pltpu.SemaphoreType.DMA((5,)),
            pltpu.SemaphoreType.DMA((rows,)),
        ],
        compiler_params=params(60),
        name="bias",
    )(pair, live, gain, shift, weight)


def turned(row):
    return jnp.broadcast_to(row, (row.shape[1], row.shape[1])).T[:, :1]


def turned_over(index, bit):
    return lax.rem(lax.div(index, bit), 2) == 1


def to_relative(x, along, chips, rows):
    row, col = lax.axis_index("row"), lax.axis_index("col")
    cols = 2 * chips
    grid = [[x[(r * cols + c) * rows : (r * cols + c + 1) * rows] for c in range(cols)] for r in range(along)]
    bit = 1
    while bit < cols:
        swap = turned_over(col, bit)
        grid = [[jnp.where(swap, line[c ^ bit], line[c]) for c in range(cols)] for line in grid]
        bit *= 2
    grid = [grid[-t % along] for t in range(along)]
    bit = 1
    while bit < along:
        move = turned_over(row, bit)
        grid = [
            [jnp.where(move, grid[(t - bit) % along][c], grid[t][c]) for c in range(cols)] for t in range(along)
        ]
        bit *= 2
    return jnp.concatenate(
        [grid[s][2 * flip + other] for other in range(2) for flip in range(chips) for s in range(along)], 0
    )


def to_devices(x, along, chips, rows):
    row, col = lax.axis_index("row"), lax.axis_index("col")
    cols = 2 * chips
    at = lambda c, s: (((c % 2) * chips + c // 2) * along + s) * rows
    grid = [[x[at(c, s) : at(c, s) + rows] for c in range(cols)] for s in range(along)]
    bit = 1
    while bit < along:
        move = turned_over(row, bit)
        grid = [
            [jnp.where(move, grid[(s + bit) % along][c], grid[s][c]) for c in range(cols)] for s in range(along)
        ]
        bit *= 2
    grid = [grid[-r % along] for r in range(along)]
    bit = 1
    while bit < cols:
        swap = turned_over(col, bit)
        grid = [[jnp.where(swap, line[c ^ bit], line[c]) for c in range(cols)] for line in grid]
        bit *= 2
    return jnp.concatenate([block for line in grid for block in line], 0)


def queries_and_gates(lines, scale, weight, offset, q_ref, g_ref):
    inner = weight.shape[1] // 4
    queries = [contract(weight[:, :inner], normed, 0, 1) for normed in lines]
    gates = [contract(weight[:, 3 * inner :], normed, 0, 1) for normed in lines]
    for w in range(WD):
        q_ref[w] = (queries[w] * scale).astype(jnp.bfloat16)
        g_ref[w] = jax.nn.sigmoid(gates[w] + offset)


def keys_and_values(lines, weight, k_ref, v_ref):
    _, heads, _, size = k_ref.shape
    inner = heads * size
    for h in range(heads):
        at = inner + h * size
        keys = [contract(normed, weight[:, at : at + size], 1, 0) for normed in lines]
        for w in range(WD):
            k_ref[w, h] = keys[w].astype(jnp.bfloat16)
    values = [contract(weight[:, 2 * inner : 3 * inner], normed, 0, 1) for normed in lines]
    for w in range(WD):
        v_ref[w] = values[w].astype(jnp.bfloat16)


def lines_kernel(along, chips, lines_ref, gain_ref, shift_ref, weight_ref, offset_ref, q_ref, k_ref, v_ref, g_ref):
    size = k_ref.shape[-1]
    rows = lines_ref.shape[1] // (2 * chips * along)
    offset = turned(offset_ref[0:1, :])
    weight = weight_ref[0]
    lines = standardize_all([lines_ref[w].astype(jnp.float32) for w in range(WD)])
    lines = [line * gain_ref[0:1, :] + shift_ref[0:1, :] for line in lines]
    keys_and_values([line.astype(jnp.bfloat16) for line in lines], weight, k_ref, v_ref)
    near = [to_relative(line, along, chips, rows).astype(jnp.bfloat16) for line in lines]
    queries_and_gates(near, size ** (-0.5), weight, offset, q_ref, g_ref)


def projected(length, inner, heads):
    wide = (WD, inner, length)
    return (
        (wide, jnp.bfloat16),
        ((WD, heads, length, inner // heads), jnp.bfloat16),
        (wide, jnp.bfloat16),
        (wide, jnp.float32),
    )


def local_lines(pair, gain, shift, weight, offset, heads, along, chips):
    _, length, channels = pair.shape
    wide = weight.shape[2]
    shapes = projected(length, wide // 4, heads)
    whole = lambda shape: pl.BlockSpec(shape, lambda i: (0,) * len(shape))
    return pl.pallas_call(
        functools.partial(lines_kernel, along, chips),
        grid=(1,),
        out_shape=tuple(jax.ShapeDtypeStruct(shape, dtype) for shape, dtype in shapes),
        in_specs=[
            whole((WD, length, channels)), whole(gain.shape), whole(gain.shape),
            whole((1, channels, wide)), whole(gain.shape),
        ],
        out_specs=tuple(whole(shape) for shape, _ in shapes),
        compiler_params=params(8 + length // 32),
        cost_estimate=pl.CostEstimate(
            flops=2 * WD * length * channels * wide, bytes_accessed=4 * WD * length * wide, transcendentals=0
        ),
        name="lines",
    )(pair, gain, shift, weight, offset)


def unpack(source, p, pack, rows, heads, turn, into, at):
    chips, along, _, lanes = source.shape
    packed = 2 * heads * rows
    half = chips * along * rows
    slots = into.shape[0]
    for lane in range(into.shape[2 - turn] // lanes):
        first = lane * packed + (p * heads + 2 * pack) * rows
        both = [
            source[flip, shift, first : first + 2 * rows, :].astype(jnp.float32)
            for flip in range(chips)
            for shift in range(along)
        ]
        there = slice(lane * lanes, (lane + 1) * lanes)
        for i in range(2):
            slot = (2 * pack + i) % slots
            block = jnp.concatenate([part[i * rows : (i + 1) * rows] for part in both], 0)
            if turn:
                into[slot, there, at : at + half] = block.T
            else:
                into[slot, at : at + half, there] = block


def score(units):
    return [contract(key, query, 1, 0) + added for key, query, added, _ in units]


def mix(units, scores):
    tops = [jnp.max(part, 0, keepdims=True) for part in scores]
    expos = [jnp.exp(part - top) for part, top in zip(scores, tops)]
    shares = [1.0 / jnp.sum(expo, 0, keepdims=True) for expo in expos]
    weights = [(expo * share).astype(jnp.bfloat16) for expo, share in zip(expos, shares)]
    return [contract(unit[3], weight, 1, 0) for unit, weight in zip(units, weights)]


def attend_groups(groups):
    if not groups:
        return
    ready = score(groups[0][0]())
    for i, (units, put) in enumerate(groups):
        ahead = score(groups[i + 1][0]()) if i + 1 < len(groups) else None
        put(mix(units(), ready))
        ready = ahead


def head_group(heads, size, q, k, v, bias, mixed, there, near):
    def units():
        return [
            (k[w, h], q[w, h * size : (h + 1) * size, there], bias[h % bias.shape[0], :, near],
             v[w, h * size : (h + 1) * size, :])
            for h in heads
            for w in range(WD)
        ]

    def put(outs):
        for i, h in enumerate(heads):
            for w in range(WD):
                mixed[w, h * size : (h + 1) * size, near] = outs[i * WD + w]

    return units, put


def start_half(source, other, q, k, v, mixed, bias):
    _, heads, length, size = k.shape
    half = length // 2
    rows = half // (source.shape[0] * source.shape[1])
    width = min(half, CHUNK)
    if half == width:
        groups = []
        for pack in range(heads // 2):
            unpack(source, 0, pack, rows, heads, 1, bias, 0)
            groups.append(
                head_group(
                    (2 * pack, 2 * pack + 1), size, q, k, v, bias, mixed,
                    pl.ds(other * half, half), pl.ds(0, half),
                )
            )
        return groups
    for pack in range(heads // 2):
        unpack(source, 0, pack, rows, heads, 1, bias, 0)

        def step(chunk):
            near = pl.ds(pl.multiple_of(chunk * width, width), width)
            there = pl.ds(pl.multiple_of(other * half + chunk * width, width), width)
            for h in (2 * pack, 2 * pack + 1):
                attend_groups([head_group((h,), size, q, k, v, bias, mixed, there, near)])

        for_each(half // width, step, False)
    return []


def early_kernel(mine_ref, q, k, v, mixed, bias):
    attend_groups(start_half(mine_ref, 0, q, k, v, mixed, bias))


def attend_early(mine, q, k, v):
    _, heads, length, size = k.shape
    return pl.pallas_call(
        early_kernel,
        out_shape=jax.ShapeDtypeStruct((WD, heads * size, length // 2), jnp.float32),
        in_specs=[VMEM] * 4,
        out_specs=VMEM,
        scratch_shapes=[pltpu.VMEM((heads if length <= CHUNK else 2, length, length // 2), jnp.float32)],
        compiler_params=params(8 if length <= CHUNK else 40),
        cost_estimate=pl.CostEstimate(
            flops=4 * WD * heads * size * length * length,
            bytes_accessed=4 * WD * heads * length * length,
            transcendentals=WD * heads * length * length // 2,
        ),
        name="early",
    )(mine, q, k, v)


def attend_kernel(
    mine_ref, other_ref, early_ref, q0, k0, v0, g0,
    gain_ref, shift_ref, proj_ref, gate_ref, weight_ref, offset_ref,
    out0, out1, turned_bias, bias, late, mixed, q1, k1, v1, g1,
):
    chips, along, _, _ = mine_ref.shape
    _, heads, length, size = k0.shape
    half = length // 2
    rows = half // (chips * along)
    packed = 2 * heads * rows * (length // mine_ref.shape[3])
    first = pl.multiple_of(packed + lax.rem(lax.axis_index("col"), 2) * WD * rows, WD * rows)
    offset = turned(gate_ref[1:2, :])
    blocks = []
    for source in (mine_ref, other_ref):
        for flip in range(chips):
            for shift in range(along):
                both = source[flip, shift, pl.ds(first, WD * rows), :].astype(jnp.float32)
                blocks.append(both.reshape(WD, rows, -1))
    lines = standardize_all([jnp.concatenate([block[w] for block in blocks], 0) for w in range(WD)])
    lines = [line * gain_ref[1:2, :] + shift_ref[1:2, :] for line in lines]
    keys_and_values([line.astype(jnp.bfloat16) for line in lines], proj_ref[1], k1, v1)
    ordered = [to_devices(line, along, chips, rows).astype(jnp.bfloat16) for line in lines]
    queries_and_gates(ordered, size ** (-0.5), proj_ref[1], offset, q1, g1)
    groups = start_half(other_ref, 1, q0, k0, v0, late, turned_bias)
    for pack in range(heads // 2):
        unpack(mine_ref, 1, pack, rows, heads, 0, bias, 0)
        unpack(other_ref, 1, pack, rows, heads, 0, bias, half)
        pair = (2 * pack, 2 * pack + 1)
        if length == CHUNK:
            groups.append(
                head_group(pair, size, q1, k1, v1, bias, mixed, pl.ds(0, length), pl.ds(0, length))
            )
            continue

        def step(chunk):
            there = pl.ds(pl.multiple_of(chunk * CHUNK, CHUNK), CHUNK)
            for h in pair:
                attend_groups([head_group((h,), size, q1, k1, v1, bias, mixed, there, there)])

        for_each(length // CHUNK, step, False)
    attend_groups(groups)
    for w in range(WD):
        gated = (jnp.concatenate([early_ref[w], late[w]], 1) * g0[w]).astype(jnp.bfloat16)
        full = contract(gated, weight_ref[0], 0, 0) + offset_ref[0:1, :]
        out0[w] = to_devices(full, along, chips, rows).astype(jnp.bfloat16)
    for w in range(WD):
        gated = (mixed[w] * g1[w]).astype(jnp.bfloat16)
        full = contract(gated, weight_ref[1], 0, 0) + offset_ref[1:2, :]
        out1[w] = full.astype(jnp.bfloat16)


def attend(mine, other, early, start, gain, shift, proj, gate, weight, offset):
    _, heads, length, size = start[1].shape
    inner, channels = weight.shape[1:]
    result = jax.ShapeDtypeStruct((WD, length, channels), jnp.bfloat16)
    slots = heads if length <= CHUNK else 2
    return pl.pallas_call(
        attend_kernel,
        out_shape=(result, result),
        in_specs=[VMEM] * 13,
        out_specs=(VMEM, VMEM),
        scratch_shapes=[
            pltpu.VMEM((slots, length, length // 2), jnp.float32),
            pltpu.VMEM((slots, length, length), jnp.float32),
            pltpu.VMEM((WD, inner, length // 2), jnp.float32),
            pltpu.VMEM((WD, inner, length), jnp.float32),
        ]
        + [pltpu.VMEM(shape, dtype) for shape, dtype in projected(length, inner, heads)],
        compiler_params=params(16 if length <= CHUNK else 60),
        name="attend",
    )(mine, other, early, *start, gain, shift, proj, gate, weight, offset)


def body(pair, residue_mask, ln_gain, ln_shift, w_proj, w_bias, gate_bias, w_out, out_bias):
    rows, length, channels = pair.shape
    heads = w_bias.shape[2]
    along, cols = lax.axis_size("row"), lax.axis_size("col")
    chips = cols // 2

    def by_row(block, shift):
        return lax.ppermute(block, "row", [(i, (i + shift) % along) for i in range(along)])

    def by_col(block, flip):
        return lax.ppermute(block, "col", [(i, i ^ flip) for i in range(cols)])

    sent = local_bias(
        pair, residue_mask[None, :], ln_gain, ln_shift, jnp.transpose(w_bias, (0, 2, 1)), along, chips
    )
    line = jnp.stack([sent[0]] + [by_row(sent[shift], shift) for shift in range(1, along)])
    start = local_lines(pair, ln_gain, ln_shift, w_proj, gate_bias, heads, along, chips)
    packed = 2 * heads * rows * (length // channels)
    both = 2 * WD * rows

    def owned_by(flip):
        at = packed + flip * both
        return jnp.concatenate([line[:, :packed], line[:, at : at + both]], 1)

    mine = jnp.stack([owned_by(0)] + [by_col(owned_by(flip), 2 * flip) for flip in range(1, chips)])
    mine, _ = lax.optimization_barrier((mine, start))
    other = by_col(mine, 1)
    early = attend_early(mine, *start[:3])
    return attend(mine, other, early, start, ln_gain, ln_shift, w_proj, gate_bias, w_out, out_bias)


def solution(mesh):
    return jax.shard_map(
        body,
        mesh=mesh,
        in_specs=(P(("row", "col"), None, None), P(), P(), P(), P(), P(), P(), P(), P()),
        out_specs=(P(("row", "col"), None, None), P(("row", "col"), None, None)),
        check_vma=False,
    )
```

```python
import functools

import jax
import jax.numpy as jnp
from jax import lax
from jax.experimental import pallas as pl
from jax.experimental.pallas import tpu as pltpu
from jax.sharding import PartitionSpec as P

WD = 2
EPS = 1e-05
MASKED = -1000000000.0
CHUNK = 256
VMEM = pl.BlockSpec(memory_space=pltpu.VMEM)
HBM = pl.BlockSpec(memory_space=pltpu.HBM)


def params(megabytes):
    return pltpu.CompilerParams(vmem_limit_bytes=megabytes * 1024 * 1024)


def for_each(count, step, unrolled):
    if unrolled:
        for index in range(count):
            step(index)
    else:
        lax.fori_loop(0, count, lambda index, carry: (step(index), carry)[1], 0)


def standardize_all(lines):
    centers = [jnp.mean(wide, -1, keepdims=True) for wide in lines]
    aways = [wide - center for wide, center in zip(lines, centers)]
    spreads = [jnp.mean(jnp.square(away), -1, keepdims=True) for away in aways]
    return [away * lax.rsqrt(spread + EPS) for away, spread in zip(aways, spreads)]


def contract(left, right, left_dim, right_dim):
    return lax.dot_general(
        left, right, (((left_dim,), (right_dim,)), ((), ())), preferred_element_type=jnp.float32
    )


def flipped(index, flip):
    bit = 1
    while bit <= flip:
        if flip & bit:
            index = index + bit - 2 * bit * lax.rem(lax.div(index, bit), 2)
        bit *= 2
    return index


def bias_kernel(along, chips, pair_hbm, live_hbm, gain_hbm, shift_hbm, weight_hbm, *rest):
    out, owned = rest[0], rest[1 : along + 1]
    pair, live_row, live_each, gain, shift, weight, blocks, rows_out, wide, picked, sems, pair_sems = rest[along + 1 :]
    rows, length, channels = pair.shape
    heads = weight.shape[1]
    lanes = out.shape[1]
    small = [
        pltpu.make_async_copy(source, target, sems.at[i])
        for i, (source, target) in enumerate(
            ((live_hbm, live_row), (live_hbm, live_each), (gain_hbm, gain), (shift_hbm, shift), (weight_hbm, weight))
        )
    ]
    large = [pltpu.make_async_copy(pair_hbm.at[a], pair.at[a], pair_sems.at[a]) for a in range(rows)]
    large[0].start()
    for copy in small:
        copy.start()
    for copy in large[1:]:
        copy.start()
    device = lax.axis_index("row") * lax.axis_size("col") + lax.axis_index("col")
    for copy in small + large:
        copy.wait()
    blocks[...] = jnp.zeros_like(blocks)
    for p in range(2):
        at = slice(p * heads, (p + 1) * heads)
        blocks[at, p * channels : (p + 1) * channels] = weight[p].astype(jnp.float32)
    paired = blocks[: 2 * heads].astype(jnp.bfloat16)
    live = jnp.broadcast_to(live_row[...], (2 * heads, length))
    first = lax.broadcasted_iota(jnp.int32, live.shape, 0) < heads
    lines = [pair[a].astype(jnp.float32) for a in range(rows)]
    for a, x in enumerate(lines):
        wide[a] = x
    lines = standardize_all(lines)
    normed = [
        jnp.concatenate(
            [(z * gain[p : p + 1, :] + shift[p : p + 1, :]).astype(jnp.bfloat16) for p in range(2)], 1
        )
        for z in lines
    ]
    biases = [contract(paired, line, 1, 1) for line in normed]
    devices = length // rows
    for a in range(rows):
        for w in range(WD):
            column = wide[a, pl.ds(w, devices, stride=rows), :]
            picked[pl.ds(w * rows + a, devices, stride=WD * rows), :] = column
    for a, bias in enumerate(biases):
        kept = jnp.where(first, live, live_each[0, device * rows + a])
        bias = jnp.where(kept > 0, bias, MASKED)
        for lane in range(length // lanes):
            part = bias[:, lane * lanes : (lane + 1) * lanes]
            rows_out[pl.ds(2 * lane * heads * rows + a, 2 * heads, stride=rows), :] = part
    out[...] = rows_out[...].astype(jnp.bfloat16)
    chip = lax.div(lax.axis_index("col"), 2)
    both = 2 * WD * rows
    for shift_by, pick in enumerate(owned):
        row = lax.rem(lax.axis_index("row") + shift_by, along)
        for flip in range(chips):
            at = pl.multiple_of((row * chips + flipped(chip, flip)) * both, both)
            pick[flip] = picked[pl.ds(at, both), :].astype(jnp.bfloat16)


def local_bias(pair, live, gain, shift, weight, along, chips):
    rows, length, channels = pair.shape
    heads = weight.shape[1]
    packed = 2 * heads * rows * (length // channels)
    owned = jax.ShapeDtypeStruct((chips, 2 * WD * rows, channels), jnp.bfloat16)
    out = pl.pallas_call(
        functools.partial(bias_kernel, along, chips),
        out_shape=(jax.ShapeDtypeStruct((packed, channels), jnp.bfloat16),) + (owned,) * along,
        in_specs=[HBM] * 5,
        out_specs=(VMEM,) * (along + 1),
        scratch_shapes=[
            pltpu.VMEM(pair.shape, pair.dtype),
            pltpu.VMEM(live.shape, live.dtype),
            pltpu.SMEM(live.shape, live.dtype),
            pltpu.VMEM(gain.shape, gain.dtype),
            pltpu.VMEM(shift.shape, shift.dtype),
            pltpu.VMEM(weight.shape, weight.dtype),
            pltpu.VMEM((4 * heads, 2 * channels), jnp.float32),
            pltpu.VMEM((packed, channels), jnp.float32),
            pltpu.VMEM(pair.shape, jnp.float32),
            pltpu.VMEM((length * WD, channels), jnp.float32),
            pltpu.SemaphoreType.DMA((5,)),
            pltpu.SemaphoreType.DMA((rows,)),
        ],
        compiler_params=params(60),
        name="bias",
    )(pair, live, gain, shift, weight)
    return out[0], out[1:]


def turned(row):
    return jnp.broadcast_to(row, (row.shape[1], row.shape[1])).T[:, :1]


def turned_over(index, bit):
    return lax.rem(lax.div(index, bit), 2) == 1


def to_relative(x, along, chips, rows):
    row, col = lax.axis_index("row"), lax.axis_index("col")
    cols = 2 * chips
    grid = [[x[(r * cols + c) * rows : (r * cols + c + 1) * rows] for c in range(cols)] for r in range(along)]
    bit = 1
    while bit < cols:
        swap = turned_over(col, bit)
        grid = [[jnp.where(swap, line[c ^ bit], line[c]) for c in range(cols)] for line in grid]
        bit *= 2
    grid = [grid[-t % along] for t in range(along)]
    bit = 1
    while bit < along:
        move = turned_over(row, bit)
        grid = [
            [jnp.where(move, grid[(t - bit) % along][c], grid[t][c]) for c in range(cols)] for t in range(along)
        ]
        bit *= 2
    return jnp.concatenate(
        [grid[s][2 * flip + other] for other in range(2) for flip in range(chips) for s in range(along)], 0
    )


def to_devices(x, along, chips, rows):
    row, col = lax.axis_index("row"), lax.axis_index("col")
    cols = 2 * chips
    at = lambda c, s: (((c % 2) * chips + c // 2) * along + s) * rows
    grid = [[x[at(c, s) : at(c, s) + rows] for c in range(cols)] for s in range(along)]
    bit = 1
    while bit < along:
        move = turned_over(row, bit)
        grid = [
            [jnp.where(move, grid[(s + bit) % along][c], grid[s][c]) for c in range(cols)] for s in range(along)
        ]
        bit *= 2
    grid = [grid[-r % along] for r in range(along)]
    bit = 1
    while bit < cols:
        swap = turned_over(col, bit)
        grid = [[jnp.where(swap, line[c ^ bit], line[c]) for c in range(cols)] for line in grid]
        bit *= 2
    return jnp.concatenate([block for line in grid for block in line], 0)


def queries_and_gates(lines, scale, weight, offset, q_ref, g_ref):
    inner = weight.shape[1] // 4
    queries = [contract(weight[:, :inner], normed, 0, 1) for normed in lines]
    gates = [contract(weight[:, 3 * inner :], normed, 0, 1) for normed in lines]
    for w in range(WD):
        q_ref[w] = (queries[w] * scale).astype(jnp.bfloat16)
        g_ref[w] = jax.nn.sigmoid(gates[w] + offset)


def keys_and_values(lines, weight, k_ref, v_ref):
    _, heads, _, size = k_ref.shape
    inner = heads * size
    for h in range(heads):
        at = inner + h * size
        keys = [contract(normed, weight[:, at : at + size], 1, 0) for normed in lines]
        for w in range(WD):
            k_ref[w, h] = keys[w].astype(jnp.bfloat16)
    values = [contract(weight[:, 2 * inner : 3 * inner], normed, 0, 1) for normed in lines]
    for w in range(WD):
        v_ref[w] = values[w].astype(jnp.bfloat16)


def lines_kernel(along, chips, lines_ref, gain_ref, shift_ref, weight_ref, offset_ref, q_ref, k_ref, v_ref, g_ref):
    size = k_ref.shape[-1]
    rows = lines_ref.shape[1] // (2 * chips * along)
    offset = turned(offset_ref[0:1, :])
    weight = weight_ref[0]
    lines = standardize_all([lines_ref[w].astype(jnp.float32) for w in range(WD)])
    lines = [line * gain_ref[0:1, :] + shift_ref[0:1, :] for line in lines]
    keys_and_values([line.astype(jnp.bfloat16) for line in lines], weight, k_ref, v_ref)
    near = [to_relative(line, along, chips, rows).astype(jnp.bfloat16) for line in lines]
    queries_and_gates(near, size ** (-0.5), weight, offset, q_ref, g_ref)


def projected(length, inner, heads):
    wide = (WD, inner, length)
    return (
        (wide, jnp.bfloat16),
        ((WD, heads, length, inner // heads), jnp.bfloat16),
        (wide, jnp.bfloat16),
        (wide, jnp.float32),
    )


def local_lines(pair, gain, shift, weight, offset, heads, along, chips):
    _, length, channels = pair.shape
    wide = weight.shape[2]
    shapes = projected(length, wide // 4, heads)
    whole = lambda shape: pl.BlockSpec(shape, lambda i: (0,) * len(shape))
    return pl.pallas_call(
        functools.partial(lines_kernel, along, chips),
        grid=(1,),
        out_shape=tuple(jax.ShapeDtypeStruct(shape, dtype) for shape, dtype in shapes),
        in_specs=[
            whole((WD, length, channels)), whole(gain.shape), whole(gain.shape),
            whole((1, channels, wide)), whole(gain.shape),
        ],
        out_specs=tuple(whole(shape) for shape, _ in shapes),
        compiler_params=params(8 + length // 32),
        cost_estimate=pl.CostEstimate(
            flops=2 * WD * length * channels * wide, bytes_accessed=4 * WD * length * wide, transcendentals=0
        ),
        name="lines",
    )(pair, gain, shift, weight, offset)


def unpack(source, p, pack, rows, heads, turn, into, at):
    chips, along, _, lanes = source.shape
    packed = 2 * heads * rows
    half = chips * along * rows
    slots = into.shape[0]
    for lane in range(into.shape[2 - turn] // lanes):
        first = lane * packed + (p * heads + 2 * pack) * rows
        both = [
            source[flip, shift, first : first + 2 * rows, :].astype(jnp.float32)
            for flip in range(chips)
            for shift in range(along)
        ]
        there = slice(lane * lanes, (lane + 1) * lanes)
        for i in range(2):
            slot = (2 * pack + i) % slots
            block = jnp.concatenate([part[i * rows : (i + 1) * rows] for part in both], 0)
            if turn:
                into[slot, there, at : at + half] = block.T
            else:
                into[slot, at : at + half, there] = block


def score(units):
    return [contract(key, query, 1, 0) + added for key, query, added, _ in units]


def mix(units, scores):
    tops = [jnp.max(part, 0, keepdims=True) for part in scores]
    expos = [jnp.exp(part - top) for part, top in zip(scores, tops)]
    shares = [1.0 / jnp.sum(expo, 0, keepdims=True) for expo in expos]
    weights = [(expo * share).astype(jnp.bfloat16) for expo, share in zip(expos, shares)]
    return [contract(unit[3], weight, 1, 0) for unit, weight in zip(units, weights)]


def attend_groups(groups):
    if not groups:
        return
    ready = score(groups[0][0]())
    for i, (units, put) in enumerate(groups):
        ahead = score(groups[i + 1][0]()) if i + 1 < len(groups) else None
        put(mix(units(), ready))
        ready = ahead


def head_group(heads, size, q, k, v, bias, mixed, there, near):
    def units():
        return [
            (k[w, h], q[w, h * size : (h + 1) * size, there], bias[h % bias.shape[0], :, near],
             v[w, h * size : (h + 1) * size, :])
            for h in heads
            for w in range(WD)
        ]

    def put(outs):
        for i, h in enumerate(heads):
            for w in range(WD):
                mixed[w, h * size : (h + 1) * size, near] = outs[i * WD + w]

    return units, put


def start_half(source, other, q, k, v, mixed, bias):
    _, heads, length, size = k.shape
    half = length // 2
    rows = half // (source.shape[0] * source.shape[1])
    width = min(half, CHUNK)
    if half == width:
        groups = []
        for pack in range(heads // 2):
            unpack(source, 0, pack, rows, heads, 1, bias, 0)
            groups.append(
                head_group(
                    (2 * pack, 2 * pack + 1), size, q, k, v, bias, mixed,
                    pl.ds(other * half, half), pl.ds(0, half),
                )
            )
        return groups
    for pack in range(heads // 2):
        unpack(source, 0, pack, rows, heads, 1, bias, 0)

        def step(chunk):
            near = pl.ds(pl.multiple_of(chunk * width, width), width)
            there = pl.ds(pl.multiple_of(other * half + chunk * width, width), width)
            for h in (2 * pack, 2 * pack + 1):
                attend_groups([head_group((h,), size, q, k, v, bias, mixed, there, near)])

        for_each(half // width, step, False)
    return []


def half_kernel(other, source_ref, q, k, v, mixed, bias):
    attend_groups(start_half(source_ref, other, q, k, v, mixed, bias))


def attend_half(source, other, q, k, v):
    _, heads, length, size = k.shape
    return pl.pallas_call(
        functools.partial(half_kernel, other),
        out_shape=jax.ShapeDtypeStruct((WD, heads * size, length // 2), jnp.float32),
        in_specs=[VMEM] * 4,
        out_specs=VMEM,
        scratch_shapes=[pltpu.VMEM((heads if length <= CHUNK else 2, length, length // 2), jnp.float32)],
        compiler_params=params(8 if length <= CHUNK else 40),
        cost_estimate=pl.CostEstimate(
            flops=4 * WD * heads * size * length * length,
            bytes_accessed=4 * WD * heads * length * length,
            transcendentals=WD * heads * length * length // 2,
        ),
        name="half",
    )(source, q, k, v)


def attend_kernel(
    mine_ref, other_ref, near_ref, far_ref, early_ref, late_ref, g0,
    gain_ref, shift_ref, proj_ref, gate_ref, weight_ref, offset_ref,
    out0, out1, bias, mixed, q1, k1, v1, g1,
):
    chips, along, _, _ = mine_ref.shape
    _, heads, length, size = k1.shape
    half = length // 2
    rows = half // (chips * along)
    first = pl.multiple_of(lax.rem(lax.axis_index("col"), 2) * WD * rows, WD * rows)
    offset = turned(gate_ref[1:2, :])
    blocks = []
    for source in (near_ref, far_ref):
        for flip in range(chips):
            for shift in range(along):
                both = source[flip, shift, pl.ds(first, WD * rows), :].astype(jnp.float32)
                blocks.append(both.reshape(WD, rows, -1))
    lines = standardize_all([jnp.concatenate([block[w] for block in blocks], 0) for w in range(WD)])
    lines = [line * gain_ref[1:2, :] + shift_ref[1:2, :] for line in lines]
    keys_and_values([line.astype(jnp.bfloat16) for line in lines], proj_ref[1], k1, v1)
    ordered = [to_devices(line, along, chips, rows).astype(jnp.bfloat16) for line in lines]
    queries_and_gates(ordered, size ** (-0.5), proj_ref[1], offset, q1, g1)
    groups = []
    for pack in range(heads // 2):
        unpack(mine_ref, 1, pack, rows, heads, 0, bias, 0)
        unpack(other_ref, 1, pack, rows, heads, 0, bias, half)
        pair = (2 * pack, 2 * pack + 1)
        if length == CHUNK:
            groups.append(
                head_group(pair, size, q1, k1, v1, bias, mixed, pl.ds(0, length), pl.ds(0, length))
            )
            continue

        def step(chunk):
            there = pl.ds(pl.multiple_of(chunk * CHUNK, CHUNK), CHUNK)
            for h in pair:
                attend_groups([head_group((h,), size, q1, k1, v1, bias, mixed, there, there)])

        for_each(length // CHUNK, step, False)
    attend_groups(groups)
    for w in range(WD):
        gated = (jnp.concatenate([early_ref[w], late_ref[w]], 1) * g0[w]).astype(jnp.bfloat16)
        full = contract(gated, weight_ref[0], 0, 0) + offset_ref[0:1, :]
        out0[w] = to_devices(full, along, chips, rows).astype(jnp.bfloat16)
    for w in range(WD):
        gated = (mixed[w] * g1[w]).astype(jnp.bfloat16)
        full = contract(gated, weight_ref[1], 0, 0) + offset_ref[1:2, :]
        out1[w] = full.astype(jnp.bfloat16)


def attend(mine, other, near, far, early, late, start, gain, shift, proj, gate, weight, offset):
    _, heads, length, size = start[1].shape
    inner, channels = weight.shape[1:]
    result = jax.ShapeDtypeStruct((WD, length, channels), jnp.bfloat16)
    slots = heads if length <= CHUNK else 2
    return pl.pallas_call(
        attend_kernel,
        out_shape=(result, result),
        in_specs=[VMEM] * 13,
        out_specs=(VMEM, VMEM),
        scratch_shapes=[
            pltpu.VMEM((slots, length, length), jnp.float32),
            pltpu.VMEM((WD, inner, length), jnp.float32),
        ]
        + [pltpu.VMEM(shape, dtype) for shape, dtype in projected(length, inner, heads)],
        compiler_params=params(16 if length <= CHUNK else 60),
        name="attend",
    )(mine, other, near, far, early, late, start[3], gain, shift, proj, gate, weight, offset)


def body(pair, residue_mask, ln_gain, ln_shift, w_proj, w_bias, gate_bias, w_out, out_bias):
    rows, length, channels = pair.shape
    heads = w_bias.shape[2]
    along, cols = lax.axis_size("row"), lax.axis_size("col")
    chips = cols // 2

    def by_row(block, shift):
        return lax.ppermute(block, "row", [(i, (i + shift) % along) for i in range(along)])

    def by_col(block, flip):
        return lax.ppermute(block, "col", [(i, i ^ flip) for i in range(cols)])

    block, owned = local_bias(
        pair, residue_mask[None, :], ln_gain, ln_shift, jnp.transpose(w_bias, (0, 2, 1)), along, chips
    )
    line = jnp.stack([block] + [by_row(block, shift) for shift in range(1, along)])
    start = local_lines(pair, ln_gain, ln_shift, w_proj, gate_bias, heads, along, chips)
    owned, _ = lax.optimization_barrier((owned, line))
    owned = jnp.stack([owned[0]] + [by_row(owned[shift], shift) for shift in range(1, along)], 1)
    mine = jnp.stack([line] + [by_col(line, 2 * flip) for flip in range(1, chips)])
    mine, _ = lax.optimization_barrier((mine, start))
    other = by_col(mine, 1)
    early = attend_half(mine, 0, *start[:3])
    owned, early = lax.optimization_barrier((owned, early))
    near = jnp.stack([owned[0]] + [by_col(owned[flip], 2 * flip) for flip in range(1, chips)])
    late = attend_half(other, 1, *start[:3])
    far = by_col(near, 1)
    return attend(
        mine, other, near, far, early, late, start, ln_gain, ln_shift, w_proj, gate_bias, w_out, out_bias
    )


def solution(mesh):
    return jax.shard_map(
        body,
        mesh=mesh,
        in_specs=(P(("row", "col"), None, None), P(), P(), P(), P(), P(), P(), P(), P()),
        out_specs=(P(("row", "col"), None, None), P(("row", "col"), None, None)),
        check_vma=False,
    )
```

```python
import functools

import jax
import jax.numpy as jnp
from jax import lax
from jax.experimental import pallas as pl
from jax.experimental.pallas import tpu as pltpu
from jax.sharding import PartitionSpec as P

WD = 2
EPS = 1e-05
MASKED = -1000000000.0
CHUNK = 256
VMEM = pl.BlockSpec(memory_space=pltpu.VMEM)
HBM = pl.BlockSpec(memory_space=pltpu.HBM)


def params(megabytes):
    return pltpu.CompilerParams(vmem_limit_bytes=megabytes * 1024 * 1024)


def for_each(count, step, unrolled):
    if unrolled:
        for index in range(count):
            step(index)
    else:
        lax.fori_loop(0, count, lambda index, carry: (step(index), carry)[1], 0)


def standardize_all(lines):
    centers = [jnp.mean(wide, -1, keepdims=True) for wide in lines]
    aways = [wide - center for wide, center in zip(lines, centers)]
    spreads = [jnp.mean(jnp.square(away), -1, keepdims=True) for away in aways]
    return [away * lax.rsqrt(spread + EPS) for away, spread in zip(aways, spreads)]


def contract(left, right, left_dim, right_dim):
    return lax.dot_general(
        left, right, (((left_dim,), (right_dim,)), ((), ())), preferred_element_type=jnp.float32
    )


def flipped(index, flip):
    bit = 1
    while bit <= flip:
        if flip & bit:
            index = index + bit - 2 * bit * lax.rem(lax.div(index, bit), 2)
        bit *= 2
    return index


def bias_kernel(along, chips, pair_hbm, live_hbm, gain_hbm, shift_hbm, weight_hbm, *rest):
    outs = rest[:along]
    pair, live_row, live_each, gain, shift, weight, blocks, rows_out, wide, picked, sems, pair_sems = rest[along:]
    rows, length, channels = pair.shape
    heads = weight.shape[1]
    lanes = outs[0].shape[1]
    small = [
        pltpu.make_async_copy(source, target, sems.at[i])
        for i, (source, target) in enumerate(
            ((live_hbm, live_row), (live_hbm, live_each), (gain_hbm, gain), (shift_hbm, shift), (weight_hbm, weight))
        )
    ]
    large = [pltpu.make_async_copy(pair_hbm.at[a], pair.at[a], pair_sems.at[a]) for a in range(rows)]
    large[0].start()
    for copy in small:
        copy.start()
    for copy in large[1:]:
        copy.start()
    device = lax.axis_index("row") * lax.axis_size("col") + lax.axis_index("col")
    for copy in small + large:
        copy.wait()
    blocks[...] = jnp.zeros_like(blocks)
    for p in range(2):
        at = slice(p * heads, (p + 1) * heads)
        blocks[at, p * channels : (p + 1) * channels] = weight[p].astype(jnp.float32)
    paired = blocks[: 2 * heads].astype(jnp.bfloat16)
    live = jnp.broadcast_to(live_row[...], (2 * heads, length))
    first = lax.broadcasted_iota(jnp.int32, live.shape, 0) < heads
    lines = [pair[a].astype(jnp.float32) for a in range(rows)]
    for a, x in enumerate(lines):
        wide[a] = x
    lines = standardize_all(lines)
    normed = [
        jnp.concatenate(
            [(z * gain[p : p + 1, :] + shift[p : p + 1, :]).astype(jnp.bfloat16) for p in range(2)], 1
        )
        for z in lines
    ]
    biases = [contract(paired, line, 1, 1) for line in normed]
    devices = length // rows
    for a in range(rows):
        for w in range(WD):
            column = wide[a, pl.ds(w, devices, stride=rows), :]
            picked[pl.ds(w * rows + a, devices, stride=WD * rows), :] = column
    for a, bias in enumerate(biases):
        kept = jnp.where(first, live, live_each[0, device * rows + a])
        bias = jnp.where(kept > 0, bias, MASKED)
        for lane in range(length // lanes):
            part = bias[:, lane * lanes : (lane + 1) * lanes]
            rows_out[pl.ds(2 * lane * heads * rows + a, 2 * heads, stride=rows), :] = part
    chip = lax.div(lax.axis_index("col"), 2)
    both = 2 * WD * rows
    packed = rows_out.shape[0]
    sent = rows_out[...].astype(jnp.bfloat16)
    for shift_by, out in enumerate(outs):
        out[:packed] = sent
        row = flipped(lax.axis_index("row"), shift_by)
        for flip in range(chips):
            at = pl.multiple_of((row * chips + flipped(chip, flip)) * both, both)
            out[packed + flip * both : packed + (flip + 1) * both] = picked[pl.ds(at, both), :].astype(jnp.bfloat16)


def local_bias(pair, live, gain, shift, weight, along, chips):
    rows, length, channels = pair.shape
    heads = weight.shape[1]
    packed = 2 * heads * rows * (length // channels)
    sent = jax.ShapeDtypeStruct((packed + chips * 2 * WD * rows, channels), jnp.bfloat16)
    return pl.pallas_call(
        functools.partial(bias_kernel, along, chips),
        out_shape=(sent,) * along,
        in_specs=[HBM] * 5,
        out_specs=(VMEM,) * along,
        scratch_shapes=[
            pltpu.VMEM(pair.shape, pair.dtype),
            pltpu.VMEM(live.shape, live.dtype),
            pltpu.SMEM(live.shape, live.dtype),
            pltpu.VMEM(gain.shape, gain.dtype),
            pltpu.VMEM(shift.shape, shift.dtype),
            pltpu.VMEM(weight.shape, weight.dtype),
            pltpu.VMEM((4 * heads, 2 * channels), jnp.float32),
            pltpu.VMEM((packed, channels), jnp.float32),
            pltpu.VMEM(pair.shape, jnp.float32),
            pltpu.VMEM((length * WD, channels), jnp.float32),
            pltpu.SemaphoreType.DMA((5,)),
            pltpu.SemaphoreType.DMA((rows,)),
        ],
        compiler_params=params(60),
        name="bias",
    )(pair, live, gain, shift, weight)


def turned(row):
    return jnp.broadcast_to(row, (row.shape[1], row.shape[1])).T[:, :1]


def turned_over(index, bit):
    return lax.rem(lax.div(index, bit), 2) == 1


def exchanged(grid, row, col):
    along, cols = len(grid), len(grid[0])
    bit = 1
    while bit < cols:
        swap = turned_over(col, bit)
        grid = [[jnp.where(swap, line[c ^ bit], line[c]) for c in range(cols)] for line in grid]
        bit *= 2
    bit = 1
    while bit < along:
        swap = turned_over(row, bit)
        grid = [[jnp.where(swap, grid[r ^ bit][c], grid[r][c]) for c in range(cols)] for r in range(along)]
        bit *= 2
    return grid


def to_relative(x, along, chips, rows):
    cols = 2 * chips
    grid = [[x[(r * cols + c) * rows : (r * cols + c + 1) * rows] for c in range(cols)] for r in range(along)]
    grid = exchanged(grid, lax.axis_index("row"), lax.axis_index("col"))
    return jnp.concatenate(
        [grid[s][2 * flip + other] for other in range(2) for flip in range(chips) for s in range(along)], 0
    )


def to_devices(x, along, chips, rows):
    at = lambda c, s: (((c % 2) * chips + c // 2) * along + s) * rows
    grid = [[x[at(c, s) : at(c, s) + rows] for c in range(2 * chips)] for s in range(along)]
    grid = exchanged(grid, lax.axis_index("row"), lax.axis_index("col"))
    return jnp.concatenate([block for line in grid for block in line], 0)


def queries_and_gates(lines, scale, weight, offset, q_ref, g_ref):
    inner = weight.shape[1] // 4
    queries = [contract(weight[:, :inner], normed, 0, 1) for normed in lines]
    gates = [contract(weight[:, 3 * inner :], normed, 0, 1) for normed in lines]
    for w in range(WD):
        q_ref[w] = (queries[w] * scale).astype(jnp.bfloat16)
        g_ref[w] = jax.nn.sigmoid(gates[w] + offset)


def keys_and_values(lines, weight, k_ref, v_ref):
    _, heads, _, size = k_ref.shape
    inner = heads * size
    for h in range(heads):
        at = inner + h * size
        keys = [contract(normed, weight[:, at : at + size], 1, 0) for normed in lines]
        for w in range(WD):
            k_ref[w, h] = keys[w].astype(jnp.bfloat16)
    values = [contract(weight[:, 2 * inner : 3 * inner], normed, 0, 1) for normed in lines]
    for w in range(WD):
        v_ref[w] = values[w].astype(jnp.bfloat16)


def lines_kernel(along, chips, lines_ref, gain_ref, shift_ref, weight_ref, offset_ref, q_ref, k_ref, v_ref, g_ref):
    size = k_ref.shape[-1]
    rows = lines_ref.shape[1] // (2 * chips * along)
    offset = turned(offset_ref[0:1, :])
    weight = weight_ref[0]
    lines = standardize_all([lines_ref[w].astype(jnp.float32) for w in range(WD)])
    lines = [line * gain_ref[0:1, :] + shift_ref[0:1, :] for line in lines]
    keys_and_values([line.astype(jnp.bfloat16) for line in lines], weight, k_ref, v_ref)
    near = [to_relative(line, along, chips, rows).astype(jnp.bfloat16) for line in lines]
    queries_and_gates(near, size ** (-0.5), weight, offset, q_ref, g_ref)


def projected(length, inner, heads):
    wide = (WD, inner, length)
    return (
        (wide, jnp.bfloat16),
        ((WD, heads, length, inner // heads), jnp.bfloat16),
        (wide, jnp.bfloat16),
        (wide, jnp.float32),
    )


def local_lines(pair, gain, shift, weight, offset, heads, along, chips):
    _, length, channels = pair.shape
    wide = weight.shape[2]
    shapes = projected(length, wide // 4, heads)
    whole = lambda shape: pl.BlockSpec(shape, lambda i: (0,) * len(shape))
    return pl.pallas_call(
        functools.partial(lines_kernel, along, chips),
        grid=(1,),
        out_shape=tuple(jax.ShapeDtypeStruct(shape, dtype) for shape, dtype in shapes),
        in_specs=[
            whole((WD, length, channels)), whole(gain.shape), whole(gain.shape),
            whole((1, channels, wide)), whole(gain.shape),
        ],
        out_specs=tuple(whole(shape) for shape, _ in shapes),
        compiler_params=params(8 + length // 32),
        cost_estimate=pl.CostEstimate(
            flops=2 * WD * length * channels * wide, bytes_accessed=4 * WD * length * wide, transcendentals=0
        ),
        name="lines",
    )(pair, gain, shift, weight, offset)


def by_flip(ref):
    return [ref.at[i] for i in range(ref.shape[0])]


def unpack(source, p, pack, rows, heads, turn, into, at):
    chips, (along, _, lanes) = len(source), source[0].shape
    packed = 2 * heads * rows
    half = chips * along * rows
    slots = into.shape[0]
    for lane in range(into.shape[2 - turn] // lanes):
        first = lane * packed + (p * heads + 2 * pack) * rows
        both = [
            source[flip][shift, first : first + 2 * rows, :].astype(jnp.float32)
            for flip in range(chips)
            for shift in range(along)
        ]
        there = slice(lane * lanes, (lane + 1) * lanes)
        for i in range(2):
            slot = (2 * pack + i) % slots
            block = jnp.concatenate([part[i * rows : (i + 1) * rows] for part in both], 0)
            if turn:
                into[slot, there, at : at + half] = block.T
            else:
                into[slot, at : at + half, there] = block


def score(units):
    return [contract(key, query, 1, 0) + added for key, query, added, _ in units]


def mix(units, scores):
    tops = [jnp.max(part, 0, keepdims=True) for part in scores]
    expos = [jnp.exp(part - top) for part, top in zip(scores, tops)]
    shares = [1.0 / jnp.sum(expo, 0, keepdims=True) for expo in expos]
    weights = [(expo * share).astype(jnp.bfloat16) for expo, share in zip(expos, shares)]
    return [contract(unit[3], weight, 1, 0) for unit, weight in zip(units, weights)]


def attend_groups(groups):
    if not groups:
        return
    ready = score(groups[0][0]())
    for i, (units, put) in enumerate(groups):
        ahead = score(groups[i + 1][0]()) if i + 1 < len(groups) else None
        put(mix(units(), ready))
        ready = ahead


def head_group(heads, size, q, k, v, bias, mixed, there, near, own_bias=None):
    def added(h):
        part = bias[h % bias.shape[0], :, near]
        return part if own_bias is None else jnp.concatenate([own_bias[h, :, near], part], 0)

    def units():
        return [
            (k[w, h], q[w, h * size : (h + 1) * size, there], added(h), v[w, h * size : (h + 1) * size, :])
            for h in heads
            for w in range(WD)
        ]

    def put(outs):
        for i, h in enumerate(heads):
            for w in range(WD):
                mixed[w, h * size : (h + 1) * size, near] = outs[i * WD + w]

    return units, put


def start_half(source, other, q, k, v, mixed, bias):
    _, heads, length, size = k.shape
    half = length // 2
    rows = half // (len(source) * source[0].shape[0])
    width = min(half, CHUNK)
    if half == width:
        groups = []
        for pack in range(heads // 2):
            unpack(source, 0, pack, rows, heads, 1, bias, 0)
            groups.append(
                head_group(
                    (2 * pack, 2 * pack + 1), size, q, k, v, bias, mixed,
                    pl.ds(other * half, half), pl.ds(0, half),
                )
            )
        return groups
    for pack in range(heads // 2):
        unpack(source, 0, pack, rows, heads, 1, bias, 0)

        def step(chunk):
            near = pl.ds(pl.multiple_of(chunk * width, width), width)
            there = pl.ds(pl.multiple_of(other * half + chunk * width, width), width)
            for h in (2 * pack, 2 * pack + 1):
                attend_groups([head_group((h,), size, q, k, v, bias, mixed, there, near)])

        for_each(half // width, step, False)
    return []


def normed_columns(pieces, first, gain, shift, rows):
    along = pieces[0].shape[0]
    blocks = [
        piece[i, pl.ds(first, WD * rows), :].astype(jnp.float32).reshape(WD, rows, -1)
        for piece in pieces
        for i in range(along)
    ]
    lines = standardize_all([jnp.concatenate([block[w] for block in blocks], 0) for w in range(WD)])
    return [line * gain + shift for line in lines]


def first_column(packed, rows):
    at = packed + lax.rem(lax.axis_index("col"), 2) * WD * rows
    return pl.multiple_of(at, WD * rows)


def early_kernel(
    mine_ref, q, k, v, gain_ref, shift_ref, proj_ref, mixed, own_bias, own_lines, own_k, own_v, bias
):
    mine = by_flip(mine_ref)
    _, heads, half, _ = own_k.shape
    length = k.shape[2]
    rows = half // (len(mine) * mine[0].shape[0])
    packed = 2 * heads * rows * (length // mine_ref.shape[3])
    lines = normed_columns(mine, first_column(packed, rows), gain_ref[1:2, :], shift_ref[1:2, :], rows)
    groups = start_half(mine, 0, q, k, v, mixed, bias)
    for w in range(WD):
        own_lines[w] = lines[w]
    keys_and_values([line.astype(jnp.bfloat16) for line in lines], proj_ref[1], own_k, own_v)
    attend_groups(groups)
    for pack in range(heads // 2):
        unpack(mine, 1, pack, rows, heads, 0, own_bias, 0)


def attend_early(mine, q, k, v, gain, shift, proj):
    _, heads, length, size = k.shape
    inner, half, channels = heads * size, length // 2, proj.shape[1]
    return pl.pallas_call(
        early_kernel,
        out_shape=(
            jax.ShapeDtypeStruct((WD, inner, half), jnp.float32),
            jax.ShapeDtypeStruct((heads, half, length), jnp.float32),
            jax.ShapeDtypeStruct((WD, half, channels), jnp.float32),
            jax.ShapeDtypeStruct((WD, heads, half, size), jnp.bfloat16),
            jax.ShapeDtypeStruct((WD, inner, half), jnp.bfloat16),
        ),
        in_specs=[VMEM] * 7,
        out_specs=(VMEM,) * 5,
        scratch_shapes=[pltpu.VMEM((heads if length <= CHUNK else 2, length, half), jnp.float32)],
        compiler_params=params(8 if length <= CHUNK else 40),
        cost_estimate=pl.CostEstimate(
            flops=4 * WD * heads * size * length * length,
            bytes_accessed=4 * WD * heads * length * length,
            transcendentals=WD * heads * length * length // 2,
        ),
        name="early",
    )(mine, q, k, v, gain, shift, proj)


def attend_kernel(
    other_ref, early_ref, own_bias, own_lines, own_k, own_v, q0, k0, v0, g0,
    gain_ref, shift_ref, proj_ref, gate_ref, weight_ref, offset_ref,
    out0, out1, turned_bias, bias, late, mixed, q1, k1, v1, g1,
):
    others = by_flip(other_ref)
    chips, (along, _, lanes) = len(others), others[0].shape
    _, heads, length, size = k0.shape
    half = length // 2
    rows = half // (chips * along)
    packed = 2 * heads * rows * (length // lanes)
    offset = turned(gate_ref[1:2, :])
    far = normed_columns(others, first_column(packed, rows), gain_ref[1:2, :], shift_ref[1:2, :], rows)
    keys_and_values([line.astype(jnp.bfloat16) for line in far], proj_ref[1], k1.at[:, :, half:], v1.at[:, :, half:])
    for w in range(WD):
        k1[w, :, :half] = own_k[w]
        v1[w, :, :half] = own_v[w]
    ordered = [
        to_devices(jnp.concatenate([own_lines[w], far[w]], 0), along, chips, rows).astype(jnp.bfloat16)
        for w in range(WD)
    ]
    queries_and_gates(ordered, size ** (-0.5), proj_ref[1], offset, q1, g1)
    groups = start_half(others, 1, q0, k0, v0, late, turned_bias)
    for pack in range(heads // 2):
        unpack(others, 1, pack, rows, heads, 0, bias, 0)
        pair = (2 * pack, 2 * pack + 1)
        if length == CHUNK:
            whole = pl.ds(0, length)
            groups.append(head_group(pair, size, q1, k1, v1, bias, mixed, whole, whole, own_bias))
            continue

        def step(chunk):
            there = pl.ds(pl.multiple_of(chunk * CHUNK, CHUNK), CHUNK)
            for h in pair:
                attend_groups([head_group((h,), size, q1, k1, v1, bias, mixed, there, there, own_bias)])

        for_each(length // CHUNK, step, False)
    attend_groups(groups)
    for w in range(WD):
        gated = (jnp.concatenate([early_ref[w], late[w]], 1) * g0[w]).astype(jnp.bfloat16)
        full = contract(gated, weight_ref[0], 0, 0) + offset_ref[0:1, :]
        out0[w] = to_devices(full, along, chips, rows).astype(jnp.bfloat16)
    for w in range(WD):
        gated = (mixed[w] * g1[w]).astype(jnp.bfloat16)
        full = contract(gated, weight_ref[1], 0, 0) + offset_ref[1:2, :]
        out1[w] = full.astype(jnp.bfloat16)


def attend(other, early, start, gain, shift, proj, gate, weight, offset):
    _, heads, length, size = start[1].shape
    inner, channels = weight.shape[1:]
    result = jax.ShapeDtypeStruct((WD, length, channels), jnp.bfloat16)
    slots = heads if length <= CHUNK else 2
    return pl.pallas_call(
        attend_kernel,
        out_shape=(result, result),
        in_specs=[VMEM] * 16,
        out_specs=(VMEM, VMEM),
        scratch_shapes=[
            pltpu.VMEM((slots, length, length // 2), jnp.float32),
            pltpu.VMEM((slots, length // 2, length), jnp.float32),
            pltpu.VMEM((WD, inner, length // 2), jnp.float32),
            pltpu.VMEM((WD, inner, length), jnp.float32),
        ]
        + [pltpu.VMEM(shape, dtype) for shape, dtype in projected(length, inner, heads)],
        compiler_params=params(16 if length <= CHUNK else 60),
        name="attend",
    )(other, *early, *start, gain, shift, proj, gate, weight, offset)


def body(pair, residue_mask, ln_gain, ln_shift, w_proj, w_bias, gate_bias, w_out, out_bias):
    rows, length, channels = pair.shape
    heads = w_bias.shape[2]
    along, cols = lax.axis_size("row"), lax.axis_size("col")
    chips = cols // 2

    def by_row(block, shift):
        return lax.ppermute(block, "row", [(i, i ^ shift) for i in range(along)])

    def by_col(block, flip):
        return lax.ppermute(block, "col", [(i, i ^ flip) for i in range(cols)])

    sent = local_bias(
        pair, residue_mask[None, :], ln_gain, ln_shift, jnp.transpose(w_bias, (0, 2, 1)), along, chips
    )
    line = jnp.stack([sent[0]] + [by_row(sent[shift], shift) for shift in range(1, along)])
    start = local_lines(pair, ln_gain, ln_shift, w_proj, gate_bias, heads, along, chips)
    line, _ = lax.optimization_barrier((line, start))
    packed = 2 * heads * rows * (length // channels)
    both = 2 * WD * rows

    def owned_by(flip):
        at = packed + flip * both
        return jnp.concatenate([line[:, :packed], line[:, at : at + both]], 1)

    mine = jnp.stack([owned_by(0)] + [by_col(owned_by(flip), 2 * flip) for flip in range(1, chips)])
    other = by_col(mine, 1)
    early = attend_early(mine, *start[:3], ln_gain, ln_shift, w_proj)
    return attend(other, early, start, ln_gain, ln_shift, w_proj, gate_bias, w_out, out_bias)


def solution(mesh):
    return jax.shard_map(
        body,
        mesh=mesh,
        in_specs=(P(("row", "col"), None, None), P(), P(), P(), P(), P(), P(), P(), P()),
        out_specs=(P(("row", "col"), None, None), P(("row", "col"), None, None)),
        check_vma=False,
    )
```

```python
import functools

import jax
import jax.numpy as jnp
from jax import lax
from jax.experimental import pallas as pl
from jax.experimental.pallas import tpu as pltpu
from jax.sharding import PartitionSpec as P

WD = 2
EPS = 1e-05
MASKED = -1000000000.0
CHUNK = 256
VMEM = pl.BlockSpec(memory_space=pltpu.VMEM)
HBM = pl.BlockSpec(memory_space=pltpu.HBM)


def params(megabytes):
    return pltpu.CompilerParams(vmem_limit_bytes=megabytes * 1024 * 1024)


def for_each(count, step, unrolled):
    if unrolled:
        for index in range(count):
            step(index)
    else:
        lax.fori_loop(0, count, lambda index, carry: (step(index), carry)[1], 0)


def standardize_all(lines):
    centers = [jnp.mean(wide, -1, keepdims=True) for wide in lines]
    aways = [wide - center for wide, center in zip(lines, centers)]
    spreads = [jnp.mean(jnp.square(away), -1, keepdims=True) for away in aways]
    return [away * lax.rsqrt(spread + EPS) for away, spread in zip(aways, spreads)]


def contract(left, right, left_dim, right_dim):
    return lax.dot_general(
        left, right, (((left_dim,), (right_dim,)), ((), ())), preferred_element_type=jnp.float32
    )


def flipped(index, flip):
    bit = 1
    while bit <= flip:
        if flip & bit:
            index = index + bit - 2 * bit * lax.rem(lax.div(index, bit), 2)
        bit *= 2
    return index


def bias_kernel(along, chips, pair_hbm, live_hbm, gain_hbm, shift_hbm, weight_hbm, *rest):
    outs = rest[:along]
    pair, live_row, live_each, gain, shift, weight, blocks, rows_out, wide, picked, sems, pair_sems = rest[along:]
    rows, length, channels = pair.shape
    heads = weight.shape[1]
    lanes = outs[0].shape[1]
    small = [
        pltpu.make_async_copy(source, target, sems.at[i])
        for i, (source, target) in enumerate(
            ((live_hbm, live_row), (live_hbm, live_each), (gain_hbm, gain), (shift_hbm, shift), (weight_hbm, weight))
        )
    ]
    large = [pltpu.make_async_copy(pair_hbm.at[a], pair.at[a], pair_sems.at[a]) for a in range(rows)]
    large[0].start()
    for copy in small:
        copy.start()
    for copy in large[1:]:
        copy.start()
    device = lax.axis_index("row") * lax.axis_size("col") + lax.axis_index("col")
    for copy in small + large:
        copy.wait()
    blocks[...] = jnp.zeros_like(blocks)
    for p in range(2):
        at = slice(p * heads, (p + 1) * heads)
        blocks[at, p * channels : (p + 1) * channels] = weight[p].astype(jnp.float32)
    paired = blocks[: 2 * heads].astype(jnp.bfloat16)
    live = jnp.broadcast_to(live_row[...], (2 * heads, length))
    first = lax.broadcasted_iota(jnp.int32, live.shape, 0) < heads
    lines = [pair[a].astype(jnp.float32) for a in range(rows)]
    for a, x in enumerate(lines):
        wide[a] = x
    lines = standardize_all(lines)
    normed = [
        jnp.concatenate(
            [(z * gain[p : p + 1, :] + shift[p : p + 1, :]).astype(jnp.bfloat16) for p in range(2)], 1
        )
        for z in lines
    ]
    biases = [contract(paired, line, 1, 1) for line in normed]
    devices = length // rows
    for a in range(rows):
        for w in range(WD):
            column = wide[a, pl.ds(w, devices, stride=rows), :]
            picked[pl.ds(w * rows + a, devices, stride=WD * rows), :] = column
    for a, bias in enumerate(biases):
        kept = jnp.where(first, live, live_each[0, device * rows + a])
        bias = jnp.where(kept > 0, bias, MASKED)
        for lane in range(length // lanes):
            part = bias[:, lane * lanes : (lane + 1) * lanes]
            rows_out[pl.ds(2 * lane * heads * rows + a, 2 * heads, stride=rows), :] = part
    chip = lax.div(lax.axis_index("col"), 2)
    both = 2 * WD * rows
    packed = rows_out.shape[0]
    sent = rows_out[...].astype(jnp.bfloat16)
    for shift_by, out in enumerate(outs):
        out[:packed] = sent
        row = flipped(lax.axis_index("row"), shift_by)
        for flip in range(chips):
            at = pl.multiple_of((row * chips + flipped(chip, flip)) * both, both)
            out[packed + flip * both : packed + (flip + 1) * both] = picked[pl.ds(at, both), :].astype(jnp.bfloat16)


def local_bias(pair, live, gain, shift, weight, along, chips):
    rows, length, channels = pair.shape
    heads = weight.shape[1]
    packed = 2 * heads * rows * (length // channels)
    sent = jax.ShapeDtypeStruct((packed + chips * 2 * WD * rows, channels), jnp.bfloat16)
    return pl.pallas_call(
        functools.partial(bias_kernel, along, chips),
        out_shape=(sent,) * along,
        in_specs=[HBM] * 5,
        out_specs=(VMEM,) * along,
        scratch_shapes=[
            pltpu.VMEM(pair.shape, pair.dtype),
            pltpu.VMEM(live.shape, live.dtype),
            pltpu.SMEM(live.shape, live.dtype),
            pltpu.VMEM(gain.shape, gain.dtype),
            pltpu.VMEM(shift.shape, shift.dtype),
            pltpu.VMEM(weight.shape, weight.dtype),
            pltpu.VMEM((4 * heads, 2 * channels), jnp.float32),
            pltpu.VMEM((packed, channels), jnp.float32),
            pltpu.VMEM(pair.shape, jnp.float32),
            pltpu.VMEM((length * WD, channels), jnp.float32),
            pltpu.SemaphoreType.DMA((5,)),
            pltpu.SemaphoreType.DMA((rows,)),
        ],
        compiler_params=params(60),
        name="bias",
    )(pair, live, gain, shift, weight)


def turned(row):
    return jnp.broadcast_to(row, (row.shape[1], row.shape[1])).T[:, :1]


def turned_over(index, bit):
    return lax.rem(lax.div(index, bit), 2) == 1


def exchanged(grid, row, col):
    along, cols = len(grid), len(grid[0])
    bit = 1
    while bit < cols:
        swap = turned_over(col, bit)
        grid = [[jnp.where(swap, line[c ^ bit], line[c]) for c in range(cols)] for line in grid]
        bit *= 2
    bit = 1
    while bit < along:
        swap = turned_over(row, bit)
        grid = [[jnp.where(swap, grid[r ^ bit][c], grid[r][c]) for c in range(cols)] for r in range(along)]
        bit *= 2
    return grid


def to_relative(x, along, chips, rows):
    cols = 2 * chips
    grid = [[x[(r * cols + c) * rows : (r * cols + c + 1) * rows] for c in range(cols)] for r in range(along)]
    grid = exchanged(grid, lax.axis_index("row"), lax.axis_index("col"))
    return jnp.concatenate(
        [grid[s][2 * flip + other] for other in range(2) for flip in range(chips) for s in reversed(range(along))], 0
    )


def to_devices(x, along, chips, rows):
    at = lambda c, s: (((c % 2) * chips + c // 2) * along + along - 1 - s) * rows
    grid = [[x[at(c, s) : at(c, s) + rows] for c in range(2 * chips)] for s in range(along)]
    grid = exchanged(grid, lax.axis_index("row"), lax.axis_index("col"))
    return jnp.concatenate([block for line in grid for block in line], 0)


def queries_and_gates(lines, scale, weight, offset, q_ref, g_ref):
    inner = weight.shape[1] // 4
    queries = [contract(weight[:, :inner], normed, 0, 1) for normed in lines]
    gates = [contract(weight[:, 3 * inner :], normed, 0, 1) for normed in lines]
    for w in range(WD):
        q_ref[w] = (queries[w] * scale).astype(jnp.bfloat16)
        g_ref[w] = jax.nn.sigmoid(gates[w] + offset)


def keys_and_values(lines, weight, k_ref, v_ref):
    _, heads, _, size = k_ref.shape
    inner = heads * size
    for h in range(heads):
        at = inner + h * size
        keys = [contract(normed, weight[:, at : at + size], 1, 0) for normed in lines]
        for w in range(WD):
            k_ref[w, h] = keys[w].astype(jnp.bfloat16)
    values = [contract(weight[:, 2 * inner : 3 * inner], normed, 0, 1) for normed in lines]
    for w in range(WD):
        v_ref[w] = values[w].astype(jnp.bfloat16)


def lines_kernel(along, chips, lines_ref, gain_ref, shift_ref, weight_ref, offset_ref, q_ref, k_ref, v_ref, g_ref):
    size = k_ref.shape[-1]
    rows = lines_ref.shape[1] // (2 * chips * along)
    offset = turned(offset_ref[0:1, :])
    weight = weight_ref[0]
    lines = standardize_all([lines_ref[w].astype(jnp.float32) for w in range(WD)])
    lines = [line * gain_ref[0:1, :] + shift_ref[0:1, :] for line in lines]
    keys_and_values([line.astype(jnp.bfloat16) for line in lines], weight, k_ref, v_ref)
    near = [to_relative(line, along, chips, rows).astype(jnp.bfloat16) for line in lines]
    queries_and_gates(near, size ** (-0.5), weight, offset, q_ref, g_ref)


def projected(length, inner, heads):
    wide = (WD, inner, length)
    return (
        (wide, jnp.bfloat16),
        ((WD, heads, length, inner // heads), jnp.bfloat16),
        (wide, jnp.bfloat16),
        (wide, jnp.float32),
    )


def local_lines(pair, gain, shift, weight, offset, heads, along, chips):
    _, length, channels = pair.shape
    wide = weight.shape[2]
    shapes = projected(length, wide // 4, heads)
    whole = lambda shape: pl.BlockSpec(shape, lambda i: (0,) * len(shape))
    return pl.pallas_call(
        functools.partial(lines_kernel, along, chips),
        grid=(1,),
        out_shape=tuple(jax.ShapeDtypeStruct(shape, dtype) for shape, dtype in shapes),
        in_specs=[
            whole((WD, length, channels)), whole(gain.shape), whole(gain.shape),
            whole((1, channels, wide)), whole(gain.shape),
        ],
        out_specs=tuple(whole(shape) for shape, _ in shapes),
        compiler_params=params(8 + length // 32),
        cost_estimate=pl.CostEstimate(
            flops=2 * WD * length * channels * wide, bytes_accessed=4 * WD * length * wide, transcendentals=0
        ),
        name="lines",
    )(pair, gain, shift, weight, offset)


def unpack(source, p, pack, rows, heads, turn, into, at):
    chips, along, _, lanes = source.shape
    packed = 2 * heads * rows
    half = chips * along * rows
    slots = into.shape[0]
    for lane in range(into.shape[2 - turn] // lanes):
        first = lane * packed + (p * heads + 2 * pack) * rows
        both = [
            source[flip, shift, first : first + 2 * rows, :].astype(jnp.float32)
            for flip in range(chips)
            for shift in range(along)
        ]
        there = slice(lane * lanes, (lane + 1) * lanes)
        for i in range(2):
            slot = (2 * pack + i) % slots
            block = jnp.concatenate([part[i * rows : (i + 1) * rows] for part in both], 0)
            if turn:
                into[slot, there, at : at + half] = block.T
            else:
                into[slot, at : at + half, there] = block


def score(units):
    return [contract(key, query, 1, 0) + added for key, query, added, _ in units]


def mix(units, scores):
    tops = [jnp.max(part, 0, keepdims=True) for part in scores]
    expos = [jnp.exp(part - top) for part, top in zip(scores, tops)]
    shares = [1.0 / jnp.sum(expo, 0, keepdims=True) for expo in expos]
    weights = [(expo * share).astype(jnp.bfloat16) for expo, share in zip(expos, shares)]
    return [contract(unit[3], weight, 1, 0) for unit, weight in zip(units, weights)]


def attend_groups(groups):
    if not groups:
        return
    ready = score(groups[0][0]())
    for i, (units, put) in enumerate(groups):
        ahead = score(groups[i + 1][0]()) if i + 1 < len(groups) else None
        put(mix(units(), ready))
        ready = ahead


def head_group(heads, size, q, k, v, bias, mixed, there, near):
    def units():
        return [
            (k[w, h], q[w, h * size : (h + 1) * size, there], bias[h % bias.shape[0], :, near],
             v[w, h * size : (h + 1) * size, :])
            for h in heads
            for w in range(WD)
        ]

    def put(outs):
        for i, h in enumerate(heads):
            for w in range(WD):
                mixed[w, h * size : (h + 1) * size, near] = outs[i * WD + w]

    return units, put


def start_half(source, other, q, k, v, mixed, bias):
    _, heads, length, size = k.shape
    half = length // 2
    rows = half // (source.shape[0] * source.shape[1])
    width = min(half, CHUNK)
    if half == width:
        groups = []
        for pack in range(heads // 2):
            unpack(source, 0, pack, rows, heads, 1, bias, 0)
            groups.append(
                head_group(
                    (2 * pack, 2 * pack + 1), size, q, k, v, bias, mixed,
                    pl.ds(other * half, half), pl.ds(0, half),
                )
            )
        return groups
    for pack in range(heads // 2):
        unpack(source, 0, pack, rows, heads, 1, bias, 0)

        def step(chunk):
            near = pl.ds(pl.multiple_of(chunk * width, width), width)
            there = pl.ds(pl.multiple_of(other * half + chunk * width, width), width)
            for h in (2 * pack, 2 * pack + 1):
                attend_groups([head_group((h,), size, q, k, v, bias, mixed, there, near)])

        for_each(half // width, step, False)
    return []


def early_kernel(mine_ref, q, k, v, mixed, bias):
    attend_groups(start_half(mine_ref, 0, q, k, v, mixed, bias))


def attend_early(mine, q, k, v):
    _, heads, length, size = k.shape
    return pl.pallas_call(
        early_kernel,
        out_shape=jax.ShapeDtypeStruct((WD, heads * size, length // 2), jnp.float32),
        in_specs=[VMEM] * 4,
        out_specs=VMEM,
        scratch_shapes=[pltpu.VMEM((heads if length <= CHUNK else 2, length, length // 2), jnp.float32)],
        compiler_params=params(8 if length <= CHUNK else 40),
        cost_estimate=pl.CostEstimate(
            flops=4 * WD * heads * size * length * length,
            bytes_accessed=4 * WD * heads * length * length,
            transcendentals=WD * heads * length * length // 2,
        ),
        name="early",
    )(mine, q, k, v)


def attend_kernel(
    mine_ref, other_ref, early_ref, q0, k0, v0, g0,
    gain_ref, shift_ref, proj_ref, gate_ref, weight_ref, offset_ref,
    out0, out1, turned_bias, bias, late, mixed, q1, k1, v1, g1,
):
    chips, along, _, _ = mine_ref.shape
    _, heads, length, size = k0.shape
    half = length // 2
    rows = half // (chips * along)
    packed = 2 * heads * rows * (length // mine_ref.shape[3])
    first = pl.multiple_of(packed + lax.rem(lax.axis_index("col"), 2) * WD * rows, WD * rows)
    offset = turned(gate_ref[1:2, :])
    blocks = []
    for source in (mine_ref, other_ref):
        for flip in range(chips):
            for shift in range(along):
                both = source[flip, shift, pl.ds(first, WD * rows), :].astype(jnp.float32)
                blocks.append(both.reshape(WD, rows, -1))
    lines = standardize_all([jnp.concatenate([block[w] for block in blocks], 0) for w in range(WD)])
    lines = [line * gain_ref[1:2, :] + shift_ref[1:2, :] for line in lines]
    keys_and_values([line.astype(jnp.bfloat16) for line in lines], proj_ref[1], k1, v1)
    ordered = [to_devices(line, along, chips, rows).astype(jnp.bfloat16) for line in lines]
    queries_and_gates(ordered, size ** (-0.5), proj_ref[1], offset, q1, g1)
    groups = start_half(other_ref, 1, q0, k0, v0, late, turned_bias)
    for pack in range(heads // 2):
        unpack(mine_ref, 1, pack, rows, heads, 0, bias, 0)
        unpack(other_ref, 1, pack, rows, heads, 0, bias, half)
        pair = (2 * pack, 2 * pack + 1)
        if length == CHUNK:
            groups.append(
                head_group(pair, size, q1, k1, v1, bias, mixed, pl.ds(0, length), pl.ds(0, length))
            )
            continue

        def step(chunk):
            there = pl.ds(pl.multiple_of(chunk * CHUNK, CHUNK), CHUNK)
            for h in pair:
                attend_groups([head_group((h,), size, q1, k1, v1, bias, mixed, there, there)])

        for_each(length // CHUNK, step, False)
    attend_groups(groups)
    for w in range(WD):
        gated = (jnp.concatenate([early_ref[w], late[w]], 1) * g0[w]).astype(jnp.bfloat16)
        full = contract(gated, weight_ref[0], 0, 0) + offset_ref[0:1, :]
        out0[w] = to_devices(full, along, chips, rows).astype(jnp.bfloat16)
    for w in range(WD):
        gated = (mixed[w] * g1[w]).astype(jnp.bfloat16)
        full = contract(gated, weight_ref[1], 0, 0) + offset_ref[1:2, :]
        out1[w] = full.astype(jnp.bfloat16)


def attend(mine, other, early, start, gain, shift, proj, gate, weight, offset):
    _, heads, length, size = start[1].shape
    inner, channels = weight.shape[1:]
    result = jax.ShapeDtypeStruct((WD, length, channels), jnp.bfloat16)
    slots = heads if length <= CHUNK else 2
    return pl.pallas_call(
        attend_kernel,
        out_shape=(result, result),
        in_specs=[VMEM] * 13,
        out_specs=(VMEM, VMEM),
        scratch_shapes=[
            pltpu.VMEM((slots, length, length // 2), jnp.float32),
            pltpu.VMEM((slots, length, length), jnp.float32),
            pltpu.VMEM((WD, inner, length // 2), jnp.float32),
            pltpu.VMEM((WD, inner, length), jnp.float32),
        ]
        + [pltpu.VMEM(shape, dtype) for shape, dtype in projected(length, inner, heads)],
        compiler_params=params(16 if length <= CHUNK else 60),
        name="attend",
    )(mine, other, early, *start, gain, shift, proj, gate, weight, offset)


def body(pair, residue_mask, ln_gain, ln_shift, w_proj, w_bias, gate_bias, w_out, out_bias):
    rows, length, channels = pair.shape
    heads = w_bias.shape[2]
    along, cols = lax.axis_size("row"), lax.axis_size("col")
    chips = cols // 2

    def by_row(block, shift):
        return lax.ppermute(block, "row", [(i, i ^ shift) for i in range(along)])

    def by_col(block, flip):
        return lax.ppermute(block, "col", [(i, i ^ flip) for i in range(cols)])

    sent = local_bias(
        pair, residue_mask[None, :], ln_gain, ln_shift, jnp.transpose(w_bias, (0, 2, 1)), along, chips
    )
    far_first = [by_row(sent[flip], flip) for flip in reversed(range(1, along))]
    line = jnp.stack(far_first + [sent[0]])
    start = local_lines(pair, ln_gain, ln_shift, w_proj, gate_bias, heads, along, chips)
    line, _ = lax.optimization_barrier((line, start))
    packed = 2 * heads * rows * (length // channels)
    both = 2 * WD * rows

    def owned_by(flip):
        at = packed + flip * both
        return jnp.concatenate([line[:, :packed], line[:, at : at + both]], 1)

    mine = jnp.stack([owned_by(0)] + [by_col(owned_by(flip), 2 * flip) for flip in range(1, chips)])
    other = by_col(mine, 1)
    early = attend_early(mine, *start[:3])
    return attend(mine, other, early, start, ln_gain, ln_shift, w_proj, gate_bias, w_out, out_bias)


def solution(mesh):
    return jax.shard_map(
        body,
        mesh=mesh,
        in_specs=(P(("row", "col"), None, None), P(), P(), P(), P(), P(), P(), P(), P()),
        out_specs=(P(("row", "col"), None, None), P(("row", "col"), None, None)),
        check_vma=False,
    )
```

```python
import functools

import jax
import jax.numpy as jnp
from jax import lax
from jax.experimental import pallas as pl
from jax.experimental.pallas import tpu as pltpu
from jax.sharding import PartitionSpec as P

WD = 2
EPS = 1e-05
MASKED = -1000000000.0
CHUNK = 256
VMEM = pl.BlockSpec(memory_space=pltpu.VMEM)
HBM = pl.BlockSpec(memory_space=pltpu.HBM)


def params(megabytes):
    return pltpu.CompilerParams(vmem_limit_bytes=megabytes * 1024 * 1024)


def for_each(count, step, unrolled):
    if unrolled:
        for index in range(count):
            step(index)
    else:
        lax.fori_loop(0, count, lambda index, carry: (step(index), carry)[1], 0)


def standardize_all(lines):
    centers = [jnp.mean(wide, -1, keepdims=True) for wide in lines]
    aways = [wide - center for wide, center in zip(lines, centers)]
    spreads = [jnp.mean(jnp.square(away), -1, keepdims=True) for away in aways]
    return [away * lax.rsqrt(spread + EPS) for away, spread in zip(aways, spreads)]


def contract(left, right, left_dim, right_dim):
    return lax.dot_general(
        left, right, (((left_dim,), (right_dim,)), ((), ())), preferred_element_type=jnp.float32
    )


def flipped(index, flip):
    bit = 1
    while bit <= flip:
        if flip & bit:
            index = index + bit - 2 * bit * lax.rem(lax.div(index, bit), 2)
        bit *= 2
    return index


def bias_kernel(along, chips, pair_hbm, live_hbm, gain_hbm, shift_hbm, weight_hbm, *rest):
    outs = rest[:along]
    pair, live_row, gain, shift, weight, blocks, rows_out, wide, picked, sems = rest[along:]
    rows, length, channels = pair.shape
    heads = weight.shape[1]
    lanes = outs[0].shape[1]
    copies = [
        pltpu.make_async_copy(source, target, sems.at[i])
        for i, (source, target) in enumerate(
            ((pair_hbm, pair), (live_hbm, live_row), (gain_hbm, gain), (shift_hbm, shift), (weight_hbm, weight))
        )
    ]
    for copy in copies:
        copy.start()
    device = lax.axis_index("row") * lax.axis_size("col") + lax.axis_index("col")
    for copy in copies:
        copy.wait()
    blocks[...] = jnp.zeros_like(blocks)
    for p in range(2):
        at = slice(p * heads, (p + 1) * heads)
        blocks[at, p * channels : (p + 1) * channels] = weight[p].astype(jnp.float32)
    paired = blocks[: 2 * heads].astype(jnp.bfloat16)
    live = jnp.broadcast_to(live_row[...], (2 * heads, length)).astype(jnp.float32)
    first = lax.broadcasted_iota(jnp.int32, live.shape, 0) < heads
    token = lax.broadcasted_iota(jnp.int32, (rows, length), 1)
    mine = device * rows + lax.broadcasted_iota(jnp.int32, (rows, length), 0)
    here = jnp.where(token == mine, live_row[...], 0).astype(jnp.float32)
    here = jnp.sum(here, 1, keepdims=True)
    lines = [pair[a].astype(jnp.float32) for a in range(rows)]
    for a, x in enumerate(lines):
        wide[a] = x
    lines = standardize_all(lines)
    normed = [
        jnp.concatenate(
            [(z * gain[p : p + 1, :] + shift[p : p + 1, :]).astype(jnp.bfloat16) for p in range(2)], 1
        )
        for z in lines
    ]
    biases = [contract(paired, line, 1, 1) for line in normed]
    devices = length // rows
    for a in range(rows):
        for w in range(WD):
            column = wide[a, pl.ds(w, devices, stride=rows), :]
            picked[pl.ds(w * rows + a, devices, stride=WD * rows), :] = column
    for a, bias in enumerate(biases):
        kept = jnp.where(first, live, here[a : a + 1])
        bias = jnp.where(kept > 0, bias, MASKED)
        for lane in range(length // lanes):
            part = bias[:, lane * lanes : (lane + 1) * lanes]
            rows_out[pl.ds(2 * lane * heads * rows + a, 2 * heads, stride=rows), :] = part
    chip = lax.div(lax.axis_index("col"), 2)
    both = 2 * WD * rows
    packed = rows_out.shape[0]
    sent = rows_out[...].astype(jnp.bfloat16)
    for shift_by, out in enumerate(outs):
        out[:packed] = sent
        row = flipped(lax.axis_index("row"), shift_by)
        for flip in range(chips):
            at = pl.multiple_of((row * chips + flipped(chip, flip)) * both, both)
            out[packed + flip * both : packed + (flip + 1) * both] = picked[pl.ds(at, both), :].astype(jnp.bfloat16)


def local_bias(pair, live, gain, shift, weight, along, chips):
    rows, length, channels = pair.shape
    heads = weight.shape[1]
    packed = 2 * heads * rows * (length // channels)
    sent = jax.ShapeDtypeStruct((packed + chips * 2 * WD * rows, channels), jnp.bfloat16)
    return pl.pallas_call(
        functools.partial(bias_kernel, along, chips),
        out_shape=(sent,) * along,
        in_specs=[HBM] * 5,
        out_specs=(VMEM,) * along,
        scratch_shapes=[
            pltpu.VMEM(pair.shape, pair.dtype),
            pltpu.VMEM(live.shape, live.dtype),
            pltpu.VMEM(gain.shape, gain.dtype),
            pltpu.VMEM(shift.shape, shift.dtype),
            pltpu.VMEM(weight.shape, weight.dtype),
            pltpu.VMEM((4 * heads, 2 * channels), jnp.float32),
            pltpu.VMEM((packed, channels), jnp.float32),
            pltpu.VMEM(pair.shape, jnp.float32),
            pltpu.VMEM((length * WD, channels), jnp.float32),
            pltpu.SemaphoreType.DMA((5,)),
        ],
        compiler_params=params(60),
        name="bias",
    )(pair, live, gain, shift, weight)


def turned(row):
    return jnp.broadcast_to(row, (row.shape[1], row.shape[1])).T[:, :1]


def turned_over(index, bit):
    return lax.rem(lax.div(index, bit), 2) == 1


def exchanged(grid, row, col):
    along, cols = len(grid), len(grid[0])
    bit = 1
    while bit < cols:
        swap = turned_over(col, bit)
        grid = [[jnp.where(swap, line[c ^ bit], line[c]) for c in range(cols)] for line in grid]
        bit *= 2
    bit = 1
    while bit < along:
        swap = turned_over(row, bit)
        grid = [[jnp.where(swap, grid[r ^ bit][c], grid[r][c]) for c in range(cols)] for r in range(along)]
        bit *= 2
    return grid


def to_relative(x, along, chips, rows):
    cols = 2 * chips
    grid = [[x[(r * cols + c) * rows : (r * cols + c + 1) * rows] for c in range(cols)] for r in range(along)]
    grid = exchanged(grid, lax.axis_index("row"), lax.axis_index("col"))
    return jnp.concatenate(
        [grid[s][2 * flip + other] for other in range(2) for flip in range(chips) for s in reversed(range(along))], 0
    )


def to_devices(x, along, chips, rows):
    at = lambda c, s: (((c % 2) * chips + c // 2) * along + along - 1 - s) * rows
    grid = [[x[at(c, s) : at(c, s) + rows] for c in range(2 * chips)] for s in range(along)]
    grid = exchanged(grid, lax.axis_index("row"), lax.axis_index("col"))
    return jnp.concatenate([block for line in grid for block in line], 0)


def queries_and_gates(lines, scale, weight, offset, q_ref, g_ref):
    inner = weight.shape[1] // 4
    queries = [contract(weight[:, :inner], normed, 0, 1) for normed in lines]
    gates = [contract(weight[:, 3 * inner :], normed, 0, 1) for normed in lines]
    for w in range(WD):
        q_ref[w] = (queries[w] * scale).astype(jnp.bfloat16)
        g_ref[w] = jax.nn.sigmoid(gates[w] + offset)


def keys_and_values(lines, weight, k_ref, v_ref):
    _, heads, _, size = k_ref.shape
    inner = heads * size
    for h in range(heads):
        at = inner + h * size
        keys = [contract(normed, weight[:, at : at + size], 1, 0) for normed in lines]
        for w in range(WD):
            k_ref[w, h] = keys[w].astype(jnp.bfloat16)
    values = [contract(weight[:, 2 * inner : 3 * inner], normed, 0, 1) for normed in lines]
    for w in range(WD):
        v_ref[w] = values[w].astype(jnp.bfloat16)


def lines_kernel(along, chips, lines_ref, gain_ref, shift_ref, weight_ref, offset_ref, q_ref, k_ref, v_ref, g_ref):
    size = k_ref.shape[-1]
    rows = lines_ref.shape[1] // (2 * chips * along)
    offset = turned(offset_ref[0:1, :])
    weight = weight_ref[0]
    lines = standardize_all([lines_ref[w].astype(jnp.float32) for w in range(WD)])
    lines = [line * gain_ref[0:1, :] + shift_ref[0:1, :] for line in lines]
    keys_and_values([line.astype(jnp.bfloat16) for line in lines], weight, k_ref, v_ref)
    near = [to_relative(line, along, chips, rows).astype(jnp.bfloat16) for line in lines]
    queries_and_gates(near, size ** (-0.5), weight, offset, q_ref, g_ref)


def projected(length, inner, heads):
    wide = (WD, inner, length)
    return (
        (wide, jnp.bfloat16),
        ((WD, heads, length, inner // heads), jnp.bfloat16),
        (wide, jnp.bfloat16),
        (wide, jnp.float32),
    )


def local_lines(pair, gain, shift, weight, offset, heads, along, chips):
    _, length, channels = pair.shape
    wide = weight.shape[2]
    shapes = projected(length, wide // 4, heads)
    whole = lambda shape: pl.BlockSpec(shape, lambda i: (0,) * len(shape))
    return pl.pallas_call(
        functools.partial(lines_kernel, along, chips),
        grid=(1,),
        out_shape=tuple(jax.ShapeDtypeStruct(shape, dtype) for shape, dtype in shapes),
        in_specs=[
            whole((WD, length, channels)), whole(gain.shape), whole(gain.shape),
            whole((1, channels, wide)), whole(gain.shape),
        ],
        out_specs=tuple(whole(shape) for shape, _ in shapes),
        compiler_params=params(8 + length // 32),
        cost_estimate=pl.CostEstimate(
            flops=2 * WD * length * channels * wide, bytes_accessed=4 * WD * length * wide, transcendentals=0
        ),
        name="lines",
    )(pair, gain, shift, weight, offset)


def unpack(source, p, pack, rows, heads, turn, into, at):
    chips, along, _, lanes = source.shape
    packed = 2 * heads * rows
    half = chips * along * rows
    slots = into.shape[0]
    for lane in range(into.shape[2 - turn] // lanes):
        first = lane * packed + (p * heads + 2 * pack) * rows
        both = [
            source[flip, shift, first : first + 2 * rows, :].astype(jnp.float32)
            for flip in range(chips)
            for shift in range(along)
        ]
        there = slice(lane * lanes, (lane + 1) * lanes)
        for i in range(2):
            slot = (2 * pack + i) % slots
            block = jnp.concatenate([part[i * rows : (i + 1) * rows] for part in both], 0)
            if turn:
                into[slot, there, at : at + half] = block.T
            else:
                into[slot, at : at + half, there] = block


def score(units):
    return [contract(key, query, 1, 0) + added for key, query, added, _ in units]


def mix(units, scores):
    tops = [jnp.max(part, 0, keepdims=True) for part in scores]
    expos = [jnp.exp(part - top) for part, top in zip(scores, tops)]
    shares = [1.0 / jnp.sum(expo, 0, keepdims=True) for expo in expos]
    weights = [(expo * share).astype(jnp.bfloat16) for expo, share in zip(expos, shares)]
    return [contract(unit[3], weight, 1, 0) for unit, weight in zip(units, weights)]


def attend_groups(groups):
    if not groups:
        return
    ready = score(groups[0][0]())
    for i, (units, put) in enumerate(groups):
        ahead = score(groups[i + 1][0]()) if i + 1 < len(groups) else None
        put(mix(units(), ready))
        ready = ahead


def head_group(heads, size, q, k, v, bias, mixed, there, near):
    def units():
        return [
            (k[w, h], q[w, h * size : (h + 1) * size, there], bias[h % bias.shape[0], :, near],
             v[w, h * size : (h + 1) * size, :])
            for h in heads
            for w in range(WD)
        ]

    def put(outs):
        for i, h in enumerate(heads):
            for w in range(WD):
                mixed[w, h * size : (h + 1) * size, near] = outs[i * WD + w]

    return units, put


def start_half(source, other, q, k, v, mixed, bias):
    _, heads, length, size = k.shape
    half = length // 2
    rows = half // (source.shape[0] * source.shape[1])
    width = min(half, CHUNK)
    if half == width:
        groups = []
        for pack in range(heads // 2):
            unpack(source, 0, pack, rows, heads, 1, bias, 0)
            groups.append(
                head_group(
                    (2 * pack, 2 * pack + 1), size, q, k, v, bias, mixed,
                    pl.ds(other * half, half), pl.ds(0, half),
                )
            )
        return groups
    for pack in range(heads // 2):
        unpack(source, 0, pack, rows, heads, 1, bias, 0)

        def step(chunk):
            near = pl.ds(pl.multiple_of(chunk * width, width), width)
            there = pl.ds(pl.multiple_of(other * half + chunk * width, width), width)
            for h in (2 * pack, 2 * pack + 1):
                attend_groups([head_group((h,), size, q, k, v, bias, mixed, there, near)])

        for_each(half // width, step, False)
    return []


def early_kernel(mine_ref, q, k, v, mixed, bias):
    attend_groups(start_half(mine_ref, 0, q, k, v, mixed, bias))


def attend_early(mine, q, k, v):
    _, heads, length, size = k.shape
    return pl.pallas_call(
        early_kernel,
        out_shape=jax.ShapeDtypeStruct((WD, heads * size, length // 2), jnp.float32),
        in_specs=[VMEM] * 4,
        out_specs=VMEM,
        scratch_shapes=[pltpu.VMEM((heads if length <= CHUNK else 2, length, length // 2), jnp.float32)],
        compiler_params=params(8 if length <= CHUNK else 40),
        cost_estimate=pl.CostEstimate(
            flops=4 * WD * heads * size * length * length,
            bytes_accessed=4 * WD * heads * length * length,
            transcendentals=WD * heads * length * length // 2,
        ),
        name="early",
    )(mine, q, k, v)


def attend_kernel(
    mine_ref, other_ref, early_ref, q0, k0, v0, g0,
    gain_ref, shift_ref, proj_ref, gate_ref, weight_ref, offset_ref,
    out0, out1, turned_bias, bias, late, mixed, kept, sem, q1, k1, v1, g1,
):
    chips, along, _, _ = mine_ref.shape
    _, heads, length, size = k0.shape
    half = length // 2
    rows = half // (chips * along)
    packed = 2 * heads * rows * (length // mine_ref.shape[3])
    first = pl.multiple_of(packed + lax.rem(lax.axis_index("col"), 2) * WD * rows, WD * rows)
    offset = turned(gate_ref[1:2, :])
    blocks = []
    for source in (mine_ref, other_ref):
        for flip in range(chips):
            for shift in range(along):
                both = source[flip, shift, pl.ds(first, WD * rows), :].astype(jnp.float32)
                blocks.append(both.reshape(WD, rows, -1))
    lines = standardize_all([jnp.concatenate([block[w] for block in blocks], 0) for w in range(WD)])
    lines = [line * gain_ref[1:2, :] + shift_ref[1:2, :] for line in lines]
    keys_and_values([line.astype(jnp.bfloat16) for line in lines], proj_ref[1], k1, v1)
    ordered = [to_devices(line, along, chips, rows).astype(jnp.bfloat16) for line in lines]
    queries_and_gates(ordered, size ** (-0.5), proj_ref[1], offset, q1, g1)
    groups = start_half(other_ref, 1, q0, k0, v0, late, turned_bias)
    leaving = pltpu.make_async_copy(kept, out0, sem)

    def finish_start():
        for w in range(WD):
            gated = (jnp.concatenate([early_ref[w], late[w]], 1) * g0[w]).astype(jnp.bfloat16)
            full = contract(gated, weight_ref[0], 0, 0) + offset_ref[0:1, :]
            kept[w] = to_devices(full, along, chips, rows).astype(jnp.bfloat16)
        leaving.start()

    if groups:
        groups[-1] = (groups[-1][0], lambda outs, put=groups[-1][1]: (put(outs), finish_start()))
    else:
        finish_start()
    for pack in range(heads // 2):
        unpack(mine_ref, 1, pack, rows, heads, 0, bias, 0)
        unpack(other_ref, 1, pack, rows, heads, 0, bias, half)
        pair = (2 * pack, 2 * pack + 1)
        if length == CHUNK:
            groups.append(
                head_group(pair, size, q1, k1, v1, bias, mixed, pl.ds(0, length), pl.ds(0, length))
            )
            continue

        def step(chunk):
            there = pl.ds(pl.multiple_of(chunk * CHUNK, CHUNK), CHUNK)
            for h in pair:
                attend_groups([head_group((h,), size, q1, k1, v1, bias, mixed, there, there)])

        for_each(length // CHUNK, step, False)
    attend_groups(groups)
    for w in range(WD):
        gated = (mixed[w] * g1[w]).astype(jnp.bfloat16)
        full = contract(gated, weight_ref[1], 0, 0) + offset_ref[1:2, :]
        out1[w] = full.astype(jnp.bfloat16)
    leaving.wait()


def attend(mine, other, early, start, gain, shift, proj, gate, weight, offset):
    _, heads, length, size = start[1].shape
    inner, channels = weight.shape[1:]
    result = jax.ShapeDtypeStruct((WD, length, channels), jnp.bfloat16)
    slots = heads if length <= CHUNK else 2
    return pl.pallas_call(
        attend_kernel,
        out_shape=(result, result),
        in_specs=[VMEM] * 13,
        out_specs=(HBM, VMEM),
        scratch_shapes=[
            pltpu.VMEM((slots, length, length // 2), jnp.float32),
            pltpu.VMEM((slots, length, length), jnp.float32),
            pltpu.VMEM((WD, inner, length // 2), jnp.float32),
            pltpu.VMEM((WD, inner, length), jnp.float32),
            pltpu.VMEM((WD, length, channels), jnp.bfloat16),
            pltpu.SemaphoreType.DMA(()),
        ]
        + [pltpu.VMEM(shape, dtype) for shape, dtype in projected(length, inner, heads)],
        compiler_params=params(16 if length <= CHUNK else 60),
        name="attend",
    )(mine, other, early, *start, gain, shift, proj, gate, weight, offset)


def body(pair, residue_mask, ln_gain, ln_shift, w_proj, w_bias, gate_bias, w_out, out_bias):
    rows, length, channels = pair.shape
    heads = w_bias.shape[2]
    along, cols = lax.axis_size("row"), lax.axis_size("col")
    chips = cols // 2

    def by_row(block, shift):
        return lax.ppermute(block, "row", [(i, i ^ shift) for i in range(along)])

    def by_col(block, flip):
        return lax.ppermute(block, "col", [(i, i ^ flip) for i in range(cols)])

    sent = local_bias(
        pair, residue_mask[None, :], ln_gain, ln_shift, jnp.transpose(w_bias, (0, 2, 1)), along, chips
    )
    far_first = [by_row(sent[flip], flip) for flip in reversed(range(1, along))]
    line = jnp.stack(far_first + [sent[0]])
    start = local_lines(pair, ln_gain, ln_shift, w_proj, gate_bias, heads, along, chips)
    line, _ = lax.optimization_barrier((line, start))
    packed = 2 * heads * rows * (length // channels)
    both = 2 * WD * rows

    def owned_by(flip):
        at = packed + flip * both
        return jnp.concatenate([line[:, :packed], line[:, at : at + both]], 1)

    mine = jnp.stack([owned_by(0)] + [by_col(owned_by(flip), 2 * flip) for flip in range(1, chips)])
    other = by_col(mine, 1)
    early = attend_early(mine, *start[:3])
    return attend(mine, other, early, start, ln_gain, ln_shift, w_proj, gate_bias, w_out, out_bias)


def solution(mesh):
    return jax.shard_map(
        body,
        mesh=mesh,
        in_specs=(P(("row", "col"), None, None), P(), P(), P(), P(), P(), P(), P(), P()),
        out_specs=(P(("row", "col"), None, None), P(("row", "col"), None, None)),
        check_vma=False,
    )
```

```python
import functools

import jax
import jax.numpy as jnp
from jax import lax
from jax.experimental import pallas as pl
from jax.experimental.pallas import tpu as pltpu
from jax.sharding import PartitionSpec as P

WD = 2
EPS = 1e-05
MASKED = -1000000000.0
CHUNK = 256
VMEM = pl.BlockSpec(memory_space=pltpu.VMEM)
HBM = pl.BlockSpec(memory_space=pltpu.HBM)


def params(megabytes):
    return pltpu.CompilerParams(vmem_limit_bytes=megabytes * 1024 * 1024)


def for_each(count, step, unrolled):
    if unrolled:
        for index in range(count):
            step(index)
    else:
        lax.fori_loop(0, count, lambda index, carry: (step(index), carry)[1], 0)


def standardize_all(lines):
    centers = [jnp.mean(wide, -1, keepdims=True) for wide in lines]
    aways = [wide - center for wide, center in zip(lines, centers)]
    spreads = [jnp.mean(jnp.square(away), -1, keepdims=True) for away in aways]
    return [away * lax.rsqrt(spread + EPS) for away, spread in zip(aways, spreads)]


def contract(left, right, left_dim, right_dim):
    return lax.dot_general(
        left, right, (((left_dim,), (right_dim,)), ((), ())), preferred_element_type=jnp.float32
    )


def flipped(index, flip):
    bit = 1
    while bit <= flip:
        if flip & bit:
            index = index + bit - 2 * bit * lax.rem(lax.div(index, bit), 2)
        bit *= 2
    return index


def bias_kernel(along, chips, pair_hbm, live_hbm, gain_hbm, shift_hbm, weight_hbm, *rest):
    outs = rest[:along]
    pair, live_row, gain, shift, weight, blocks, rows_out, wide, picked, sems = rest[along:]
    rows, length, channels = pair.shape
    heads = weight.shape[1]
    lanes = outs[0].shape[1]
    copies = [
        pltpu.make_async_copy(source, target, sems.at[i])
        for i, (source, target) in enumerate(
            ((pair_hbm, pair), (live_hbm, live_row), (gain_hbm, gain), (shift_hbm, shift), (weight_hbm, weight))
        )
    ]
    for copy in copies:
        copy.start()
    device = lax.axis_index("row") * lax.axis_size("col") + lax.axis_index("col")
    for copy in copies:
        copy.wait()
    blocks[...] = jnp.zeros_like(blocks)
    for p in range(2):
        at = slice(p * heads, (p + 1) * heads)
        blocks[at, p * channels : (p + 1) * channels] = weight[p].astype(jnp.float32)
    paired = blocks[: 2 * heads].astype(jnp.bfloat16)
    live = jnp.broadcast_to(live_row[...], (2 * heads, length)).astype(jnp.float32)
    first = lax.broadcasted_iota(jnp.int32, live.shape, 0) < heads
    token = lax.broadcasted_iota(jnp.int32, (rows, length), 1)
    mine = device * rows + lax.broadcasted_iota(jnp.int32, (rows, length), 0)
    here = jnp.where(token == mine, live_row[...], 0).astype(jnp.float32)
    here = jnp.sum(here, 1, keepdims=True)
    lines = [pair[a].astype(jnp.float32) for a in range(rows)]
    for a, x in enumerate(lines):
        wide[a] = x
    lines = standardize_all(lines)
    normed = [
        jnp.concatenate(
            [(z * gain[p : p + 1, :] + shift[p : p + 1, :]).astype(jnp.bfloat16) for p in range(2)], 1
        )
        for z in lines
    ]
    biases = [contract(paired, line, 1, 1) for line in normed]
    devices = length // rows
    for a in range(rows):
        for w in range(WD):
            column = wide[a, pl.ds(w, devices, stride=rows), :]
            picked[pl.ds(w * rows + a, devices, stride=WD * rows), :] = column
    for a, bias in enumerate(biases):
        kept = jnp.where(first, live, here[a : a + 1])
        bias = jnp.where(kept > 0, bias, MASKED)
        for lane in range(length // lanes):
            part = bias[:, lane * lanes : (lane + 1) * lanes]
            rows_out[pl.ds(2 * lane * heads * rows + a, 2 * heads, stride=rows), :] = part
    chip = lax.div(lax.axis_index("col"), 2)
    both = 2 * WD * rows
    packed = rows_out.shape[0]
    sent = rows_out[...].astype(jnp.bfloat16)
    for shift_by, out in enumerate(outs):
        out[:packed] = sent
        row = flipped(lax.axis_index("row"), shift_by)
        for flip in range(chips):
            at = pl.multiple_of((row * chips + flipped(chip, flip)) * both, both)
            out[packed + flip * both : packed + (flip + 1) * both] = picked[pl.ds(at, both), :].astype(jnp.bfloat16)


def local_bias(pair, live, gain, shift, weight, along, chips):
    rows, length, channels = pair.shape
    heads = weight.shape[1]
    packed = 2 * heads * rows * (length // channels)
    sent = jax.ShapeDtypeStruct((packed + chips * 2 * WD * rows, channels), jnp.bfloat16)
    return pl.pallas_call(
        functools.partial(bias_kernel, along, chips),
        out_shape=(sent,) * along,
        in_specs=[HBM] * 5,
        out_specs=(VMEM,) * along,
        scratch_shapes=[
            pltpu.VMEM(pair.shape, pair.dtype),
            pltpu.VMEM(live.shape, live.dtype),
            pltpu.VMEM(gain.shape, gain.dtype),
            pltpu.VMEM(shift.shape, shift.dtype),
            pltpu.VMEM(weight.shape, weight.dtype),
            pltpu.VMEM((4 * heads, 2 * channels), jnp.float32),
            pltpu.VMEM((packed, channels), jnp.float32),
            pltpu.VMEM(pair.shape, jnp.float32),
            pltpu.VMEM((length * WD, channels), jnp.float32),
            pltpu.SemaphoreType.DMA((5,)),
        ],
        compiler_params=params(60),
        name="bias",
    )(pair, live, gain, shift, weight)


def turned(row):
    return jnp.broadcast_to(row, (row.shape[1], row.shape[1])).T[:, :1]


def turned_over(index, bit):
    return lax.rem(lax.div(index, bit), 2) == 1


def exchanged(grid, row, col):
    along, cols = len(grid), len(grid[0])
    bit = 1
    while bit < cols:
        swap = turned_over(col, bit)
        grid = [[jnp.where(swap, line[c ^ bit], line[c]) for c in range(cols)] for line in grid]
        bit *= 2
    bit = 1
    while bit < along:
        swap = turned_over(row, bit)
        grid = [[jnp.where(swap, grid[r ^ bit][c], grid[r][c]) for c in range(cols)] for r in range(along)]
        bit *= 2
    return grid


def to_relative(x, along, chips, rows):
    cols = 2 * chips
    grid = [[x[(r * cols + c) * rows : (r * cols + c + 1) * rows] for c in range(cols)] for r in range(along)]
    grid = exchanged(grid, lax.axis_index("row"), lax.axis_index("col"))
    return jnp.concatenate(
        [grid[s][2 * flip + other] for other in range(2) for flip in range(chips) for s in reversed(range(along))], 0
    )


def to_devices(x, along, chips, rows):
    at = lambda c, s: (((c % 2) * chips + c // 2) * along + along - 1 - s) * rows
    grid = [[x[at(c, s) : at(c, s) + rows] for c in range(2 * chips)] for s in range(along)]
    grid = exchanged(grid, lax.axis_index("row"), lax.axis_index("col"))
    return jnp.concatenate([block for line in grid for block in line], 0)


def queries_and_gates(lines, scale, weight, offset, q_ref, g_ref):
    inner = weight.shape[1] // 4
    queries = [contract(weight[:, :inner], normed, 0, 1) for normed in lines]
    gates = [contract(weight[:, 3 * inner :], normed, 0, 1) for normed in lines]
    for w in range(WD):
        q_ref[w] = (queries[w] * scale).astype(jnp.bfloat16)
        g_ref[w] = jax.nn.sigmoid(gates[w] + offset)


def keys_and_values(lines, weight, k_ref, v_ref):
    _, heads, _, size = k_ref.shape
    inner = heads * size
    for h in range(heads):
        at = inner + h * size
        keys = [contract(normed, weight[:, at : at + size], 1, 0) for normed in lines]
        for w in range(WD):
            k_ref[w, h] = keys[w].astype(jnp.bfloat16)
    values = [contract(weight[:, 2 * inner : 3 * inner], normed, 0, 1) for normed in lines]
    for w in range(WD):
        v_ref[w] = values[w].astype(jnp.bfloat16)


def lines_kernel(along, chips, lines_ref, gain_ref, shift_ref, weight_ref, offset_ref, q_ref, k_ref, v_ref, g_ref):
    size = k_ref.shape[-1]
    rows = lines_ref.shape[1] // (2 * chips * along)
    offset = turned(offset_ref[0:1, :])
    weight = weight_ref[0]
    lines = standardize_all([lines_ref[w].astype(jnp.float32) for w in range(WD)])
    lines = [line * gain_ref[0:1, :] + shift_ref[0:1, :] for line in lines]
    keys_and_values([line.astype(jnp.bfloat16) for line in lines], weight, k_ref, v_ref)
    near = [to_relative(line, along, chips, rows).astype(jnp.bfloat16) for line in lines]
    queries_and_gates(near, size ** (-0.5), weight, offset, q_ref, g_ref)


def projected(length, inner, heads):
    wide = (WD, inner, length)
    return (
        (wide, jnp.bfloat16),
        ((WD, heads, length, inner // heads), jnp.bfloat16),
        (wide, jnp.bfloat16),
        (wide, jnp.float32),
    )


def local_lines(pair, gain, shift, weight, offset, heads, along, chips):
    _, length, channels = pair.shape
    wide = weight.shape[2]
    shapes = projected(length, wide // 4, heads)
    whole = lambda shape: pl.BlockSpec(shape, lambda i: (0,) * len(shape))
    return pl.pallas_call(
        functools.partial(lines_kernel, along, chips),
        grid=(1,),
        out_shape=tuple(jax.ShapeDtypeStruct(shape, dtype) for shape, dtype in shapes),
        in_specs=[
            whole((WD, length, channels)), whole(gain.shape), whole(gain.shape),
            whole((1, channels, wide)), whole(gain.shape),
        ],
        out_specs=tuple(whole(shape) for shape, _ in shapes),
        compiler_params=params(8 + length // 32),
        cost_estimate=pl.CostEstimate(
            flops=2 * WD * length * channels * wide, bytes_accessed=4 * WD * length * wide, transcendentals=0
        ),
        name="lines",
    )(pair, gain, shift, weight, offset)


def unpack(source, p, pack, rows, heads, turn, into, at):
    chips, along, _, lanes = source.shape
    packed = 2 * heads * rows
    half = chips * along * rows
    slots = into.shape[0]
    for lane in range(into.shape[2 - turn] // lanes):
        first = lane * packed + (p * heads + 2 * pack) * rows
        both = [
            source[flip, shift, first : first + 2 * rows, :].astype(jnp.float32)
            for flip in range(chips)
            for shift in range(along)
        ]
        there = slice(lane * lanes, (lane + 1) * lanes)
        for i in range(2):
            slot = (2 * pack + i) % slots
            block = jnp.concatenate([part[i * rows : (i + 1) * rows] for part in both], 0)
            if turn:
                into[slot, there, at : at + half] = block.T
            else:
                into[slot, at : at + half, there] = block


def score(units):
    return [contract(key, query, 1, 0) + added for key, query, added, _ in units]


def mix(units, scores):
    tops = [jnp.max(part, 0, keepdims=True) for part in scores]
    expos = [jnp.exp(part - top) for part, top in zip(scores, tops)]
    shares = [1.0 / jnp.sum(expo, 0, keepdims=True) for expo in expos]
    weights = [(expo * share).astype(jnp.bfloat16) for expo, share in zip(expos, shares)]
    return [contract(unit[3], weight, 1, 0) for unit, weight in zip(units, weights)]


def attend_groups(groups, ready=None):
    if not groups:
        return
    if ready is None:
        ready = score(groups[0][0]())
    for i, (units, put) in enumerate(groups):
        ahead = score(groups[i + 1][0]()) if i + 1 < len(groups) else None
        put(mix(units(), ready))
        ready = ahead


def head_group(heads, size, q, k, v, bias, mixed, there, near):
    def units():
        return [
            (k[w, h], q[w, h * size : (h + 1) * size, there], bias[h % bias.shape[0], :, near],
             v[w, h * size : (h + 1) * size, :])
            for h in heads
            for w in range(WD)
        ]

    def put(outs):
        for i, h in enumerate(heads):
            for w in range(WD):
                mixed[w, h * size : (h + 1) * size, near] = outs[i * WD + w]

    return units, put


def start_half(source, other, q, k, v, mixed, bias):
    _, heads, length, size = k.shape
    half = length // 2
    rows = half // (source.shape[0] * source.shape[1])
    width = min(half, CHUNK)
    if half == width:
        groups = []
        for pack in range(heads // 2):
            unpack(source, 0, pack, rows, heads, 1, bias, 0)
            groups.append(
                head_group(
                    (2 * pack, 2 * pack + 1), size, q, k, v, bias, mixed,
                    pl.ds(other * half, half), pl.ds(0, half),
                )
            )
        return groups
    for pack in range(heads // 2):
        unpack(source, 0, pack, rows, heads, 1, bias, 0)

        def step(chunk):
            near = pl.ds(pl.multiple_of(chunk * width, width), width)
            there = pl.ds(pl.multiple_of(other * half + chunk * width, width), width)
            for h in (2 * pack, 2 * pack + 1):
                attend_groups([head_group((h,), size, q, k, v, bias, mixed, there, near)])

        for_each(half // width, step, False)
    return []


def early_kernel(mine_ref, q, k, v, mixed, bias):
    attend_groups(start_half(mine_ref, 0, q, k, v, mixed, bias))


def attend_early(mine, q, k, v):
    _, heads, length, size = k.shape
    return pl.pallas_call(
        early_kernel,
        out_shape=jax.ShapeDtypeStruct((WD, heads * size, length // 2), jnp.float32),
        in_specs=[VMEM] * 4,
        out_specs=VMEM,
        scratch_shapes=[pltpu.VMEM((heads if length <= CHUNK else 2, length, length // 2), jnp.float32)],
        compiler_params=params(8 if length <= CHUNK else 40),
        cost_estimate=pl.CostEstimate(
            flops=4 * WD * heads * size * length * length,
            bytes_accessed=4 * WD * heads * length * length,
            transcendentals=WD * heads * length * length // 2,
        ),
        name="early",
    )(mine, q, k, v)


def attend_kernel(
    mine_ref, other_ref, early_ref, q0, k0, v0, g0,
    gain_ref, shift_ref, proj_ref, gate_ref, weight_ref, offset_ref,
    out0, out1, turned_bias, bias, late, mixed, q1, k1, v1, g1,
):
    chips, along, _, _ = mine_ref.shape
    _, heads, length, size = k0.shape
    half = length // 2
    rows = half // (chips * along)
    packed = 2 * heads * rows * (length // mine_ref.shape[3])
    first = pl.multiple_of(packed + lax.rem(lax.axis_index("col"), 2) * WD * rows, WD * rows)
    groups = start_half(other_ref, 1, q0, k0, v0, late, turned_bias)
    ready = score(groups[0][0]()) if groups else None
    offset = turned(gate_ref[1:2, :])
    blocks = []
    for source in (mine_ref, other_ref):
        for flip in range(chips):
            for shift in range(along):
                both = source[flip, shift, pl.ds(first, WD * rows), :].astype(jnp.float32)
                blocks.append(both.reshape(WD, rows, -1))
    lines = standardize_all([jnp.concatenate([block[w] for block in blocks], 0) for w in range(WD)])
    lines = [line * gain_ref[1:2, :] + shift_ref[1:2, :] for line in lines]
    keys_and_values([line.astype(jnp.bfloat16) for line in lines], proj_ref[1], k1, v1)
    ordered = [to_devices(line, along, chips, rows).astype(jnp.bfloat16) for line in lines]
    queries_and_gates(ordered, size ** (-0.5), proj_ref[1], offset, q1, g1)
    for pack in range(heads // 2):
        unpack(mine_ref, 1, pack, rows, heads, 0, bias, 0)
        unpack(other_ref, 1, pack, rows, heads, 0, bias, half)
        pair = (2 * pack, 2 * pack + 1)
        if length == CHUNK:
            groups.append(
                head_group(pair, size, q1, k1, v1, bias, mixed, pl.ds(0, length), pl.ds(0, length))
            )
            continue

        def step(chunk):
            there = pl.ds(pl.multiple_of(chunk * CHUNK, CHUNK), CHUNK)
            for h in pair:
                attend_groups([head_group((h,), size, q1, k1, v1, bias, mixed, there, there)])

        for_each(length // CHUNK, step, False)
    attend_groups(groups, ready)
    for w in range(WD):
        gated = (jnp.concatenate([early_ref[w], late[w]], 1) * g0[w]).astype(jnp.bfloat16)
        full = contract(gated, weight_ref[0], 0, 0) + offset_ref[0:1, :]
        out0[w] = to_devices(full, along, chips, rows).astype(jnp.bfloat16)
    for w in range(WD):
        gated = (mixed[w] * g1[w]).astype(jnp.bfloat16)
        full = contract(gated, weight_ref[1], 0, 0) + offset_ref[1:2, :]
        out1[w] = full.astype(jnp.bfloat16)


def attend(mine, other, early, start, gain, shift, proj, gate, weight, offset):
    _, heads, length, size = start[1].shape
    inner, channels = weight.shape[1:]
    result = jax.ShapeDtypeStruct((WD, length, channels), jnp.bfloat16)
    slots = heads if length <= CHUNK else 2
    return pl.pallas_call(
        attend_kernel,
        out_shape=(result, result),
        in_specs=[VMEM] * 13,
        out_specs=(VMEM, VMEM),
        scratch_shapes=[
            pltpu.VMEM((slots, length, length // 2), jnp.float32),
            pltpu.VMEM((slots, length, length), jnp.float32),
            pltpu.VMEM((WD, inner, length // 2), jnp.float32),
            pltpu.VMEM((WD, inner, length), jnp.float32),
        ]
        + [pltpu.VMEM(shape, dtype) for shape, dtype in projected(length, inner, heads)],
        compiler_params=params(16 if length <= CHUNK else 60),
        name="attend",
    )(mine, other, early, *start, gain, shift, proj, gate, weight, offset)


def body(pair, residue_mask, ln_gain, ln_shift, w_proj, w_bias, gate_bias, w_out, out_bias):
    rows, length, channels = pair.shape
    heads = w_bias.shape[2]
    along, cols = lax.axis_size("row"), lax.axis_size("col")
    chips = cols // 2

    def by_row(block, shift):
        return lax.ppermute(block, "row", [(i, i ^ shift) for i in range(along)])

    def by_col(block, flip):
        return lax.ppermute(block, "col", [(i, i ^ flip) for i in range(cols)])

    sent = local_bias(
        pair, residue_mask[None, :], ln_gain, ln_shift, jnp.transpose(w_bias, (0, 2, 1)), along, chips
    )
    far_first = [by_row(sent[flip], flip) for flip in reversed(range(1, along))]
    line = jnp.stack(far_first + [sent[0]])
    start = local_lines(pair, ln_gain, ln_shift, w_proj, gate_bias, heads, along, chips)
    line, _ = lax.optimization_barrier((line, start))
    packed = 2 * heads * rows * (length // channels)
    both = 2 * WD * rows

    def owned_by(flip):
        at = packed + flip * both
        return jnp.concatenate([line[:, :packed], line[:, at : at + both]], 1)

    mine = jnp.stack([owned_by(0)] + [by_col(owned_by(flip), 2 * flip) for flip in range(1, chips)])
    other = by_col(mine, 1)
    early = attend_early(mine, *start[:3])
    return attend(mine, other, early, start, ln_gain, ln_shift, w_proj, gate_bias, w_out, out_bias)


def solution(mesh):
    return jax.shard_map(
        body,
        mesh=mesh,
        in_specs=(P(("row", "col"), None, None), P(), P(), P(), P(), P(), P(), P(), P()),
        out_specs=(P(("row", "col"), None, None), P(("row", "col"), None, None)),
        check_vma=False,
    )
```

```python
import functools

import jax
import jax.numpy as jnp
from jax import lax
from jax.experimental import pallas as pl
from jax.experimental.pallas import tpu as pltpu
from jax.sharding import PartitionSpec as P

WD = 2
EPS = 1e-05
MASKED = -1000000000.0
CHUNK = 256
VMEM = pl.BlockSpec(memory_space=pltpu.VMEM)
HBM = pl.BlockSpec(memory_space=pltpu.HBM)


def params(megabytes):
    return pltpu.CompilerParams(vmem_limit_bytes=megabytes * 1024 * 1024)


def for_each(count, step, unrolled):
    if unrolled:
        for index in range(count):
            step(index)
    else:
        lax.fori_loop(0, count, lambda index, carry: (step(index), carry)[1], 0)


def standardize_all(lines):
    centers = [jnp.mean(wide, -1, keepdims=True) for wide in lines]
    aways = [wide - center for wide, center in zip(lines, centers)]
    spreads = [jnp.mean(jnp.square(away), -1, keepdims=True) for away in aways]
    return [away * lax.rsqrt(spread + EPS) for away, spread in zip(aways, spreads)]


def contract(left, right, left_dim, right_dim):
    return lax.dot_general(
        left, right, (((left_dim,), (right_dim,)), ((), ())), preferred_element_type=jnp.float32
    )


def flipped(index, flip):
    bit = 1
    while bit <= flip:
        if flip & bit:
            index = index + bit - 2 * bit * lax.rem(lax.div(index, bit), 2)
        bit *= 2
    return index


def bias_kernel(along, chips, pair_hbm, live_hbm, gain_hbm, shift_hbm, weight_hbm, *rest):
    outs = rest[:along]
    pair, live_row, gain, shift, weight, blocks, rows_out, wide, picked, sems = rest[along:]
    rows, length, channels = pair.shape
    heads = weight.shape[1]
    lanes = outs[0].shape[1]
    copies = [
        pltpu.make_async_copy(source, target, sems.at[i])
        for i, (source, target) in enumerate(
            ((pair_hbm, pair), (live_hbm, live_row), (gain_hbm, gain), (shift_hbm, shift), (weight_hbm, weight))
        )
    ]
    for copy in copies:
        copy.start()
    device = lax.axis_index("row") * lax.axis_size("col") + lax.axis_index("col")
    for copy in copies:
        copy.wait()
    blocks[...] = jnp.zeros_like(blocks)
    for p in range(2):
        at = slice(p * heads, (p + 1) * heads)
        blocks[at, p * channels : (p + 1) * channels] = weight[p].astype(jnp.float32)
    paired = blocks[: 2 * heads].astype(jnp.bfloat16)
    live = jnp.broadcast_to(live_row[...], (2 * heads, length)).astype(jnp.float32)
    first = lax.broadcasted_iota(jnp.int32, live.shape, 0) < heads
    token = lax.broadcasted_iota(jnp.int32, (rows, length), 1)
    mine = device * rows + lax.broadcasted_iota(jnp.int32, (rows, length), 0)
    here = jnp.where(token == mine, live_row[...], 0).astype(jnp.float32)
    here = jnp.sum(here, 1, keepdims=True)
    lines = [pair[a].astype(jnp.float32) for a in range(rows)]
    for a, x in enumerate(lines):
        wide[a] = x
    lines = standardize_all(lines)
    normed = [
        jnp.concatenate(
            [(z * gain[p : p + 1, :] + shift[p : p + 1, :]).astype(jnp.bfloat16) for p in range(2)], 1
        )
        for z in lines
    ]
    biases = [contract(paired, line, 1, 1) for line in normed]
    devices = length // rows
    for a in range(rows):
        for w in range(WD):
            column = wide[a, pl.ds(w, devices, stride=rows), :]
            picked[pl.ds(w * rows + a, devices, stride=WD * rows), :] = column
    for a, bias in enumerate(biases):
        kept = jnp.where(first, live, here[a : a + 1])
        bias = jnp.where(kept > 0, bias, MASKED)
        for lane in range(length // lanes):
            part = bias[:, lane * lanes : (lane + 1) * lanes]
            rows_out[pl.ds(2 * lane * heads * rows + a, 2 * heads, stride=rows), :] = part
    chip = lax.div(lax.axis_index("col"), 2)
    both = 2 * WD * rows
    packed = rows_out.shape[0]
    sent = rows_out[...].astype(jnp.bfloat16)
    for shift_by, out in enumerate(outs):
        out[:packed] = sent
        row = flipped(lax.axis_index("row"), shift_by)
        for flip in range(chips):
            at = pl.multiple_of((row * chips + flipped(chip, flip)) * both, both)
            out[packed + flip * both : packed + (flip + 1) * both] = picked[pl.ds(at, both), :].astype(jnp.bfloat16)


def local_bias(pair, live, gain, shift, weight, along, chips):
    rows, length, channels = pair.shape
    heads = weight.shape[1]
    packed = 2 * heads * rows * (length // channels)
    sent = jax.ShapeDtypeStruct((packed + chips * 2 * WD * rows, channels), jnp.bfloat16)
    return pl.pallas_call(
        functools.partial(bias_kernel, along, chips),
        out_shape=(sent,) * along,
        in_specs=[HBM] * 5,
        out_specs=(VMEM,) * along,
        scratch_shapes=[
            pltpu.VMEM(pair.shape, pair.dtype),
            pltpu.VMEM(live.shape, live.dtype),
            pltpu.VMEM(gain.shape, gain.dtype),
            pltpu.VMEM(shift.shape, shift.dtype),
            pltpu.VMEM(weight.shape, weight.dtype),
            pltpu.VMEM((4 * heads, 2 * channels), jnp.float32),
            pltpu.VMEM((packed, channels), jnp.float32),
            pltpu.VMEM(pair.shape, jnp.float32),
            pltpu.VMEM((length * WD, channels), jnp.float32),
            pltpu.SemaphoreType.DMA((5,)),
        ],
        compiler_params=params(60),
        name="bias",
    )(pair, live, gain, shift, weight)


def turned(row):
    return jnp.broadcast_to(row, (row.shape[1], row.shape[1])).T[:, :1]


def turned_over(index, bit):
    return lax.rem(lax.div(index, bit), 2) == 1


def exchanged(grid, row, col):
    along, cols = len(grid), len(grid[0])
    bit = 1
    while bit < cols:
        swap = turned_over(col, bit)
        grid = [[jnp.where(swap, line[c ^ bit], line[c]) for c in range(cols)] for line in grid]
        bit *= 2
    bit = 1
    while bit < along:
        swap = turned_over(row, bit)
        grid = [[jnp.where(swap, grid[r ^ bit][c], grid[r][c]) for c in range(cols)] for r in range(along)]
        bit *= 2
    return grid


def to_relative(x, along, chips, rows):
    cols = 2 * chips
    grid = [[x[(r * cols + c) * rows : (r * cols + c + 1) * rows] for c in range(cols)] for r in range(along)]
    grid = exchanged(grid, lax.axis_index("row"), lax.axis_index("col"))
    return jnp.concatenate(
        [grid[s][2 * flip + other] for other in range(2) for flip in range(chips) for s in reversed(range(along))], 0
    )


def to_devices(x, along, chips, rows):
    at = lambda c, s: (((c % 2) * chips + c // 2) * along + along - 1 - s) * rows
    grid = [[x[at(c, s) : at(c, s) + rows] for c in range(2 * chips)] for s in range(along)]
    grid = exchanged(grid, lax.axis_index("row"), lax.axis_index("col"))
    return jnp.concatenate([block for line in grid for block in line], 0)


def queries_and_gates(lines, scale, weight, offset, q_ref, g_ref):
    inner = weight.shape[1] // 4
    queries = [contract(weight[:, :inner], normed, 0, 1) for normed in lines]
    gates = [contract(weight[:, 3 * inner :], normed, 0, 1) for normed in lines]
    for w in range(WD):
        q_ref[w] = (queries[w] * scale).astype(jnp.bfloat16)
        g_ref[w] = jax.nn.sigmoid(gates[w] + offset)


def keys_and_values(lines, weight, k_ref, v_ref):
    _, heads, _, size = k_ref.shape
    inner = heads * size
    for h in range(heads):
        at = inner + h * size
        keys = [contract(normed, weight[:, at : at + size], 1, 0) for normed in lines]
        for w in range(WD):
            k_ref[w, h] = keys[w].astype(jnp.bfloat16)
    values = [contract(weight[:, 2 * inner : 3 * inner], normed, 0, 1) for normed in lines]
    for w in range(WD):
        v_ref[w] = values[w].astype(jnp.bfloat16)


def lines_kernel(along, chips, lines_ref, gain_ref, shift_ref, weight_ref, offset_ref, q_ref, k_ref, v_ref, g_ref):
    size = k_ref.shape[-1]
    rows = lines_ref.shape[1] // (2 * chips * along)
    offset = turned(offset_ref[0:1, :])
    weight = weight_ref[0]
    lines = standardize_all([lines_ref[w].astype(jnp.float32) for w in range(WD)])
    lines = [line * gain_ref[0:1, :] + shift_ref[0:1, :] for line in lines]
    keys_and_values([line.astype(jnp.bfloat16) for line in lines], weight, k_ref, v_ref)
    near = [to_relative(line, along, chips, rows).astype(jnp.bfloat16) for line in lines]
    queries_and_gates(near, size ** (-0.5), weight, offset, q_ref, g_ref)


def projected(length, inner, heads):
    wide = (WD, inner, length)
    return (
        (wide, jnp.bfloat16),
        ((WD, heads, length, inner // heads), jnp.bfloat16),
        (wide, jnp.bfloat16),
        (wide, jnp.float32),
    )


def local_lines(pair, gain, shift, weight, offset, heads, along, chips):
    _, length, channels = pair.shape
    wide = weight.shape[2]
    shapes = projected(length, wide // 4, heads)
    whole = lambda shape: pl.BlockSpec(shape, lambda i: (0,) * len(shape))
    return pl.pallas_call(
        functools.partial(lines_kernel, along, chips),
        grid=(1,),
        out_shape=tuple(jax.ShapeDtypeStruct(shape, dtype) for shape, dtype in shapes),
        in_specs=[
            whole((WD, length, channels)), whole(gain.shape), whole(gain.shape),
            whole((1, channels, wide)), whole(gain.shape),
        ],
        out_specs=tuple(whole(shape) for shape, _ in shapes),
        compiler_params=params(8 + length // 32),
        cost_estimate=pl.CostEstimate(
            flops=2 * WD * length * channels * wide, bytes_accessed=4 * WD * length * wide, transcendentals=0
        ),
        name="lines",
    )(pair, gain, shift, weight, offset)


def unpack(source, p, pack, rows, heads, turn, into, at):
    chips, along, _, lanes = source.shape
    packed = 2 * heads * rows
    half = chips * along * rows
    slots = into.shape[0]
    for lane in range(into.shape[2 - turn] // lanes):
        first = lane * packed + (p * heads + 2 * pack) * rows
        both = [
            source[flip, shift, first : first + 2 * rows, :].astype(jnp.float32)
            for flip in range(chips)
            for shift in range(along)
        ]
        there = slice(lane * lanes, (lane + 1) * lanes)
        for i in range(2):
            slot = (2 * pack + i) % slots
            block = jnp.concatenate([part[i * rows : (i + 1) * rows] for part in both], 0)
            if turn:
                into[slot, there, at : at + half] = block.T
            else:
                into[slot, at : at + half, there] = block


def score(units):
    return [contract(key, query, 1, 0) + added for key, query, added, _ in units]


def mix(units, scores):
    tops = [jnp.max(part, 0, keepdims=True) for part in scores]
    expos = [jnp.exp(part - top) for part, top in zip(scores, tops)]
    shares = [1.0 / jnp.sum(expo, 0, keepdims=True) for expo in expos]
    weights = [(expo * share).astype(jnp.bfloat16) for expo, share in zip(expos, shares)]
    return [contract(unit[3], weight, 1, 0) for unit, weight in zip(units, weights)]


def attend_groups(groups):
    if not groups:
        return
    ready = score(groups[0][0]())
    for i, (units, put) in enumerate(groups):
        ahead = score(groups[i + 1][0]()) if i + 1 < len(groups) else None
        put(mix(units(), ready))
        ready = ahead


def head_group(heads, size, q, k, v, bias, mixed, there, near):
    def units():
        return [
            (k[w, h], q[w, h * size : (h + 1) * size, there], bias[h % bias.shape[0], :, near],
             v[w, h * size : (h + 1) * size, :])
            for h in heads
            for w in range(WD)
        ]

    def put(outs):
        for i, h in enumerate(heads):
            for w in range(WD):
                mixed[w, h * size : (h + 1) * size, near] = outs[i * WD + w]

    return units, put


def start_half(source, other, q, k, v, mixed, bias):
    _, heads, length, size = k.shape
    half = length // 2
    rows = half // (source.shape[0] * source.shape[1])
    width = min(half, CHUNK)
    if half == width:
        groups = []
        for pack in range(heads // 2):
            unpack(source, 0, pack, rows, heads, 1, bias, 0)
            groups.append(
                head_group(
                    (2 * pack, 2 * pack + 1), size, q, k, v, bias, mixed,
                    pl.ds(other * half, half), pl.ds(0, half),
                )
            )
        return groups
    for pack in range(heads // 2):
        unpack(source, 0, pack, rows, heads, 1, bias, 0)

        def step(chunk):
            near = pl.ds(pl.multiple_of(chunk * width, width), width)
            there = pl.ds(pl.multiple_of(other * half + chunk * width, width), width)
            for h in (2 * pack, 2 * pack + 1):
                attend_groups([head_group((h,), size, q, k, v, bias, mixed, there, near)])

        for_each(half // width, step, False)
    return []


def early_kernel(mine_ref, q, k, v, mixed, bias):
    attend_groups(start_half(mine_ref, 0, q, k, v, mixed, bias))


def attend_early(mine, q, k, v):
    _, heads, length, size = k.shape
    return pl.pallas_call(
        early_kernel,
        out_shape=jax.ShapeDtypeStruct((WD, heads * size, length // 2), jnp.float32),
        in_specs=[VMEM] * 4,
        out_specs=VMEM,
        scratch_shapes=[pltpu.VMEM((heads if length <= CHUNK else 2, length, length // 2), jnp.float32)],
        compiler_params=params(8 if length <= CHUNK else 40),
        cost_estimate=pl.CostEstimate(
            flops=4 * WD * heads * size * length * length,
            bytes_accessed=4 * WD * heads * length * length,
            transcendentals=WD * heads * length * length // 2,
        ),
        name="early",
    )(mine, q, k, v)


def attend_kernel(
    mine_ref, other_ref, early_ref, q0, k0, v0, g0,
    gain_ref, shift_ref, proj_ref, gate_ref, weight_ref, offset_ref,
    out0, out1, turned_bias, bias, late, mixed, kept, sem, q1, k1, v1, g1,
):
    chips, along, _, _ = mine_ref.shape
    _, heads, length, size = k0.shape
    half = length // 2
    rows = half // (chips * along)
    packed = 2 * heads * rows * (length // mine_ref.shape[3])
    first = pl.multiple_of(packed + lax.rem(lax.axis_index("col"), 2) * WD * rows, WD * rows)
    attend_groups(start_half(other_ref, 1, q0, k0, v0, late, turned_bias))
    gated = [
        (jnp.concatenate([early_ref[w], late[w]], 1) * g0[w]).astype(jnp.bfloat16) for w in range(WD)
    ]
    full = [contract(line, weight_ref[0], 0, 0) + offset_ref[0:1, :] for line in gated]
    for w in range(WD):
        kept[w] = to_devices(full[w], along, chips, rows).astype(jnp.bfloat16)
    leaving = pltpu.make_async_copy(kept, out0, sem)
    leaving.start()
    groups = []
    offset = turned(gate_ref[1:2, :])
    blocks = []
    for source in (mine_ref, other_ref):
        for flip in range(chips):
            for shift in range(along):
                both = source[flip, shift, pl.ds(first, WD * rows), :].astype(jnp.float32)
                blocks.append(both.reshape(WD, rows, -1))
    lines = standardize_all([jnp.concatenate([block[w] for block in blocks], 0) for w in range(WD)])
    lines = [line * gain_ref[1:2, :] + shift_ref[1:2, :] for line in lines]
    keys_and_values([line.astype(jnp.bfloat16) for line in lines], proj_ref[1], k1, v1)
    ordered = [to_devices(line, along, chips, rows).astype(jnp.bfloat16) for line in lines]
    queries_and_gates(ordered, size ** (-0.5), proj_ref[1], offset, q1, g1)
    for pack in range(heads // 2):
        unpack(mine_ref, 1, pack, rows, heads, 0, bias, 0)
        unpack(other_ref, 1, pack, rows, heads, 0, bias, half)
        pair = (2 * pack, 2 * pack + 1)
        if length == CHUNK:
            groups.append(
                head_group(pair, size, q1, k1, v1, bias, mixed, pl.ds(0, length), pl.ds(0, length))
            )
            continue

        def step(chunk):
            there = pl.ds(pl.multiple_of(chunk * CHUNK, CHUNK), CHUNK)
            for h in pair:
                attend_groups([head_group((h,), size, q1, k1, v1, bias, mixed, there, there)])

        for_each(length // CHUNK, step, False)
    attend_groups(groups)
    gated = [(mixed[w] * g1[w]).astype(jnp.bfloat16) for w in range(WD)]
    full = [contract(line, weight_ref[1], 0, 0) + offset_ref[1:2, :] for line in gated]
    for w in range(WD):
        out1[w] = full[w].astype(jnp.bfloat16)
    leaving.wait()


def attend(mine, other, early, start, gain, shift, proj, gate, weight, offset):
    _, heads, length, size = start[1].shape
    inner, channels = weight.shape[1:]
    result = jax.ShapeDtypeStruct((WD, length, channels), jnp.bfloat16)
    slots = heads if length <= CHUNK else 2
    return pl.pallas_call(
        attend_kernel,
        out_shape=(result, result),
        in_specs=[VMEM] * 13,
        out_specs=(HBM, VMEM),
        scratch_shapes=[
            pltpu.VMEM((slots, length, length // 2), jnp.float32),
            pltpu.VMEM((slots, length, length), jnp.float32),
            pltpu.VMEM((WD, inner, length // 2), jnp.float32),
            pltpu.VMEM((WD, inner, length), jnp.float32),
            pltpu.VMEM((WD, length, channels), jnp.bfloat16),
            pltpu.SemaphoreType.DMA(()),
        ]
        + [pltpu.VMEM(shape, dtype) for shape, dtype in projected(length, inner, heads)],
        compiler_params=params(16 if length <= CHUNK else 60),
        name="attend",
    )(mine, other, early, *start, gain, shift, proj, gate, weight, offset)


def body(pair, residue_mask, ln_gain, ln_shift, w_proj, w_bias, gate_bias, w_out, out_bias):
    rows, length, channels = pair.shape
    heads = w_bias.shape[2]
    along, cols = lax.axis_size("row"), lax.axis_size("col")
    chips = cols // 2

    def by_row(block, shift):
        return lax.ppermute(block, "row", [(i, i ^ shift) for i in range(along)])

    def by_col(block, flip):
        return lax.ppermute(block, "col", [(i, i ^ flip) for i in range(cols)])

    sent = local_bias(
        pair, residue_mask[None, :], ln_gain, ln_shift, jnp.transpose(w_bias, (0, 2, 1)), along, chips
    )
    far_first = [by_row(sent[flip], flip) for flip in reversed(range(1, along))]
    line = jnp.stack(far_first + [sent[0]])
    start = local_lines(pair, ln_gain, ln_shift, w_proj, gate_bias, heads, along, chips)
    line, _ = lax.optimization_barrier((line, start))
    packed = 2 * heads * rows * (length // channels)
    both = 2 * WD * rows

    def owned_by(flip):
        at = packed + flip * both
        return jnp.concatenate([line[:, :packed], line[:, at : at + both]], 1)

    mine = jnp.stack([owned_by(0)] + [by_col(owned_by(flip), 2 * flip) for flip in range(1, chips)])
    other = by_col(mine, 1)
    early = attend_early(mine, *start[:3])
    return attend(mine, other, early, start, ln_gain, ln_shift, w_proj, gate_bias, w_out, out_bias)


def solution(mesh):
    return jax.shard_map(
        body,
        mesh=mesh,
        in_specs=(P(("row", "col"), None, None), P(), P(), P(), P(), P(), P(), P(), P()),
        out_specs=(P(("row", "col"), None, None), P(("row", "col"), None, None)),
        check_vma=False,
    )
```

```python
import functools

import jax
import jax.numpy as jnp
from jax import lax
from jax.experimental import pallas as pl
from jax.experimental.pallas import tpu as pltpu
from jax.sharding import PartitionSpec as P

WD = 2
EPS = 1e-05
MASKED = -1000000000.0
CHUNK = 256
VMEM = pl.BlockSpec(memory_space=pltpu.VMEM)
HBM = pl.BlockSpec(memory_space=pltpu.HBM)


def params(megabytes):
    return pltpu.CompilerParams(vmem_limit_bytes=megabytes * 1024 * 1024)


def for_each(count, step, unrolled):
    if unrolled:
        for index in range(count):
            step(index)
    else:
        lax.fori_loop(0, count, lambda index, carry: (step(index), carry)[1], 0)


def standardize_all(lines):
    centers = [jnp.mean(wide, -1, keepdims=True) for wide in lines]
    aways = [wide - center for wide, center in zip(lines, centers)]
    spreads = [jnp.mean(jnp.square(away), -1, keepdims=True) for away in aways]
    return [away * lax.rsqrt(spread + EPS) for away, spread in zip(aways, spreads)]


def contract(left, right, left_dim, right_dim):
    return lax.dot_general(
        left, right, (((left_dim,), (right_dim,)), ((), ())), preferred_element_type=jnp.float32
    )


def flipped(index, flip):
    bit = 1
    while bit <= flip:
        if flip & bit:
            index = index + bit - 2 * bit * lax.rem(lax.div(index, bit), 2)
        bit *= 2
    return index


def bias_kernel(along, chips, pair_hbm, live_hbm, gain_hbm, shift_hbm, weight_hbm, *rest):
    outs = rest[:along]
    pair, live_row, gain, shift, weight, blocks, rows_out, wide, picked, sems = rest[along:]
    rows, length, channels = pair.shape
    heads = weight.shape[1]
    lanes = outs[0].shape[1]
    copies = [
        pltpu.make_async_copy(source, target, sems.at[i])
        for i, (source, target) in enumerate(
            ((pair_hbm, pair), (live_hbm, live_row), (gain_hbm, gain), (shift_hbm, shift), (weight_hbm, weight))
        )
    ]
    for copy in copies:
        copy.start()
    device = lax.axis_index("row") * lax.axis_size("col") + lax.axis_index("col")
    for copy in copies:
        copy.wait()
    blocks[...] = jnp.zeros_like(blocks)
    for p in range(2):
        at = slice(p * heads, (p + 1) * heads)
        blocks[at, p * channels : (p + 1) * channels] = weight[p].astype(jnp.float32)
    paired = blocks[: 2 * heads].astype(jnp.bfloat16)
    live = jnp.broadcast_to(live_row[...], (2 * heads, length)).astype(jnp.float32)
    first = lax.broadcasted_iota(jnp.int32, live.shape, 0) < heads
    token = lax.broadcasted_iota(jnp.int32, (rows, length), 1)
    mine = device * rows + lax.broadcasted_iota(jnp.int32, (rows, length), 0)
    here = jnp.where(token == mine, live_row[...], 0).astype(jnp.float32)
    here = jnp.sum(here, 1, keepdims=True)
    lines = [pair[a].astype(jnp.float32) for a in range(rows)]
    for a, x in enumerate(lines):
        wide[a] = x
    lines = standardize_all(lines)
    normed = [
        jnp.concatenate(
            [(z * gain[p : p + 1, :] + shift[p : p + 1, :]).astype(jnp.bfloat16) for p in range(2)], 1
        )
        for z in lines
    ]
    biases = [contract(paired, line, 1, 1) for line in normed]
    devices = length // rows
    for a in range(rows):
        for w in range(WD):
            column = wide[a, pl.ds(w, devices, stride=rows), :]
            picked[pl.ds(w * rows + a, devices, stride=WD * rows), :] = column
    for a, bias in enumerate(biases):
        kept = jnp.where(first, live, here[a : a + 1])
        bias = jnp.where(kept > 0, bias, MASKED)
        for lane in range(length // lanes):
            part = bias[:, lane * lanes : (lane + 1) * lanes]
            rows_out[pl.ds(2 * lane * heads * rows + a, 2 * heads, stride=rows), :] = part
    chip = lax.div(lax.axis_index("col"), 2)
    both = 2 * WD * rows
    packed = rows_out.shape[0]
    sent = rows_out[...].astype(jnp.bfloat16)
    for shift_by, out in enumerate(outs):
        out[:packed] = sent
        row = flipped(lax.axis_index("row"), shift_by)
        for flip in range(chips):
            at = pl.multiple_of((row * chips + flipped(chip, flip)) * both, both)
            out[packed + flip * both : packed + (flip + 1) * both] = picked[pl.ds(at, both), :].astype(jnp.bfloat16)


def local_bias(pair, live, gain, shift, weight, along, chips):
    rows, length, channels = pair.shape
    heads = weight.shape[1]
    packed = 2 * heads * rows * (length // channels)
    sent = jax.ShapeDtypeStruct((packed + chips * 2 * WD * rows, channels), jnp.bfloat16)
    return pl.pallas_call(
        functools.partial(bias_kernel, along, chips),
        out_shape=(sent,) * along,
        in_specs=[HBM] * 5,
        out_specs=(VMEM,) * along,
        scratch_shapes=[
            pltpu.VMEM(pair.shape, pair.dtype),
            pltpu.VMEM(live.shape, live.dtype),
            pltpu.VMEM(gain.shape, gain.dtype),
            pltpu.VMEM(shift.shape, shift.dtype),
            pltpu.VMEM(weight.shape, weight.dtype),
            pltpu.VMEM((4 * heads, 2 * channels), jnp.float32),
            pltpu.VMEM((packed, channels), jnp.float32),
            pltpu.VMEM(pair.shape, jnp.float32),
            pltpu.VMEM((length * WD, channels), jnp.float32),
            pltpu.SemaphoreType.DMA((5,)),
        ],
        compiler_params=params(60),
        name="bias",
    )(pair, live, gain, shift, weight)


def turned(row):
    return jnp.broadcast_to(row, (row.shape[1], row.shape[1])).T[:, :1]


def turned_over(index, bit):
    return lax.rem(lax.div(index, bit), 2) == 1


def exchanged(grid, row, col):
    along, cols = len(grid), len(grid[0])
    bit = 1
    while bit < cols:
        swap = turned_over(col, bit)
        grid = [[jnp.where(swap, line[c ^ bit], line[c]) for c in range(cols)] for line in grid]
        bit *= 2
    bit = 1
    while bit < along:
        swap = turned_over(row, bit)
        grid = [[jnp.where(swap, grid[r ^ bit][c], grid[r][c]) for c in range(cols)] for r in range(along)]
        bit *= 2
    return grid


def to_relative(x, along, chips, rows):
    cols = 2 * chips
    grid = [[x[(r * cols + c) * rows : (r * cols + c + 1) * rows] for c in range(cols)] for r in range(along)]
    grid = exchanged(grid, lax.axis_index("row"), lax.axis_index("col"))
    return jnp.concatenate(
        [grid[s][2 * flip + other] for other in range(2) for flip in range(chips) for s in reversed(range(along))], 0
    )


def to_devices(x, along, chips, rows):
    at = lambda c, s: (((c % 2) * chips + c // 2) * along + along - 1 - s) * rows
    grid = [[x[at(c, s) : at(c, s) + rows] for c in range(2 * chips)] for s in range(along)]
    grid = exchanged(grid, lax.axis_index("row"), lax.axis_index("col"))
    return jnp.concatenate([block for line in grid for block in line], 0)


def queries_and_gates(lines, scale, weight, offset, q_ref, g_ref):
    inner = weight.shape[1] // 4
    queries = [contract(weight[:, :inner], normed, 0, 1) for normed in lines]
    gates = [contract(weight[:, 3 * inner :], normed, 0, 1) for normed in lines]
    for w in range(WD):
        q_ref[w] = (queries[w] * scale).astype(jnp.bfloat16)
        g_ref[w] = jax.nn.sigmoid(gates[w] + offset)


def keys_and_values(lines, weight, k_ref, v_ref):
    _, heads, _, size = k_ref.shape
    inner = heads * size
    for h in range(heads):
        at = inner + h * size
        keys = [contract(normed, weight[:, at : at + size], 1, 0) for normed in lines]
        for w in range(WD):
            k_ref[w, h] = keys[w].astype(jnp.bfloat16)
    values = [contract(weight[:, 2 * inner : 3 * inner], normed, 0, 1) for normed in lines]
    for w in range(WD):
        v_ref[w] = values[w].astype(jnp.bfloat16)


def lines_kernel(along, chips, lines_ref, gain_ref, shift_ref, weight_ref, offset_ref, q_ref, k_ref, v_ref, g_ref):
    size = k_ref.shape[-1]
    rows = lines_ref.shape[1] // (2 * chips * along)
    offset = turned(offset_ref[0:1, :])
    weight = weight_ref[0]
    lines = standardize_all([lines_ref[w].astype(jnp.float32) for w in range(WD)])
    lines = [line * gain_ref[0:1, :] + shift_ref[0:1, :] for line in lines]
    keys_and_values([line.astype(jnp.bfloat16) for line in lines], weight, k_ref, v_ref)
    near = [to_relative(line, along, chips, rows).astype(jnp.bfloat16) for line in lines]
    queries_and_gates(near, size ** (-0.5), weight, offset, q_ref, g_ref)


def projected(length, inner, heads):
    wide = (WD, inner, length)
    return (
        (wide, jnp.bfloat16),
        ((WD, heads, length, inner // heads), jnp.bfloat16),
        (wide, jnp.bfloat16),
        (wide, jnp.float32),
    )


def local_lines(pair, gain, shift, weight, offset, heads, along, chips):
    _, length, channels = pair.shape
    wide = weight.shape[2]
    shapes = projected(length, wide // 4, heads)
    whole = lambda shape: pl.BlockSpec(shape, lambda i: (0,) * len(shape))
    return pl.pallas_call(
        functools.partial(lines_kernel, along, chips),
        grid=(1,),
        out_shape=tuple(jax.ShapeDtypeStruct(shape, dtype) for shape, dtype in shapes),
        in_specs=[
            whole((WD, length, channels)), whole(gain.shape), whole(gain.shape),
            whole((1, channels, wide)), whole(gain.shape),
        ],
        out_specs=tuple(whole(shape) for shape, _ in shapes),
        compiler_params=params(8 + length // 32),
        cost_estimate=pl.CostEstimate(
            flops=2 * WD * length * channels * wide, bytes_accessed=4 * WD * length * wide, transcendentals=0
        ),
        name="lines",
    )(pair, gain, shift, weight, offset)


def unpack(source, p, pack, rows, heads, turn, into, at):
    chips, along, _, lanes = source.shape
    packed = 2 * heads * rows
    half = chips * along * rows
    slots = into.shape[0]
    for lane in range(into.shape[2 - turn] // lanes):
        first = lane * packed + (p * heads + 2 * pack) * rows
        both = [
            source[flip, shift, first : first + 2 * rows, :].astype(jnp.float32)
            for flip in range(chips)
            for shift in range(along)
        ]
        there = slice(lane * lanes, (lane + 1) * lanes)
        for i in range(2):
            slot = (2 * pack + i) % slots
            block = jnp.concatenate([part[i * rows : (i + 1) * rows] for part in both], 0)
            if turn:
                into[slot, there, at : at + half] = block.T
            else:
                into[slot, at : at + half, there] = block


def stages(units, put):
    return (
        lambda _: [contract(key, query, 1, 0) + added for key, query, added, _ in units()],
        lambda scores: [(part, jnp.max(part, 0, keepdims=True)) for part in scores],
        lambda pairs: [jnp.exp(part - top) for part, top in pairs],
        lambda expos: [(expo, 1.0 / jnp.sum(expo, 0, keepdims=True)) for expo in expos],
        lambda pairs: [(expo * share).astype(jnp.bfloat16) for expo, share in pairs],
        lambda weights: put(
            [contract(unit[3], weight, 1, 0) for unit, weight in zip(units(), weights)]
        ),
    )


def attend_groups(groups):
    steps = [stages(*group) for group in groups]
    held = [None] * len(groups)
    for t in range(len(groups) + 5 if groups else 0):
        for g in range(len(groups)):
            if 0 <= t - g < 6:
                held[g] = steps[g][t - g](held[g])


def head_group(heads, size, q, k, v, bias, mixed, there, near):
    def units():
        return [
            (k[w, h], q[w, h * size : (h + 1) * size, there], bias[h % bias.shape[0], :, near],
             v[w, h * size : (h + 1) * size, :])
            for h in heads
            for w in range(WD)
        ]

    def put(outs):
        for i, h in enumerate(heads):
            for w in range(WD):
                mixed[w, h * size : (h + 1) * size, near] = outs[i * WD + w]

    return units, put


def start_half(source, other, q, k, v, mixed, bias):
    _, heads, length, size = k.shape
    half = length // 2
    rows = half // (source.shape[0] * source.shape[1])
    width = min(half, CHUNK)
    if half == width:
        groups = []
        for pack in range(heads // 2):
            unpack(source, 0, pack, rows, heads, 1, bias, 0)
            for h in (2 * pack, 2 * pack + 1):
                groups.append(
                    head_group((h,), size, q, k, v, bias, mixed, pl.ds(other * half, half), pl.ds(0, half))
                )
        return groups
    for pack in range(heads // 2):
        unpack(source, 0, pack, rows, heads, 1, bias, 0)

        def step(chunk):
            near = pl.ds(pl.multiple_of(chunk * width, width), width)
            there = pl.ds(pl.multiple_of(other * half + chunk * width, width), width)
            for h in (2 * pack, 2 * pack + 1):
                attend_groups([head_group((h,), size, q, k, v, bias, mixed, there, near)])

        for_each(half // width, step, False)
    return []


def early_kernel(mine_ref, q, k, v, mixed, bias):
    attend_groups(start_half(mine_ref, 0, q, k, v, mixed, bias))


def attend_early(mine, q, k, v):
    _, heads, length, size = k.shape
    return pl.pallas_call(
        early_kernel,
        out_shape=jax.ShapeDtypeStruct((WD, heads * size, length // 2), jnp.float32),
        in_specs=[VMEM] * 4,
        out_specs=VMEM,
        scratch_shapes=[pltpu.VMEM((heads if length <= CHUNK else 2, length, length // 2), jnp.float32)],
        compiler_params=params(8 if length <= CHUNK else 40),
        cost_estimate=pl.CostEstimate(
            flops=4 * WD * heads * size * length * length,
            bytes_accessed=4 * WD * heads * length * length,
            transcendentals=WD * heads * length * length // 2,
        ),
        name="early",
    )(mine, q, k, v)


def attend_kernel(
    mine_ref, other_ref, early_ref, q0, k0, v0, g0,
    gain_ref, shift_ref, proj_ref, gate_ref, weight_ref, offset_ref,
    out0, out1, turned_bias, bias, late, mixed, q1, k1, v1, g1,
):
    chips, along, _, _ = mine_ref.shape
    _, heads, length, size = k0.shape
    half = length // 2
    rows = half // (chips * along)
    packed = 2 * heads * rows * (length // mine_ref.shape[3])
    first = pl.multiple_of(packed + lax.rem(lax.axis_index("col"), 2) * WD * rows, WD * rows)
    groups = start_half(other_ref, 1, q0, k0, v0, late, turned_bias)
    offset = turned(gate_ref[1:2, :])
    blocks = []
    for source in (mine_ref, other_ref):
        for flip in range(chips):
            for shift in range(along):
                both = source[flip, shift, pl.ds(first, WD * rows), :].astype(jnp.float32)
                blocks.append(both.reshape(WD, rows, -1))
    lines = standardize_all([jnp.concatenate([block[w] for block in blocks], 0) for w in range(WD)])
    lines = [line * gain_ref[1:2, :] + shift_ref[1:2, :] for line in lines]
    keys_and_values([line.astype(jnp.bfloat16) for line in lines], proj_ref[1], k1, v1)
    ordered = [to_devices(line, along, chips, rows).astype(jnp.bfloat16) for line in lines]
    queries_and_gates(ordered, size ** (-0.5), proj_ref[1], offset, q1, g1)
    for pack in range(heads // 2):
        unpack(mine_ref, 1, pack, rows, heads, 0, bias, 0)
        unpack(other_ref, 1, pack, rows, heads, 0, bias, half)
        pair = (2 * pack, 2 * pack + 1)
        if length == CHUNK:
            for h in pair:
                groups.append(
                    head_group((h,), size, q1, k1, v1, bias, mixed, pl.ds(0, length), pl.ds(0, length))
                )
            continue

        def step(chunk):
            there = pl.ds(pl.multiple_of(chunk * CHUNK, CHUNK), CHUNK)
            for h in pair:
                attend_groups([head_group((h,), size, q1, k1, v1, bias, mixed, there, there)])

        for_each(length // CHUNK, step, False)
    attend_groups(groups)
    for w in range(WD):
        gated = (jnp.concatenate([early_ref[w], late[w]], 1) * g0[w]).astype(jnp.bfloat16)
        full = contract(gated, weight_ref[0], 0, 0) + offset_ref[0:1, :]
        out0[w] = to_devices(full, along, chips, rows).astype(jnp.bfloat16)
    for w in range(WD):
        gated = (mixed[w] * g1[w]).astype(jnp.bfloat16)
        full = contract(gated, weight_ref[1], 0, 0) + offset_ref[1:2, :]
        out1[w] = full.astype(jnp.bfloat16)


def attend(mine, other, early, start, gain, shift, proj, gate, weight, offset):
    _, heads, length, size = start[1].shape
    inner, channels = weight.shape[1:]
    result = jax.ShapeDtypeStruct((WD, length, channels), jnp.bfloat16)
    slots = heads if length <= CHUNK else 2
    return pl.pallas_call(
        attend_kernel,
        out_shape=(result, result),
        in_specs=[VMEM] * 13,
        out_specs=(VMEM, VMEM),
        scratch_shapes=[
            pltpu.VMEM((slots, length, length // 2), jnp.float32),
            pltpu.VMEM((slots, length, length), jnp.float32),
            pltpu.VMEM((WD, inner, length // 2), jnp.float32),
            pltpu.VMEM((WD, inner, length), jnp.float32),
        ]
        + [pltpu.VMEM(shape, dtype) for shape, dtype in projected(length, inner, heads)],
        compiler_params=params(16 if length <= CHUNK else 60),
        name="attend",
    )(mine, other, early, *start, gain, shift, proj, gate, weight, offset)


def body(pair, residue_mask, ln_gain, ln_shift, w_proj, w_bias, gate_bias, w_out, out_bias):
    rows, length, channels = pair.shape
    heads = w_bias.shape[2]
    along, cols = lax.axis_size("row"), lax.axis_size("col")
    chips = cols // 2

    def by_row(block, shift):
        return lax.ppermute(block, "row", [(i, i ^ shift) for i in range(along)])

    def by_col(block, flip):
        return lax.ppermute(block, "col", [(i, i ^ flip) for i in range(cols)])

    sent = local_bias(
        pair, residue_mask[None, :], ln_gain, ln_shift, jnp.transpose(w_bias, (0, 2, 1)), along, chips
    )
    far_first = [by_row(sent[flip], flip) for flip in reversed(range(1, along))]
    line = jnp.stack(far_first + [sent[0]])
    start = local_lines(pair, ln_gain, ln_shift, w_proj, gate_bias, heads, along, chips)
    line, _ = lax.optimization_barrier((line, start))
    packed = 2 * heads * rows * (length // channels)
    both = 2 * WD * rows

    def owned_by(flip):
        at = packed + flip * both
        return jnp.concatenate([line[:, :packed], line[:, at : at + both]], 1)

    mine = jnp.stack([owned_by(0)] + [by_col(owned_by(flip), 2 * flip) for flip in range(1, chips)])
    other = by_col(mine, 1)
    early = attend_early(mine, *start[:3])
    return attend(mine, other, early, start, ln_gain, ln_shift, w_proj, gate_bias, w_out, out_bias)


def solution(mesh):
    return jax.shard_map(
        body,
        mesh=mesh,
        in_specs=(P(("row", "col"), None, None), P(), P(), P(), P(), P(), P(), P(), P()),
        out_specs=(P(("row", "col"), None, None), P(("row", "col"), None, None)),
        check_vma=False,
    )
```

```python
import functools

import jax
import jax.numpy as jnp
from jax import lax
from jax.experimental import pallas as pl
from jax.experimental.pallas import tpu as pltpu
from jax.sharding import PartitionSpec as P

WD = 2
EPS = 1e-05
MASKED = -1000000000.0
CHUNK = 256
VMEM = pl.BlockSpec(memory_space=pltpu.VMEM)
HBM = pl.BlockSpec(memory_space=pltpu.HBM)


def params(megabytes):
    return pltpu.CompilerParams(vmem_limit_bytes=megabytes * 1024 * 1024)


def for_each(count, step, unrolled):
    if unrolled:
        for index in range(count):
            step(index)
    else:
        lax.fori_loop(0, count, lambda index, carry: (step(index), carry)[1], 0)


def standardize_all(lines):
    centers = [jnp.mean(wide, -1, keepdims=True) for wide in lines]
    aways = [wide - center for wide, center in zip(lines, centers)]
    spreads = [jnp.mean(jnp.square(away), -1, keepdims=True) for away in aways]
    return [away * lax.rsqrt(spread + EPS) for away, spread in zip(aways, spreads)]


def contract(left, right, left_dim, right_dim):
    return lax.dot_general(
        left, right, (((left_dim,), (right_dim,)), ((), ())), preferred_element_type=jnp.float32
    )


def flipped(index, flip):
    bit = 1
    while bit <= flip:
        if flip & bit:
            index = index + bit - 2 * bit * lax.rem(lax.div(index, bit), 2)
        bit *= 2
    return index


def bias_kernel(along, chips, pair_hbm, live_hbm, gain_hbm, shift_hbm, weight_hbm, *rest):
    outs = rest[:along]
    pair, live_row, gain, shift, weight, blocks, rows_out, wide, picked, sems = rest[along:]
    rows, length, channels = pair.shape
    heads = weight.shape[1]
    lanes = outs[0].shape[1]
    copies = [
        pltpu.make_async_copy(source, target, sems.at[i])
        for i, (source, target) in enumerate(
            ((pair_hbm, pair), (live_hbm, live_row), (gain_hbm, gain), (shift_hbm, shift), (weight_hbm, weight))
        )
    ]
    for copy in copies:
        copy.start()
    device = lax.axis_index("row") * lax.axis_size("col") + lax.axis_index("col")
    for copy in copies:
        copy.wait()
    blocks[...] = jnp.zeros_like(blocks)
    for p in range(2):
        at = slice(p * heads, (p + 1) * heads)
        blocks[at, p * channels : (p + 1) * channels] = weight[p].astype(jnp.float32)
    paired = blocks[: 2 * heads].astype(jnp.bfloat16)
    live = jnp.broadcast_to(live_row[...], (2 * heads, length)).astype(jnp.float32)
    first = lax.broadcasted_iota(jnp.int32, live.shape, 0) < heads
    token = lax.broadcasted_iota(jnp.int32, (rows, length), 1)
    mine = device * rows + lax.broadcasted_iota(jnp.int32, (rows, length), 0)
    here = jnp.where(token == mine, live_row[...], 0).astype(jnp.float32)
    here = jnp.sum(here, 1, keepdims=True)
    lines = [pair[a].astype(jnp.float32) for a in range(rows)]
    for a, x in enumerate(lines):
        wide[a] = x
    lines = standardize_all(lines)
    normed = [
        jnp.concatenate(
            [(z * gain[p : p + 1, :] + shift[p : p + 1, :]).astype(jnp.bfloat16) for p in range(2)], 1
        )
        for z in lines
    ]
    biases = [contract(paired, line, 1, 1) for line in normed]
    devices = length // rows
    for a in range(rows):
        for w in range(WD):
            column = wide[a, pl.ds(w, devices, stride=rows), :]
            picked[pl.ds(w * rows + a, devices, stride=WD * rows), :] = column
    for a, bias in enumerate(biases):
        kept = jnp.where(first, live, here[a : a + 1])
        bias = jnp.where(kept > 0, bias, MASKED)
        for lane in range(length // lanes):
            part = bias[:, lane * lanes : (lane + 1) * lanes]
            rows_out[pl.ds(2 * lane * heads * rows + a, 2 * heads, stride=rows), :] = part
    chip = lax.div(lax.axis_index("col"), 2)
    both = 2 * WD * rows
    packed = rows_out.shape[0]
    sent = rows_out[...].astype(jnp.bfloat16)
    for shift_by, out in enumerate(outs):
        out[:packed] = sent
        row = flipped(lax.axis_index("row"), shift_by)
        for flip in range(chips):
            at = pl.multiple_of((row * chips + flipped(chip, flip)) * both, both)
            out[packed + flip * both : packed + (flip + 1) * both] = picked[pl.ds(at, both), :].astype(jnp.bfloat16)


def local_bias(pair, live, gain, shift, weight, along, chips):
    rows, length, channels = pair.shape
    heads = weight.shape[1]
    packed = 2 * heads * rows * (length // channels)
    sent = jax.ShapeDtypeStruct((packed + chips * 2 * WD * rows, channels), jnp.bfloat16)
    return pl.pallas_call(
        functools.partial(bias_kernel, along, chips),
        out_shape=(sent,) * along,
        in_specs=[HBM] * 5,
        out_specs=(VMEM,) * along,
        scratch_shapes=[
            pltpu.VMEM(pair.shape, pair.dtype),
            pltpu.VMEM(live.shape, live.dtype),
            pltpu.VMEM(gain.shape, gain.dtype),
            pltpu.VMEM(shift.shape, shift.dtype),
            pltpu.VMEM(weight.shape, weight.dtype),
            pltpu.VMEM((4 * heads, 2 * channels), jnp.float32),
            pltpu.VMEM((packed, channels), jnp.float32),
            pltpu.VMEM(pair.shape, jnp.float32),
            pltpu.VMEM((length * WD, channels), jnp.float32),
            pltpu.SemaphoreType.DMA((5,)),
        ],
        compiler_params=params(60),
        name="bias",
    )(pair, live, gain, shift, weight)


def turned(row):
    return jnp.broadcast_to(row, (row.shape[1], row.shape[1])).T[:, :1]


def turned_over(index, bit):
    return lax.rem(lax.div(index, bit), 2) == 1


def exchanged(grid, row, col):
    along, cols = len(grid), len(grid[0])
    bit = 1
    while bit < cols:
        swap = turned_over(col, bit)
        grid = [[jnp.where(swap, line[c ^ bit], line[c]) for c in range(cols)] for line in grid]
        bit *= 2
    bit = 1
    while bit < along:
        swap = turned_over(row, bit)
        grid = [[jnp.where(swap, grid[r ^ bit][c], grid[r][c]) for c in range(cols)] for r in range(along)]
        bit *= 2
    return grid


def to_relative(x, along, chips, rows):
    cols = 2 * chips
    grid = [[x[(r * cols + c) * rows : (r * cols + c + 1) * rows] for c in range(cols)] for r in range(along)]
    grid = exchanged(grid, lax.axis_index("row"), lax.axis_index("col"))
    return jnp.concatenate(
        [
            grid[s][2 * flip + other]
            for other in range(2)
            for flip in reversed(range(chips))
            for s in reversed(range(along))
        ],
        0,
    )


def to_devices(x, along, chips, rows):
    at = lambda c, s: (((c % 2) * chips + chips - 1 - c // 2) * along + along - 1 - s) * rows
    grid = [[x[at(c, s) : at(c, s) + rows] for c in range(2 * chips)] for s in range(along)]
    grid = exchanged(grid, lax.axis_index("row"), lax.axis_index("col"))
    return jnp.concatenate([block for line in grid for block in line], 0)


def queries_and_gates(lines, scale, weight, offset, q_ref, g_ref):
    inner = weight.shape[1] // 4
    queries = [contract(weight[:, :inner], normed, 0, 1) for normed in lines]
    gates = [contract(weight[:, 3 * inner :], normed, 0, 1) for normed in lines]
    for w in range(WD):
        q_ref[w] = (queries[w] * scale).astype(jnp.bfloat16)
        g_ref[w] = jax.nn.sigmoid(gates[w] + offset)


def keys_and_values(lines, weight, k_ref, v_ref):
    _, heads, _, size = k_ref.shape
    inner = heads * size
    for h in range(heads):
        at = inner + h * size
        keys = [contract(normed, weight[:, at : at + size], 1, 0) for normed in lines]
        for w in range(WD):
            k_ref[w, h] = keys[w].astype(jnp.bfloat16)
    values = [contract(weight[:, 2 * inner : 3 * inner], normed, 0, 1) for normed in lines]
    for w in range(WD):
        v_ref[w] = values[w].astype(jnp.bfloat16)


def lines_kernel(along, chips, lines_ref, gain_ref, shift_ref, weight_ref, offset_ref, q_ref, k_ref, v_ref, g_ref):
    size = k_ref.shape[-1]
    rows = lines_ref.shape[1] // (2 * chips * along)
    offset = turned(offset_ref[0:1, :])
    weight = weight_ref[0]
    lines = standardize_all([lines_ref[w].astype(jnp.float32) for w in range(WD)])
    lines = [line * gain_ref[0:1, :] + shift_ref[0:1, :] for line in lines]
    keys_and_values([line.astype(jnp.bfloat16) for line in lines], weight, k_ref, v_ref)
    near = [to_relative(line, along, chips, rows).astype(jnp.bfloat16) for line in lines]
    queries_and_gates(near, size ** (-0.5), weight, offset, q_ref, g_ref)


def projected(length, inner, heads):
    wide = (WD, inner, length)
    return (
        (wide, jnp.bfloat16),
        ((WD, heads, length, inner // heads), jnp.bfloat16),
        (wide, jnp.bfloat16),
        (wide, jnp.float32),
    )


def local_lines(pair, gain, shift, weight, offset, heads, along, chips):
    _, length, channels = pair.shape
    wide = weight.shape[2]
    shapes = projected(length, wide // 4, heads)
    whole = lambda shape: pl.BlockSpec(shape, lambda i: (0,) * len(shape))
    return pl.pallas_call(
        functools.partial(lines_kernel, along, chips),
        grid=(1,),
        out_shape=tuple(jax.ShapeDtypeStruct(shape, dtype) for shape, dtype in shapes),
        in_specs=[
            whole((WD, length, channels)), whole(gain.shape), whole(gain.shape),
            whole((1, channels, wide)), whole(gain.shape),
        ],
        out_specs=tuple(whole(shape) for shape, _ in shapes),
        compiler_params=params(8 + length // 32),
        cost_estimate=pl.CostEstimate(
            flops=2 * WD * length * channels * wide, bytes_accessed=4 * WD * length * wide, transcendentals=0
        ),
        name="lines",
    )(pair, gain, shift, weight, offset)


def unpack(source, p, pack, rows, heads, turn, into, at):
    chips, along, _, lanes = source.shape
    packed = 2 * heads * rows
    half = chips * along * rows
    slots = into.shape[0]
    for lane in range(into.shape[2 - turn] // lanes):
        first = lane * packed + (p * heads + 2 * pack) * rows
        both = [
            source[flip, shift, first : first + 2 * rows, :].astype(jnp.float32)
            for flip in range(chips)
            for shift in range(along)
        ]
        there = slice(lane * lanes, (lane + 1) * lanes)
        for i in range(2):
            slot = (2 * pack + i) % slots
            block = jnp.concatenate([part[i * rows : (i + 1) * rows] for part in both], 0)
            if turn:
                into[slot, there, at : at + half] = block.T
            else:
                into[slot, at : at + half, there] = block


def stages(units, put):
    return (
        lambda _: [contract(key, query, 1, 0) + added for key, query, added, _ in units()],
        lambda scores: [(part, jnp.max(part, 0, keepdims=True)) for part in scores],
        lambda pairs: [jnp.exp(part - top) for part, top in pairs],
        lambda expos: [(expo, 1.0 / jnp.sum(expo, 0, keepdims=True)) for expo in expos],
        lambda pairs: [(expo * share).astype(jnp.bfloat16) for expo, share in pairs],
        lambda weights: put(
            [contract(unit[3], weight, 1, 0) for unit, weight in zip(units(), weights)]
        ),
    )


def attend_groups(groups):
    steps = [stages(*group) for group in groups]
    held = [None] * len(groups)
    for t in range(len(groups) + 5 if groups else 0):
        for g in range(len(groups)):
            if 0 <= t - g < 6:
                held[g] = steps[g][t - g](held[g])


def head_group(heads, size, q, k, v, bias, mixed, there, near):
    def units():
        return [
            (k[w, h], q[w, h * size : (h + 1) * size, there], bias[h % bias.shape[0], :, near],
             v[w, h * size : (h + 1) * size, :])
            for h in heads
            for w in range(WD)
        ]

    def put(outs):
        for i, h in enumerate(heads):
            for w in range(WD):
                mixed[w, h * size : (h + 1) * size, near] = outs[i * WD + w]

    return units, put


def start_half(source, other, q, k, v, mixed, bias):
    _, heads, length, size = k.shape
    half = length // 2
    rows = half // (source.shape[0] * source.shape[1])
    width = min(half, CHUNK)
    if half == width:
        groups = []
        for pack in range(heads // 2):
            unpack(source, 0, pack, rows, heads, 1, bias, 0)
            for h in (2 * pack, 2 * pack + 1):
                groups.append(
                    head_group((h,), size, q, k, v, bias, mixed, pl.ds(other * half, half), pl.ds(0, half))
                )
        return groups
    for pack in range(heads // 2):
        unpack(source, 0, pack, rows, heads, 1, bias, 0)

        def step(chunk):
            near = pl.ds(pl.multiple_of(chunk * width, width), width)
            there = pl.ds(pl.multiple_of(other * half + chunk * width, width), width)
            for h in (2 * pack, 2 * pack + 1):
                attend_groups([head_group((h,), size, q, k, v, bias, mixed, there, near)])

        for_each(half // width, step, False)
    return []


def early_kernel(mine_ref, q, k, v, mixed, bias):
    attend_groups(start_half(mine_ref, 0, q, k, v, mixed, bias))


def attend_early(mine, q, k, v):
    _, heads, length, size = k.shape
    return pl.pallas_call(
        early_kernel,
        out_shape=jax.ShapeDtypeStruct((WD, heads * size, length // 2), jnp.float32),
        in_specs=[VMEM] * 4,
        out_specs=VMEM,
        scratch_shapes=[pltpu.VMEM((heads if length <= CHUNK else 2, length, length // 2), jnp.float32)],
        compiler_params=params(8 if length <= CHUNK else 40),
        cost_estimate=pl.CostEstimate(
            flops=4 * WD * heads * size * length * length,
            bytes_accessed=4 * WD * heads * length * length,
            transcendentals=WD * heads * length * length // 2,
        ),
        name="early",
    )(mine, q, k, v)


def attend_kernel(
    mine_ref, other_ref, early_ref, q0, k0, v0, g0,
    gain_ref, shift_ref, proj_ref, gate_ref, weight_ref, offset_ref,
    out0, out1, turned_bias, bias, late, mixed, q1, k1, v1, g1,
):
    chips, along, _, _ = mine_ref.shape
    _, heads, length, size = k0.shape
    half = length // 2
    rows = half // (chips * along)
    packed = 2 * heads * rows * (length // mine_ref.shape[3])
    first = pl.multiple_of(packed + lax.rem(lax.axis_index("col"), 2) * WD * rows, WD * rows)
    groups = start_half(other_ref, 1, q0, k0, v0, late, turned_bias)
    offset = turned(gate_ref[1:2, :])
    blocks = []
    for source in (mine_ref, other_ref):
        for flip in range(chips):
            for shift in range(along):
                both = source[flip, shift, pl.ds(first, WD * rows), :].astype(jnp.float32)
                blocks.append(both.reshape(WD, rows, -1))
    lines = standardize_all([jnp.concatenate([block[w] for block in blocks], 0) for w in range(WD)])
    lines = [line * gain_ref[1:2, :] + shift_ref[1:2, :] for line in lines]
    keys_and_values([line.astype(jnp.bfloat16) for line in lines], proj_ref[1], k1, v1)
    ordered = [to_devices(line, along, chips, rows).astype(jnp.bfloat16) for line in lines]
    queries_and_gates(ordered, size ** (-0.5), proj_ref[1], offset, q1, g1)
    for pack in range(heads // 2):
        unpack(mine_ref, 1, pack, rows, heads, 0, bias, 0)
        unpack(other_ref, 1, pack, rows, heads, 0, bias, half)
        pair = (2 * pack, 2 * pack + 1)
        if length == CHUNK:
            for h in pair:
                groups.append(
                    head_group((h,), size, q1, k1, v1, bias, mixed, pl.ds(0, length), pl.ds(0, length))
                )
            continue

        def step(chunk):
            there = pl.ds(pl.multiple_of(chunk * CHUNK, CHUNK), CHUNK)
            for h in pair:
                attend_groups([head_group((h,), size, q1, k1, v1, bias, mixed, there, there)])

        for_each(length // CHUNK, step, False)
    attend_groups(groups)
    for w in range(WD):
        gated = (jnp.concatenate([early_ref[w], late[w]], 1) * g0[w]).astype(jnp.bfloat16)
        full = contract(gated, weight_ref[0], 0, 0) + offset_ref[0:1, :]
        out0[w] = to_devices(full, along, chips, rows).astype(jnp.bfloat16)
    for w in range(WD):
        gated = (mixed[w] * g1[w]).astype(jnp.bfloat16)
        full = contract(gated, weight_ref[1], 0, 0) + offset_ref[1:2, :]
        out1[w] = full.astype(jnp.bfloat16)


def attend(mine, other, early, start, gain, shift, proj, gate, weight, offset):
    _, heads, length, size = start[1].shape
    inner, channels = weight.shape[1:]
    result = jax.ShapeDtypeStruct((WD, length, channels), jnp.bfloat16)
    slots = heads if length <= CHUNK else 2
    return pl.pallas_call(
        attend_kernel,
        out_shape=(result, result),
        in_specs=[VMEM] * 13,
        out_specs=(VMEM, VMEM),
        scratch_shapes=[
            pltpu.VMEM((slots, length, length // 2), jnp.float32),
            pltpu.VMEM((slots, length, length), jnp.float32),
            pltpu.VMEM((WD, inner, length // 2), jnp.float32),
            pltpu.VMEM((WD, inner, length), jnp.float32),
        ]
        + [pltpu.VMEM(shape, dtype) for shape, dtype in projected(length, inner, heads)],
        compiler_params=params(16 if length <= CHUNK else 60),
        name="attend",
    )(mine, other, early, *start, gain, shift, proj, gate, weight, offset)


def body(pair, residue_mask, ln_gain, ln_shift, w_proj, w_bias, gate_bias, w_out, out_bias):
    rows, length, channels = pair.shape
    heads = w_bias.shape[2]
    along, cols = lax.axis_size("row"), lax.axis_size("col")
    chips = cols // 2

    def by_row(block, shift):
        return lax.ppermute(block, "row", [(i, i ^ shift) for i in range(along)])

    def by_col(block, flip):
        return lax.ppermute(block, "col", [(i, i ^ flip) for i in range(cols)])

    sent = local_bias(
        pair, residue_mask[None, :], ln_gain, ln_shift, jnp.transpose(w_bias, (0, 2, 1)), along, chips
    )
    far_first = [by_row(sent[flip], flip) for flip in reversed(range(1, along))]
    line = jnp.stack(far_first + [sent[0]])
    start = local_lines(pair, ln_gain, ln_shift, w_proj, gate_bias, heads, along, chips)
    line, _ = lax.optimization_barrier((line, start))
    packed = 2 * heads * rows * (length // channels)
    both = 2 * WD * rows

    def owned_by(flip):
        at = packed + flip * both
        return jnp.concatenate([line[:, :packed], line[:, at : at + both]], 1)

    far_first = [by_col(owned_by(flip), 2 * flip) for flip in reversed(range(1, chips))]
    mine = jnp.stack(far_first + [owned_by(0)])
    other = by_col(mine, 1)
    early = attend_early(mine, *start[:3])
    return attend(mine, other, early, start, ln_gain, ln_shift, w_proj, gate_bias, w_out, out_bias)


def solution(mesh):
    return jax.shard_map(
        body,
        mesh=mesh,
        in_specs=(P(("row", "col"), None, None), P(), P(), P(), P(), P(), P(), P(), P()),
        out_specs=(P(("row", "col"), None, None), P(("row", "col"), None, None)),
        check_vma=False,
    )
```

```python
import functools

import jax
import jax.numpy as jnp
from jax import lax
from jax.experimental import pallas as pl
from jax.experimental.pallas import tpu as pltpu
from jax.sharding import PartitionSpec as P

WD = 2
EPS = 1e-05
MASKED = -1000000000.0
CHUNK = 256
VMEM = pl.BlockSpec(memory_space=pltpu.VMEM)
HBM = pl.BlockSpec(memory_space=pltpu.HBM)


def params(megabytes):
    return pltpu.CompilerParams(vmem_limit_bytes=megabytes * 1024 * 1024)


def for_each(count, step, unrolled):
    if unrolled:
        for index in range(count):
            step(index)
    else:
        lax.fori_loop(0, count, lambda index, carry: (step(index), carry)[1], 0)


def standardize_all(lines):
    centers = [jnp.mean(wide, -1, keepdims=True) for wide in lines]
    aways = [wide - center for wide, center in zip(lines, centers)]
    spreads = [jnp.mean(jnp.square(away), -1, keepdims=True) for away in aways]
    return [away * lax.rsqrt(spread + EPS) for away, spread in zip(aways, spreads)]


def contract(left, right, left_dim, right_dim):
    return lax.dot_general(
        left, right, (((left_dim,), (right_dim,)), ((), ())), preferred_element_type=jnp.float32
    )


def flipped(index, flip):
    bit = 1
    while bit <= flip:
        if flip & bit:
            index = index + bit - 2 * bit * lax.rem(lax.div(index, bit), 2)
        bit *= 2
    return index


def bias_kernel(along, chips, pair_hbm, live_hbm, gain_hbm, shift_hbm, weight_hbm, *rest):
    outs = rest[:along]
    pair, live_row, gain, shift, weight, blocks, rows_out, wide, picked, sems = rest[along:]
    rows, length, channels = pair.shape
    heads = weight.shape[1]
    lanes = outs[0].shape[1]
    copies = [
        pltpu.make_async_copy(source, target, sems.at[i])
        for i, (source, target) in enumerate(
            ((pair_hbm, pair), (live_hbm, live_row), (gain_hbm, gain), (shift_hbm, shift), (weight_hbm, weight))
        )
    ]
    for copy in copies:
        copy.start()
    device = lax.axis_index("row") * lax.axis_size("col") + lax.axis_index("col")
    for copy in copies:
        copy.wait()
    blocks[...] = jnp.zeros_like(blocks)
    for p in range(2):
        at = slice(p * heads, (p + 1) * heads)
        blocks[at, p * channels : (p + 1) * channels] = weight[p].astype(jnp.float32)
    paired = blocks[: 2 * heads].astype(jnp.bfloat16)
    live = jnp.broadcast_to(live_row[...], (2 * heads, length)).astype(jnp.float32)
    first = lax.broadcasted_iota(jnp.int32, live.shape, 0) < heads
    token = lax.broadcasted_iota(jnp.int32, (rows, length), 1)
    mine = device * rows + lax.broadcasted_iota(jnp.int32, (rows, length), 0)
    here = jnp.where(token == mine, live_row[...], 0).astype(jnp.float32)
    here = jnp.sum(here, 1, keepdims=True)
    lines = [pair[a].astype(jnp.float32) for a in range(rows)]
    for a, x in enumerate(lines):
        wide[a] = x
    lines = standardize_all(lines)
    normed = [
        jnp.concatenate(
            [(z * gain[p : p + 1, :] + shift[p : p + 1, :]).astype(jnp.bfloat16) for p in range(2)], 1
        )
        for z in lines
    ]
    biases = [contract(paired, line, 1, 1) for line in normed]
    devices = length // rows
    for a in range(rows):
        for w in range(WD):
            column = wide[a, pl.ds(w, devices, stride=rows), :]
            picked[pl.ds(w * rows + a, devices, stride=WD * rows), :] = column
    for a, bias in enumerate(biases):
        kept = jnp.where(first, live, here[a : a + 1])
        bias = jnp.where(kept > 0, bias, MASKED)
        for lane in range(length // lanes):
            part = bias[:, lane * lanes : (lane + 1) * lanes]
            rows_out[pl.ds(2 * lane * heads * rows + a, 2 * heads, stride=rows), :] = part
    chip = lax.div(lax.axis_index("col"), 2)
    both = 2 * WD * rows
    packed = rows_out.shape[0]
    sent = rows_out[...].astype(jnp.bfloat16)
    for shift_by, out in enumerate(outs):
        out[:packed] = sent
        row = flipped(lax.axis_index("row"), shift_by)
        for flip in range(chips):
            at = pl.multiple_of((row * chips + flipped(chip, flip)) * both, both)
            out[packed + flip * both : packed + (flip + 1) * both] = picked[pl.ds(at, both), :].astype(jnp.bfloat16)


def local_bias(pair, live, gain, shift, weight, along, chips):
    rows, length, channels = pair.shape
    heads = weight.shape[1]
    packed = 2 * heads * rows * (length // channels)
    sent = jax.ShapeDtypeStruct((packed + chips * 2 * WD * rows, channels), jnp.bfloat16)
    return pl.pallas_call(
        functools.partial(bias_kernel, along, chips),
        out_shape=(sent,) * along,
        in_specs=[HBM] * 5,
        out_specs=(VMEM,) * along,
        scratch_shapes=[
            pltpu.VMEM(pair.shape, pair.dtype),
            pltpu.VMEM(live.shape, live.dtype),
            pltpu.VMEM(gain.shape, gain.dtype),
            pltpu.VMEM(shift.shape, shift.dtype),
            pltpu.VMEM(weight.shape, weight.dtype),
            pltpu.VMEM((4 * heads, 2 * channels), jnp.float32),
            pltpu.VMEM((packed, channels), jnp.float32),
            pltpu.VMEM(pair.shape, jnp.float32),
            pltpu.VMEM((length * WD, channels), jnp.float32),
            pltpu.SemaphoreType.DMA((5,)),
        ],
        compiler_params=params(60),
        name="bias",
    )(pair, live, gain, shift, weight)


def turned(row):
    return jnp.broadcast_to(row, (row.shape[1], row.shape[1])).T[:, :1]


def turned_over(index, bit):
    return lax.rem(lax.div(index, bit), 2) == 1


def exchanged(grid, row, col):
    along, cols = len(grid), len(grid[0])
    bit = 1
    while bit < cols:
        swap = turned_over(col, bit)
        grid = [[jnp.where(swap, line[c ^ bit], line[c]) for c in range(cols)] for line in grid]
        bit *= 2
    bit = 1
    while bit < along:
        swap = turned_over(row, bit)
        grid = [[jnp.where(swap, grid[r ^ bit][c], grid[r][c]) for c in range(cols)] for r in range(along)]
        bit *= 2
    return grid


def to_relative(x, along, chips, rows):
    cols = 2 * chips
    grid = [[x[(r * cols + c) * rows : (r * cols + c + 1) * rows] for c in range(cols)] for r in range(along)]
    grid = exchanged(grid, lax.axis_index("row"), lax.axis_index("col"))
    return jnp.concatenate(
        [
            grid[s][2 * flip + other]
            for other in range(2)
            for flip in reversed(range(chips))
            for s in reversed(range(along))
        ],
        0,
    )


def to_devices(x, along, chips, rows):
    at = lambda c, s: (((c % 2) * chips + chips - 1 - c // 2) * along + along - 1 - s) * rows
    grid = [[x[at(c, s) : at(c, s) + rows] for c in range(2 * chips)] for s in range(along)]
    grid = exchanged(grid, lax.axis_index("row"), lax.axis_index("col"))
    return jnp.concatenate([block for line in grid for block in line], 0)


def queries_and_gates(lines, scale, weight, offset, q_ref, g_ref):
    inner = weight.shape[1] // 4
    queries = [contract(weight[:, :inner], normed, 0, 1) for normed in lines]
    gates = [contract(weight[:, 3 * inner :], normed, 0, 1) for normed in lines]
    for w in range(WD):
        q_ref[w] = (queries[w] * scale).astype(jnp.bfloat16)
        g_ref[w] = jax.nn.sigmoid(gates[w] + offset)


def keys_and_values(lines, weight, k_ref, v_ref):
    _, heads, _, size = k_ref.shape
    inner = heads * size
    for h in range(heads):
        at = inner + h * size
        keys = [contract(normed, weight[:, at : at + size], 1, 0) for normed in lines]
        for w in range(WD):
            k_ref[w, h] = keys[w].astype(jnp.bfloat16)
    values = [contract(weight[:, 2 * inner : 3 * inner], normed, 0, 1) for normed in lines]
    for w in range(WD):
        v_ref[w] = values[w].astype(jnp.bfloat16)


def lines_kernel(along, chips, lines_ref, gain_ref, shift_ref, weight_ref, offset_ref, q_ref, k_ref, v_ref, g_ref):
    size = k_ref.shape[-1]
    rows = lines_ref.shape[1] // (2 * chips * along)
    offset = turned(offset_ref[0:1, :])
    weight = weight_ref[0]
    lines = standardize_all([lines_ref[w].astype(jnp.float32) for w in range(WD)])
    lines = [line * gain_ref[0:1, :] + shift_ref[0:1, :] for line in lines]
    keys_and_values([line.astype(jnp.bfloat16) for line in lines], weight, k_ref, v_ref)
    near = [to_relative(line, along, chips, rows).astype(jnp.bfloat16) for line in lines]
    queries_and_gates(near, size ** (-0.5), weight, offset, q_ref, g_ref)


def projected(length, inner, heads):
    wide = (WD, inner, length)
    return (
        (wide, jnp.bfloat16),
        ((WD, heads, length, inner // heads), jnp.bfloat16),
        (wide, jnp.bfloat16),
        (wide, jnp.float32),
    )


def local_lines(pair, gain, shift, weight, offset, heads, along, chips):
    _, length, channels = pair.shape
    wide = weight.shape[2]
    shapes = projected(length, wide // 4, heads)
    whole = lambda shape: pl.BlockSpec(shape, lambda i: (0,) * len(shape))
    return pl.pallas_call(
        functools.partial(lines_kernel, along, chips),
        grid=(1,),
        out_shape=tuple(jax.ShapeDtypeStruct(shape, dtype) for shape, dtype in shapes),
        in_specs=[
            whole((WD, length, channels)), whole(gain.shape), whole(gain.shape),
            whole((1, channels, wide)), whole(gain.shape),
        ],
        out_specs=tuple(whole(shape) for shape, _ in shapes),
        compiler_params=params(8 + length // 32),
        cost_estimate=pl.CostEstimate(
            flops=2 * WD * length * channels * wide, bytes_accessed=4 * WD * length * wide, transcendentals=0
        ),
        name="lines",
    )(pair, gain, shift, weight, offset)


def unpack(source, p, pack, rows, heads, turn, into, at):
    chips, along, _, lanes = source.shape
    packed = 2 * heads * rows
    half = chips * along * rows
    slots = into.shape[0]
    for lane in range(into.shape[2 - turn] // lanes):
        first = lane * packed + (p * heads + 2 * pack) * rows
        both = [
            source[flip, shift, first : first + 2 * rows, :].astype(jnp.float32)
            for flip in range(chips)
            for shift in range(along)
        ]
        there = slice(lane * lanes, (lane + 1) * lanes)
        for i in range(2):
            slot = (2 * pack + i) % slots
            block = jnp.concatenate([part[i * rows : (i + 1) * rows] for part in both], 0)
            if turn:
                into[slot, there, at : at + half] = block.T
            else:
                into[slot, at : at + half, there] = block


def stages(units, put):
    return (
        lambda _: [contract(key, query, 1, 0) + added for key, query, added, _ in units()],
        lambda scores: [(part, jnp.max(part, 0, keepdims=True)) for part in scores],
        lambda pairs: [jnp.exp(part - top) for part, top in pairs],
        lambda expos: [(expo, 1.0 / jnp.sum(expo, 0, keepdims=True)) for expo in expos],
        lambda pairs: [(expo * share).astype(jnp.bfloat16) for expo, share in pairs],
        lambda weights: put(
            [contract(unit[3], weight, 1, 0) for unit, weight in zip(units(), weights)]
        ),
    )


def attend_groups(groups):
    steps = [stages(*group) for group in groups]
    held = [None] * len(groups)
    for t in range(len(groups) + 5 if groups else 0):
        for g in range(len(groups)):
            if 0 <= t - g < 6:
                held[g] = steps[g][t - g](held[g])


def head_group(heads, size, q, k, v, bias, mixed, there, near):
    def units():
        return [
            (k[w, h], q[w, h * size : (h + 1) * size, there], bias[h % bias.shape[0], :, near],
             v[w, h * size : (h + 1) * size, :])
            for h in heads
            for w in range(WD)
        ]

    def put(outs):
        for i, h in enumerate(heads):
            for w in range(WD):
                mixed[w, h * size : (h + 1) * size, near] = outs[i * WD + w]

    return units, put


def start_half(source, other, q, k, v, mixed, bias):
    _, heads, length, size = k.shape
    half = length // 2
    rows = half // (source.shape[0] * source.shape[1])
    width = min(half, CHUNK)
    if half == width:
        groups = []
        for pack in range(heads // 2):
            unpack(source, 0, pack, rows, heads, 1, bias, 0)
            for h in (2 * pack, 2 * pack + 1):
                groups.append(
                    head_group((h,), size, q, k, v, bias, mixed, pl.ds(other * half, half), pl.ds(0, half))
                )
        return groups
    for pack in range(heads // 2):
        unpack(source, 0, pack, rows, heads, 1, bias, 0)

        def step(chunk):
            near = pl.ds(pl.multiple_of(chunk * width, width), width)
            there = pl.ds(pl.multiple_of(other * half + chunk * width, width), width)
            for h in (2 * pack, 2 * pack + 1):
                attend_groups([head_group((h,), size, q, k, v, bias, mixed, there, near)])

        for_each(half // width, step, False)
    return []


def early_kernel(mine_ref, q, k, v, mixed, bias):
    attend_groups(start_half(mine_ref, 0, q, k, v, mixed, bias))


def attend_early(mine, q, k, v):
    _, heads, length, size = k.shape
    return pl.pallas_call(
        early_kernel,
        out_shape=jax.ShapeDtypeStruct((WD, heads * size, length // 2), jnp.float32),
        in_specs=[VMEM] * 4,
        out_specs=VMEM,
        scratch_shapes=[pltpu.VMEM((heads if length <= CHUNK else 2, length, length // 2), jnp.float32)],
        compiler_params=params(8 if length <= CHUNK else 40),
        cost_estimate=pl.CostEstimate(
            flops=4 * WD * heads * size * length * length,
            bytes_accessed=4 * WD * heads * length * length,
            transcendentals=WD * heads * length * length // 2,
        ),
        name="early",
    )(mine, q, k, v)


def attend_kernel(
    mine_ref, other_ref, early_ref, q0, k0, v0, g0,
    gain_ref, shift_ref, proj_ref, gate_ref, weight_ref, offset_ref,
    out0, out1, turned_bias, bias, late, mixed, q1, k1, v1, g1,
):
    chips, along, _, _ = mine_ref.shape
    _, heads, length, size = k0.shape
    half = length // 2
    rows = half // (chips * along)
    packed = 2 * heads * rows * (length // mine_ref.shape[3])
    first = pl.multiple_of(packed + lax.rem(lax.axis_index("col"), 2) * WD * rows, WD * rows)
    groups = start_half(other_ref, 1, q0, k0, v0, late, turned_bias)

    def finish_start():
        gated = [
            (jnp.concatenate([early_ref[w], late[w]], 1) * g0[w]).astype(jnp.bfloat16) for w in range(WD)
        ]
        full = [contract(line, weight_ref[0], 0, 0) + offset_ref[0:1, :] for line in gated]
        for w in range(WD):
            out0[w] = to_devices(full[w], along, chips, rows).astype(jnp.bfloat16)

    if groups:
        groups[-1] = (groups[-1][0], lambda outs, put=groups[-1][1]: (put(outs), finish_start()))
    else:
        finish_start()
    offset = turned(gate_ref[1:2, :])
    blocks = []
    for source in (mine_ref, other_ref):
        for flip in range(chips):
            for shift in range(along):
                both = source[flip, shift, pl.ds(first, WD * rows), :].astype(jnp.float32)
                blocks.append(both.reshape(WD, rows, -1))
    lines = standardize_all([jnp.concatenate([block[w] for block in blocks], 0) for w in range(WD)])
    lines = [line * gain_ref[1:2, :] + shift_ref[1:2, :] for line in lines]
    keys_and_values([line.astype(jnp.bfloat16) for line in lines], proj_ref[1], k1, v1)
    ordered = [to_devices(line, along, chips, rows).astype(jnp.bfloat16) for line in lines]
    queries_and_gates(ordered, size ** (-0.5), proj_ref[1], offset, q1, g1)
    for pack in range(heads // 2):
        unpack(mine_ref, 1, pack, rows, heads, 0, bias, 0)
        unpack(other_ref, 1, pack, rows, heads, 0, bias, half)
        pair = (2 * pack, 2 * pack + 1)
        if length == CHUNK:
            for h in pair:
                groups.append(
                    head_group((h,), size, q1, k1, v1, bias, mixed, pl.ds(0, length), pl.ds(0, length))
                )
            continue

        def step(chunk):
            there = pl.ds(pl.multiple_of(chunk * CHUNK, CHUNK), CHUNK)
            for h in pair:
                attend_groups([head_group((h,), size, q1, k1, v1, bias, mixed, there, there)])

        for_each(length // CHUNK, step, False)
    attend_groups(groups)
    gated = [(mixed[w] * g1[w]).astype(jnp.bfloat16) for w in range(WD)]
    full = [contract(line, weight_ref[1], 0, 0) + offset_ref[1:2, :] for line in gated]
    for w in range(WD):
        out1[w] = full[w].astype(jnp.bfloat16)


def attend(mine, other, early, start, gain, shift, proj, gate, weight, offset):
    _, heads, length, size = start[1].shape
    inner, channels = weight.shape[1:]
    result = jax.ShapeDtypeStruct((WD, length, channels), jnp.bfloat16)
    slots = heads if length <= CHUNK else 2
    return pl.pallas_call(
        attend_kernel,
        out_shape=(result, result),
        in_specs=[VMEM] * 13,
        out_specs=(VMEM, VMEM),
        scratch_shapes=[
            pltpu.VMEM((slots, length, length // 2), jnp.float32),
            pltpu.VMEM((slots, length, length), jnp.float32),
            pltpu.VMEM((WD, inner, length // 2), jnp.float32),
            pltpu.VMEM((WD, inner, length), jnp.float32),
        ]
        + [pltpu.VMEM(shape, dtype) for shape, dtype in projected(length, inner, heads)],
        compiler_params=params(16 if length <= CHUNK else 60),
        name="attend",
    )(mine, other, early, *start, gain, shift, proj, gate, weight, offset)


def body(pair, residue_mask, ln_gain, ln_shift, w_proj, w_bias, gate_bias, w_out, out_bias):
    rows, length, channels = pair.shape
    heads = w_bias.shape[2]
    along, cols = lax.axis_size("row"), lax.axis_size("col")
    chips = cols // 2

    def by_row(block, shift):
        return lax.ppermute(block, "row", [(i, i ^ shift) for i in range(along)])

    def by_col(block, flip):
        return lax.ppermute(block, "col", [(i, i ^ flip) for i in range(cols)])

    sent = local_bias(
        pair, residue_mask[None, :], ln_gain, ln_shift, jnp.transpose(w_bias, (0, 2, 1)), along, chips
    )
    far_first = [by_row(sent[flip], flip) for flip in reversed(range(1, along))]
    line = jnp.stack(far_first + [sent[0]])
    start = local_lines(pair, ln_gain, ln_shift, w_proj, gate_bias, heads, along, chips)
    line, _ = lax.optimization_barrier((line, start))
    packed = 2 * heads * rows * (length // channels)
    both = 2 * WD * rows

    def owned_by(flip):
        at = packed + flip * both
        return jnp.concatenate([line[:, :packed], line[:, at : at + both]], 1)

    far_first = [by_col(owned_by(flip), 2 * flip) for flip in reversed(range(1, chips))]
    mine = jnp.stack(far_first + [owned_by(0)])
    other = by_col(mine, 1)
    early = attend_early(mine, *start[:3])
    return attend(mine, other, early, start, ln_gain, ln_shift, w_proj, gate_bias, w_out, out_bias)


def solution(mesh):
    return jax.shard_map(
        body,
        mesh=mesh,
        in_specs=(P(("row", "col"), None, None), P(), P(), P(), P(), P(), P(), P(), P()),
        out_specs=(P(("row", "col"), None, None), P(("row", "col"), None, None)),
        check_vma=False,
    )
```

```python
import functools

import jax
import jax.numpy as jnp
from jax import lax
from jax.experimental import pallas as pl
from jax.experimental.pallas import tpu as pltpu
from jax.sharding import PartitionSpec as P

WD = 2
EPS = 1e-05
MASKED = -1000000000.0
CHUNK = 256
VMEM = pl.BlockSpec(memory_space=pltpu.VMEM)
HBM = pl.BlockSpec(memory_space=pltpu.HBM)


def params(megabytes):
    return pltpu.CompilerParams(vmem_limit_bytes=megabytes * 1024 * 1024)


def for_each(count, step, unrolled):
    if unrolled:
        for index in range(count):
            step(index)
    else:
        lax.fori_loop(0, count, lambda index, carry: (step(index), carry)[1], 0)


def standardize_all(lines):
    channels = lines[0].shape[-1]
    ones = jnp.ones((channels, channels), jnp.bfloat16)
    centers = [contract(wide.astype(jnp.bfloat16), ones, 1, 0) * (1.0 / channels) for wide in lines]
    aways = [wide - center for wide, center in zip(lines, centers)]
    spreads = [jnp.mean(jnp.square(away), -1, keepdims=True) for away in aways]
    return [away * lax.rsqrt(spread + EPS) for away, spread in zip(aways, spreads)]


def contract(left, right, left_dim, right_dim):
    return lax.dot_general(
        left, right, (((left_dim,), (right_dim,)), ((), ())), preferred_element_type=jnp.float32
    )


def flipped(index, flip):
    bit = 1
    while bit <= flip:
        if flip & bit:
            index = index + bit - 2 * bit * lax.rem(lax.div(index, bit), 2)
        bit *= 2
    return index


def bias_kernel(along, chips, pair_hbm, live_hbm, gain_hbm, shift_hbm, weight_hbm, *rest):
    outs = rest[:along]
    pair, live_row, gain, shift, weight, blocks, rows_out, wide, picked, sems = rest[along:]
    rows, length, channels = pair.shape
    heads = weight.shape[1]
    lanes = outs[0].shape[1]
    copies = [
        pltpu.make_async_copy(source, target, sems.at[i])
        for i, (source, target) in enumerate(
            ((pair_hbm, pair), (live_hbm, live_row), (gain_hbm, gain), (shift_hbm, shift), (weight_hbm, weight))
        )
    ]
    for copy in copies:
        copy.start()
    device = lax.axis_index("row") * lax.axis_size("col") + lax.axis_index("col")
    for copy in copies:
        copy.wait()
    blocks[...] = jnp.zeros_like(blocks)
    for p in range(2):
        at = slice(p * heads, (p + 1) * heads)
        blocks[at, p * channels : (p + 1) * channels] = weight[p].astype(jnp.float32)
    paired = blocks[: 2 * heads].astype(jnp.bfloat16)
    live = jnp.broadcast_to(live_row[...], (2 * heads, length)).astype(jnp.float32)
    first = lax.broadcasted_iota(jnp.int32, live.shape, 0) < heads
    token = lax.broadcasted_iota(jnp.int32, (rows, length), 1)
    mine = device * rows + lax.broadcasted_iota(jnp.int32, (rows, length), 0)
    here = jnp.where(token == mine, live_row[...], 0).astype(jnp.float32)
    here = jnp.sum(here, 1, keepdims=True)
    lines = [pair[a].astype(jnp.float32) for a in range(rows)]
    for a, x in enumerate(lines):
        wide[a] = x
    lines = standardize_all(lines)
    normed = [
        jnp.concatenate(
            [(z * gain[p : p + 1, :] + shift[p : p + 1, :]).astype(jnp.bfloat16) for p in range(2)], 1
        )
        for z in lines
    ]
    biases = [contract(paired, line, 1, 1) for line in normed]
    devices = length // rows
    for a in range(rows):
        for w in range(WD):
            column = wide[a, pl.ds(w, devices, stride=rows), :]
            picked[pl.ds(w * rows + a, devices, stride=WD * rows), :] = column
    for a, bias in enumerate(biases):
        kept = jnp.where(first, live, here[a : a + 1])
        bias = jnp.where(kept > 0, bias, MASKED)
        for lane in range(length // lanes):
            part = bias[:, lane * lanes : (lane + 1) * lanes]
            rows_out[pl.ds(2 * lane * heads * rows + a, 2 * heads, stride=rows), :] = part
    chip = lax.div(lax.axis_index("col"), 2)
    both = 2 * WD * rows
    packed = rows_out.shape[0]
    sent = rows_out[...].astype(jnp.bfloat16)
    for shift_by, out in enumerate(outs):
        out[:packed] = sent
        row = flipped(lax.axis_index("row"), shift_by)
        for flip in range(chips):
            at = pl.multiple_of((row * chips + flipped(chip, flip)) * both, both)
            out[packed + flip * both : packed + (flip + 1) * both] = picked[pl.ds(at, both), :].astype(jnp.bfloat16)


def local_bias(pair, live, gain, shift, weight, along, chips):
    rows, length, channels = pair.shape
    heads = weight.shape[1]
    packed = 2 * heads * rows * (length // channels)
    sent = jax.ShapeDtypeStruct((packed + chips * 2 * WD * rows, channels), jnp.bfloat16)
    return pl.pallas_call(
        functools.partial(bias_kernel, along, chips),
        out_shape=(sent,) * along,
        in_specs=[HBM] * 5,
        out_specs=(VMEM,) * along,
        scratch_shapes=[
            pltpu.VMEM(pair.shape, pair.dtype),
            pltpu.VMEM(live.shape, live.dtype),
            pltpu.VMEM(gain.shape, gain.dtype),
            pltpu.VMEM(shift.shape, shift.dtype),
            pltpu.VMEM(weight.shape, weight.dtype),
            pltpu.VMEM((4 * heads, 2 * channels), jnp.float32),
            pltpu.VMEM((packed, channels), jnp.float32),
            pltpu.VMEM(pair.shape, jnp.float32),
            pltpu.VMEM((length * WD, channels), jnp.float32),
            pltpu.SemaphoreType.DMA((5,)),
        ],
        compiler_params=params(60),
        name="bias",
    )(pair, live, gain, shift, weight)


def turned(row):
    return jnp.broadcast_to(row, (row.shape[1], row.shape[1])).T[:, :1]


def turned_over(index, bit):
    return lax.rem(lax.div(index, bit), 2) == 1


def exchanged(grid, row, col):
    along, cols = len(grid), len(grid[0])
    bit = 1
    while bit < cols:
        swap = turned_over(col, bit)
        grid = [[jnp.where(swap, line[c ^ bit], line[c]) for c in range(cols)] for line in grid]
        bit *= 2
    bit = 1
    while bit < along:
        swap = turned_over(row, bit)
        grid = [[jnp.where(swap, grid[r ^ bit][c], grid[r][c]) for c in range(cols)] for r in range(along)]
        bit *= 2
    return grid


def to_relative(x, along, chips, rows):
    cols = 2 * chips
    grid = [[x[(r * cols + c) * rows : (r * cols + c + 1) * rows] for c in range(cols)] for r in range(along)]
    grid = exchanged(grid, lax.axis_index("row"), lax.axis_index("col"))
    return jnp.concatenate(
        [
            grid[s][2 * flip + other]
            for other in range(2)
            for flip in reversed(range(chips))
            for s in reversed(range(along))
        ],
        0,
    )


def to_devices(x, along, chips, rows):
    at = lambda c, s: (((c % 2) * chips + chips - 1 - c // 2) * along + along - 1 - s) * rows
    grid = [[x[at(c, s) : at(c, s) + rows] for c in range(2 * chips)] for s in range(along)]
    grid = exchanged(grid, lax.axis_index("row"), lax.axis_index("col"))
    return jnp.concatenate([block for line in grid for block in line], 0)


def queries_and_gates(lines, scale, weight, offset, q_ref, g_ref):
    inner = weight.shape[1] // 4
    queries = [contract(weight[:, :inner], normed, 0, 1) for normed in lines]
    gates = [contract(weight[:, 3 * inner :], normed, 0, 1) for normed in lines]
    for w in range(WD):
        q_ref[w] = (queries[w] * scale).astype(jnp.bfloat16)
        g_ref[w] = jax.nn.sigmoid(gates[w] + offset)


def keys_and_values(lines, weight, k_ref, v_ref):
    _, heads, _, size = k_ref.shape
    inner = heads * size
    for h in range(heads):
        at = inner + h * size
        keys = [contract(normed, weight[:, at : at + size], 1, 0) for normed in lines]
        for w in range(WD):
            k_ref[w, h] = keys[w].astype(jnp.bfloat16)
    values = [contract(weight[:, 2 * inner : 3 * inner], normed, 0, 1) for normed in lines]
    for w in range(WD):
        v_ref[w] = values[w].astype(jnp.bfloat16)


def lines_kernel(along, chips, lines_ref, gain_ref, shift_ref, weight_ref, offset_ref, q_ref, k_ref, v_ref, g_ref):
    size = k_ref.shape[-1]
    rows = lines_ref.shape[1] // (2 * chips * along)
    offset = turned(offset_ref[0:1, :])
    weight = weight_ref[0]
    lines = standardize_all([lines_ref[w].astype(jnp.float32) for w in range(WD)])
    lines = [line * gain_ref[0:1, :] + shift_ref[0:1, :] for line in lines]
    keys_and_values([line.astype(jnp.bfloat16) for line in lines], weight, k_ref, v_ref)
    near = [to_relative(line, along, chips, rows).astype(jnp.bfloat16) for line in lines]
    queries_and_gates(near, size ** (-0.5), weight, offset, q_ref, g_ref)


def projected(length, inner, heads):
    wide = (WD, inner, length)
    return (
        (wide, jnp.bfloat16),
        ((WD, heads, length, inner // heads), jnp.bfloat16),
        (wide, jnp.bfloat16),
        (wide, jnp.float32),
    )


def local_lines(pair, gain, shift, weight, offset, heads, along, chips):
    _, length, channels = pair.shape
    wide = weight.shape[2]
    shapes = projected(length, wide // 4, heads)
    whole = lambda shape: pl.BlockSpec(shape, lambda i: (0,) * len(shape))
    return pl.pallas_call(
        functools.partial(lines_kernel, along, chips),
        grid=(1,),
        out_shape=tuple(jax.ShapeDtypeStruct(shape, dtype) for shape, dtype in shapes),
        in_specs=[
            whole((WD, length, channels)), whole(gain.shape), whole(gain.shape),
            whole((1, channels, wide)), whole(gain.shape),
        ],
        out_specs=tuple(whole(shape) for shape, _ in shapes),
        compiler_params=params(8 + length // 32),
        cost_estimate=pl.CostEstimate(
            flops=2 * WD * length * channels * wide, bytes_accessed=4 * WD * length * wide, transcendentals=0
        ),
        name="lines",
    )(pair, gain, shift, weight, offset)


def unpack(source, p, pack, rows, heads, turn, into, at):
    chips, along, _, lanes = source.shape
    packed = 2 * heads * rows
    half = chips * along * rows
    slots = into.shape[0]
    for lane in range(into.shape[2 - turn] // lanes):
        first = lane * packed + (p * heads + 2 * pack) * rows
        both = [
            source[flip, shift, first : first + 2 * rows, :].astype(jnp.float32)
            for flip in range(chips)
            for shift in range(along)
        ]
        there = slice(lane * lanes, (lane + 1) * lanes)
        for i in range(2):
            slot = (2 * pack + i) % slots
            block = jnp.concatenate([part[i * rows : (i + 1) * rows] for part in both], 0)
            if turn:
                into[slot, there, at : at + half] = block.T
            else:
                into[slot, at : at + half, there] = block


def stages(units, put):
    return (
        lambda _: [contract(key, query, 1, 0) + added for key, query, added, _ in units()],
        lambda scores: [(part, jnp.max(part, 0, keepdims=True)) for part in scores],
        lambda pairs: [jnp.exp(part - top) for part, top in pairs],
        lambda expos: [(expo, 1.0 / jnp.sum(expo, 0, keepdims=True)) for expo in expos],
        lambda pairs: [(expo * share).astype(jnp.bfloat16) for expo, share in pairs],
        lambda weights: put(
            [contract(unit[3], weight, 1, 0) for unit, weight in zip(units(), weights)]
        ),
    )


def attend_groups(groups):
    steps = [stages(*group) for group in groups]
    held = [None] * len(groups)
    for t in range(len(groups) + 5 if groups else 0):
        for g in range(len(groups)):
            if 0 <= t - g < 6:
                held[g] = steps[g][t - g](held[g])


def head_group(heads, size, q, k, v, bias, mixed, there, near):
    def units():
        return [
            (k[w, h], q[w, h * size : (h + 1) * size, there], bias[h % bias.shape[0], :, near],
             v[w, h * size : (h + 1) * size, :])
            for h in heads
            for w in range(WD)
        ]

    def put(outs):
        for i, h in enumerate(heads):
            for w in range(WD):
                mixed[w, h * size : (h + 1) * size, near] = outs[i * WD + w]

    return units, put


def start_half(source, other, q, k, v, mixed, bias):
    _, heads, length, size = k.shape
    half = length // 2
    rows = half // (source.shape[0] * source.shape[1])
    width = min(half, CHUNK)
    if half == width:
        groups = []
        for pack in range(heads // 2):
            unpack(source, 0, pack, rows, heads, 1, bias, 0)
            for h in (2 * pack, 2 * pack + 1):
                groups.append(
                    head_group((h,), size, q, k, v, bias, mixed, pl.ds(other * half, half), pl.ds(0, half))
                )
        return groups
    for pack in range(heads // 2):
        unpack(source, 0, pack, rows, heads, 1, bias, 0)

        def step(chunk):
            near = pl.ds(pl.multiple_of(chunk * width, width), width)
            there = pl.ds(pl.multiple_of(other * half + chunk * width, width), width)
            for h in (2 * pack, 2 * pack + 1):
                attend_groups([head_group((h,), size, q, k, v, bias, mixed, there, near)])

        for_each(half // width, step, False)
    return []


def early_kernel(mine_ref, q, k, v, mixed, bias):
    attend_groups(start_half(mine_ref, 0, q, k, v, mixed, bias))


def attend_early(mine, q, k, v):
    _, heads, length, size = k.shape
    return pl.pallas_call(
        early_kernel,
        out_shape=jax.ShapeDtypeStruct((WD, heads * size, length // 2), jnp.float32),
        in_specs=[VMEM] * 4,
        out_specs=VMEM,
        scratch_shapes=[pltpu.VMEM((heads if length <= CHUNK else 2, length, length // 2), jnp.float32)],
        compiler_params=params(8 if length <= CHUNK else 40),
        cost_estimate=pl.CostEstimate(
            flops=4 * WD * heads * size * length * length,
            bytes_accessed=4 * WD * heads * length * length,
            transcendentals=WD * heads * length * length // 2,
        ),
        name="early",
    )(mine, q, k, v)


def attend_kernel(
    mine_ref, other_ref, early_ref, q0, k0, v0, g0,
    gain_ref, shift_ref, proj_ref, gate_ref, weight_ref, offset_ref,
    out0, out1, turned_bias, bias, late, mixed, q1, k1, v1, g1,
):
    chips, along, _, _ = mine_ref.shape
    _, heads, length, size = k0.shape
    half = length // 2
    rows = half // (chips * along)
    packed = 2 * heads * rows * (length // mine_ref.shape[3])
    first = pl.multiple_of(packed + lax.rem(lax.axis_index("col"), 2) * WD * rows, WD * rows)
    groups = start_half(other_ref, 1, q0, k0, v0, late, turned_bias)
    offset = turned(gate_ref[1:2, :])
    blocks = []
    for source in (mine_ref, other_ref):
        for flip in range(chips):
            for shift in range(along):
                both = source[flip, shift, pl.ds(first, WD * rows), :].astype(jnp.float32)
                blocks.append(both.reshape(WD, rows, -1))
    lines = standardize_all([jnp.concatenate([block[w] for block in blocks], 0) for w in range(WD)])
    lines = [line * gain_ref[1:2, :] + shift_ref[1:2, :] for line in lines]
    keys_and_values([line.astype(jnp.bfloat16) for line in lines], proj_ref[1], k1, v1)
    ordered = [to_devices(line, along, chips, rows).astype(jnp.bfloat16) for line in lines]
    queries_and_gates(ordered, size ** (-0.5), proj_ref[1], offset, q1, g1)
    for pack in range(heads // 2):
        unpack(mine_ref, 1, pack, rows, heads, 0, bias, 0)
        unpack(other_ref, 1, pack, rows, heads, 0, bias, half)
        pair = (2 * pack, 2 * pack + 1)
        if length == CHUNK:
            for h in pair:
                groups.append(
                    head_group((h,), size, q1, k1, v1, bias, mixed, pl.ds(0, length), pl.ds(0, length))
                )
            continue

        def step(chunk):
            there = pl.ds(pl.multiple_of(chunk * CHUNK, CHUNK), CHUNK)
            for h in pair:
                attend_groups([head_group((h,), size, q1, k1, v1, bias, mixed, there, there)])

        for_each(length // CHUNK, step, False)
    attend_groups(groups)
    for w in range(WD):
        gated = (jnp.concatenate([early_ref[w], late[w]], 1) * g0[w]).astype(jnp.bfloat16)
        full = contract(gated, weight_ref[0], 0, 0) + offset_ref[0:1, :]
        out0[w] = to_devices(full, along, chips, rows).astype(jnp.bfloat16)
    for w in range(WD):
        gated = (mixed[w] * g1[w]).astype(jnp.bfloat16)
        full = contract(gated, weight_ref[1], 0, 0) + offset_ref[1:2, :]
        out1[w] = full.astype(jnp.bfloat16)


def attend(mine, other, early, start, gain, shift, proj, gate, weight, offset):
    _, heads, length, size = start[1].shape
    inner, channels = weight.shape[1:]
    result = jax.ShapeDtypeStruct((WD, length, channels), jnp.bfloat16)
    slots = heads if length <= CHUNK else 2
    return pl.pallas_call(
        attend_kernel,
        out_shape=(result, result),
        in_specs=[VMEM] * 13,
        out_specs=(VMEM, VMEM),
        scratch_shapes=[
            pltpu.VMEM((slots, length, length // 2), jnp.float32),
            pltpu.VMEM((slots, length, length), jnp.float32),
            pltpu.VMEM((WD, inner, length // 2), jnp.float32),
            pltpu.VMEM((WD, inner, length), jnp.float32),
        ]
        + [pltpu.VMEM(shape, dtype) for shape, dtype in projected(length, inner, heads)],
        compiler_params=params(16 if length <= CHUNK else 60),
        name="attend",
    )(mine, other, early, *start, gain, shift, proj, gate, weight, offset)


def body(pair, residue_mask, ln_gain, ln_shift, w_proj, w_bias, gate_bias, w_out, out_bias):
    rows, length, channels = pair.shape
    heads = w_bias.shape[2]
    along, cols = lax.axis_size("row"), lax.axis_size("col")
    chips = cols // 2

    def by_row(block, shift):
        return lax.ppermute(block, "row", [(i, i ^ shift) for i in range(along)])

    def by_col(block, flip):
        return lax.ppermute(block, "col", [(i, i ^ flip) for i in range(cols)])

    sent = local_bias(
        pair, residue_mask[None, :], ln_gain, ln_shift, jnp.transpose(w_bias, (0, 2, 1)), along, chips
    )
    far_first = [by_row(sent[flip], flip) for flip in reversed(range(1, along))]
    line = jnp.stack(far_first + [sent[0]])
    start = local_lines(pair, ln_gain, ln_shift, w_proj, gate_bias, heads, along, chips)
    line, _ = lax.optimization_barrier((line, start))
    packed = 2 * heads * rows * (length // channels)
    both = 2 * WD * rows

    def owned_by(flip):
        at = packed + flip * both
        return jnp.concatenate([line[:, :packed], line[:, at : at + both]], 1)

    far_first = [by_col(owned_by(flip), 2 * flip) for flip in reversed(range(1, chips))]
    mine = jnp.stack(far_first + [owned_by(0)])
    other = by_col(mine, 1)
    early = attend_early(mine, *start[:3])
    return attend(mine, other, early, start, ln_gain, ln_shift, w_proj, gate_bias, w_out, out_bias)


def solution(mesh):
    return jax.shard_map(
        body,
        mesh=mesh,
        in_specs=(P(("row", "col"), None, None), P(), P(), P(), P(), P(), P(), P(), P()),
        out_specs=(P(("row", "col"), None, None), P(("row", "col"), None, None)),
        check_vma=False,
    )
```
